32 devices in a mesh: dp: 8 (over z, y), section: 4 (over x, core).
Axes of the slice: x: 2, y: 2, z: 4, core: 2. Of those that a mesh axis runs over, the one named last changes fastest.
Arguments:
- tokens: bfloat16 [4096, 768], P('dp'), may hold values from -6 to 6
- lengths: int32 [64], P('dp'), may hold values from 4 to 64, as said below
- pair_index: int32 [64], P('dp'), may hold values from 0 to 63, each once
- images: bfloat16 [64, 768], P('dp'), may hold values from -6 to 6
- ln1_gain: float32 [4, 768], P('section'), may hold values from 0.5 to 1.5
- ln1_bias: float32 [4, 768], P('section'), may hold values from -1 to 1
- qkv_weight: bfloat16 [4, 768, 2304], P('section'), may hold values from -0.21875 to 0.21875
- out_weight: bfloat16 [4, 768, 768], P('section'), may hold values from -0.875 to 0.875
- ln2_gain: float32 [4, 768], P('section'), may hold values from 0.5 to 1.5
- ln2_bias: float32 [4, 768], P('section'), may hold values from -1 to 1
- up_weight: bfloat16 [4, 768, 3072], P('section'), may hold values from -0.21875 to 0.21875
- down_weight: bfloat16 [4, 3072, 768], P('section'), may hold values from -0.109375 to 0.109375
- final_gain: float32 [768], replicated, may hold values from 0.5 to 1.5
- final_bias: float32 [768], replicated, may hold values from -1 to 1
- proj_weight: bfloat16 [768, 768], replicated, may hold values from -0.21875 to 0.21875
Outputs:
- hidden_out: bfloat16 [4, 4096, 768], P('section', 'dp')
- input_grads: float32 [4, 4096, 768], P('section', 'dp')
- ln1_gain_grad: float32 [4, 768], P('section', 'dp')
- ln1_bias_grad: float32 [4, 768], P('section', 'dp')
- qkv_weight_grad: float32 [4, 768, 2304], P('section', 'dp')
- out_weight_grad: float32 [4, 768, 768], P('section', 'dp')
- ln2_gain_grad: float32 [4, 768], P('section', 'dp')
- ln2_bias_grad: float32 [4, 768], P('section', 'dp')
- up_weight_grad: float32 [4, 768, 3072], P('section', 'dp')
- down_weight_grad: float32 [4, 3072, 768], P('section', 'dp')
- final_gain_grad: float32 [768], replicated
- final_bias_grad: float32 [768], replicated
- proj_weight_grad: float32 [768, 768], replicated
- pair_loss: float32 [64], replicated
The draws below stay inside these ranges and needn't reach their ends.
Inputs may be any that keep to these rules, and one draw needn't show every extreme that they name: Each sequence's valid tokens are its first lengths positions; among the 8 sequences of each index of dp one has all 64. `pair_index`: every image row is named by exactly one text sequence.
All inputs are finite; a program needn't handle non-finite values.
Results may differ from the reference program's by a relative error of at most 0.017.
Values may be sent and summed in bfloat16 or wider, within the bound.
No kernel may reach another device: no remote copies, remote signals or barrier semaphores. Data moves between devices by JAX's collectives and lax.ppermute only.
A program may use at most 384 MiB of HBM per device.

```python
import jax
import jax.numpy as jnp
from jax import lax

D = 768
HEADS = 12
HEAD = 64
FF = 3072
E = 768
SEQ = 64
SEQ_DEV = 8
BLOCKS = 4
PAIRS = 64
TOKENS = 4096
N_DP = 8


def draw_lengths(key, part):
    key = jax.random.fold_in(key, 11)
    first_key, second_key = jax.random.split(key)
    drawn = jax.random.randint(first_key, (PAIRS,), 4, SEQ + 1)
    chosen = jax.random.randint(second_key, (PAIRS // SEQ_DEV, 1), 0, SEQ_DEV)
    full_row = (jnp.arange(SEQ_DEV)[None, :] == chosen).reshape(PAIRS)
    return jnp.where(full_row, SEQ, drawn).astype(jnp.int32)


def level_of(own_key, shape, cuts, smallest, high):
    def one(axis_at, parts):
        draws = jax.random.uniform(jax.random.fold_in(jax.random.fold_in(own_key, 6), axis_at), (parts,), jnp.float32, smallest / len(cuts), high / len(cuts))
        return jnp.repeat(jnp.exp(draws), shape[axis_at] // parts).reshape((-1,) + (1,) * (len(shape) - axis_at - 1))

    level = one(*cuts[0])
    for cut in cuts[1:]:
        level = level * one(*cut)
    return level


def normal_values(own_key, shape, width, most, shards=(), kind=jnp.bfloat16):
    factor_of = level_of(own_key, shape, shards, -0.22, 0.18) if shards else 1.0
    values = jax.random.normal(own_key, shape, jnp.float32) * width * factor_of
    return jnp.minimum(jnp.maximum(values, -most), most).astype(kind)


def setup_inputs(seed: int = 0) -> dict:
    splits = jax.random.split(jax.random.key(seed), 16)
    tokens = normal_values(splits[0], (TOKENS, D), 1.0, 6.0, ((0, 8),))
    lengths = draw_lengths(jax.random.fold_in(splits[15], 71), 0)
    pair_index = jax.random.permutation(splits[2], PAIRS).astype(jnp.int32)
    images = normal_values(splits[3], (PAIRS, E), 1.0, 6.0, ((0, 8),))
    ln1_gain = jnp.clip(1.0 + 0.1 * jax.random.normal(splits[4], (BLOCKS, D), jnp.float32), 0.5, 1.5)
    ln1_bias = normal_values(splits[5], (BLOCKS, D), 0.2, 1.0, ((0, 4),), jnp.float32)
    qkv_weight = normal_values(splits[6], (BLOCKS, D, 3 * D), D ** -0.5, 0.21875, ((0, 4),))
    out_weight = normal_values(splits[7], (BLOCKS, D, D), (D // 16) ** -0.5, 0.875, ((0, 4),))
    ln2_gain = jnp.clip(1.0 + 0.1 * jax.random.normal(splits[8], (BLOCKS, D), jnp.float32), 0.5, 1.5)
    ln2_bias = normal_values(splits[9], (BLOCKS, D), 0.2, 1.0, ((0, 4),), jnp.float32)
    up_weight = normal_values(splits[10], (BLOCKS, D, FF), D ** -0.5, 0.21875, ((0, 4),))
    down_weight = normal_values(splits[11], (BLOCKS, FF, D), FF ** -0.5, 0.109375, ((0, 4),))
    final_gain = jnp.clip(1.0 + 0.1 * jax.random.normal(splits[12], (D,), jnp.float32), 0.5, 1.5)
    final_bias = normal_values(splits[13], (D,), 0.2, 1.0, (), jnp.float32)
    proj_weight = normal_values(splits[14], (D, E), D ** -0.5, 0.21875)
    return {"tokens": tokens, "lengths": lengths, "pair_index": pair_index, "images": images, "ln1_gain": ln1_gain, "ln1_bias": ln1_bias, "qkv_weight": qkv_weight, "out_weight": out_weight, "ln2_gain": ln2_gain, "ln2_bias": ln2_bias, "up_weight": up_weight, "down_weight": down_weight, "final_gain": final_gain, "final_bias": final_bias, "proj_weight": proj_weight}


norm_eps = 1e-06
masked_score = -1000000000.0
highest = lax.Precision.HIGHEST

@jax.custom_vjp
def low(v):
    return lax.optimization_barrier(v.astype(jnp.bfloat16)).astype(jnp.float32)

@jax.custom_vjp
def low_back(v):
    return v

def low_keep(v):
    return (low(v), None)

def low_pass(kept, grad):
    return (grad,)

def back_keep(v):
    return (v, None)

def back_low(kept, grad):
    return (low(grad),)
low.defvjp(low_keep, low_pass)
low_back.defvjp(back_keep, back_low)

def layer_norm(values, gain, offset):
    centred = values - lax.optimization_barrier(jnp.mean(values, -1, keepdims=True))
    return centred * lax.rsqrt(lax.optimization_barrier(jnp.mean(centred * centred, -1, keepdims=True)) + norm_eps) * gain + offset

def text_block(inputs, lengths, params):
    gain_one, bias_one, qkv_matrix, out_matrix, gain_two, bias_two, up_matrix, down_matrix = params
    seq_count, seq_length, model_width = inputs.shape
    normed = low(layer_norm(inputs, gain_one, bias_one))
    qkv_all = low(low_back(jnp.einsum('std,de->ste', normed, qkv_matrix, precision=highest)))
    qkv_heads = qkv_all.reshape(seq_count, seq_length, 3, HEADS, HEAD)
    queries = qkv_heads[:, :, 0]
    key_heads = qkv_heads[:, :, 1]
    value_heads = qkv_heads[:, :, 2]
    key_ok = (jnp.arange(seq_length)[None, :] < lengths[:, None])[:, None, None, :]
    raw_scores = jnp.einsum('bqhd,bkhd->bhqk', queries, key_heads, precision=highest) * HEAD ** (-0.5)
    scores = low_back(jnp.where(key_ok, raw_scores, masked_score))
    attn_probs = low(jax.nn.softmax(scores, -1))
    attn_mixed = jnp.einsum('bhqk,bkhd->bqhd', attn_probs, value_heads, precision=highest)
    attn_mixed = low(low_back(attn_mixed.reshape(seq_count, seq_length, model_width)))
    attended = inputs + low_back(jnp.einsum('std,de->ste', attn_mixed, out_matrix, precision=highest))
    normed_two = low(layer_norm(attended, gain_two, bias_two))
    up_val = low_back(jnp.einsum('std,df->stf', normed_two, up_matrix, precision=highest))
    down_val = jnp.einsum('stf,fd->std', low(jax.nn.gelu(up_val)), down_matrix, precision=highest)
    return attended + low_back(down_val)

def tower_group(params, group_tokens, group_lengths, group_probes):
    hidden = group_tokens + group_probes[0]
    outputs = []
    for block_index in range(BLOCKS):
        if block_index > 0:
            hidden = low_back(low(hidden)) + group_probes[block_index]
        hidden = text_block(hidden, group_lengths, tuple((weight[block_index] for weight in params)))
        outputs.append(hidden)
    return jnp.stack(outputs)

def forward_pass(params, head_params, probes, tokens_float, lengths, image_unit, pair_index):
    logit_scale = 1.5 * E ** 0.5
    group_tokens = tokens_float.reshape(N_DP, SEQ_DEV, SEQ, D)
    group_lengths = lengths.reshape(N_DP, SEQ_DEV)
    group_probes = probes.reshape(BLOCKS, N_DP, SEQ_DEV, SEQ, D).transpose(1, 0, 2, 3, 4)
    group_step = jax.checkpoint(tower_group)

    def map_step(pieces):
        return group_step(params, pieces[0], pieces[1], pieces[2])
    stacked = lax.map(map_step, (group_tokens, group_lengths, group_probes))
    final_rows = stacked[:, BLOCKS - 1].reshape(PAIRS, SEQ, D)
    final_gain, final_bias, proj_weight = head_params
    normed = layer_norm(final_rows, final_gain, final_bias)
    token_ok = (jnp.arange(SEQ)[None, :] < lengths[:, None]).astype(jnp.float32)
    pooled = low(lax.optimization_barrier(jnp.sum(normed * token_ok[:, :, None], 1)) / lengths.astype(jnp.float32)[:, None])
    text_emb = low_back(jnp.dot(pooled, proj_weight, precision=highest))
    text_unit = low(text_emb * lax.rsqrt(lax.optimization_barrier(jnp.sum(text_emb * text_emb, -1, keepdims=True)) + norm_eps))
    logits = low_back(logit_scale * jnp.dot(text_unit, image_unit.T, precision=highest))
    row_lse = jax.nn.logsumexp(logits, 1)
    col_lse = jax.nn.logsumexp(logits, 0)
    target_hot = (pair_index[:, None] == jnp.arange(PAIRS)[None, :]).astype(jnp.float32)
    target_logit = lax.optimization_barrier(jnp.sum(logits * target_hot, 1))
    col_at = lax.optimization_barrier(jnp.sum(target_hot * col_lse[None, :], 1))
    pair_loss = 0.5 * (row_lse - target_logit) + 0.5 * (col_at - target_logit)
    return (jnp.sum(pair_loss), (stacked, pair_loss))

def reference(tokens, lengths, pair_index, images, ln1_gain, ln1_bias, qkv_weight, out_weight, ln2_gain, ln2_bias, up_weight, down_weight, final_gain, final_bias, proj_weight):
    params = tuple((weight.astype(jnp.float32) for weight in (ln1_gain, ln1_bias, qkv_weight, out_weight, ln2_gain, ln2_bias, up_weight, down_weight)))
    head_params = (final_gain.astype(jnp.float32), final_bias.astype(jnp.float32), proj_weight.astype(jnp.float32))
    probes = jnp.zeros((BLOCKS, PAIRS * SEQ, D), jnp.float32)
    image_all = images.astype(jnp.float32)
    image_unit = low(image_all * lax.rsqrt(lax.optimization_barrier(jnp.sum(image_all * image_all, -1, keepdims=True)) + norm_eps))
    tokens_float = tokens.astype(jnp.float32)

    def objective(params, head_params, probes):
        return forward_pass(params, head_params, probes, tokens_float, lengths, image_unit, pair_index)
    total_loss, pullback, extras = jax.vjp(objective, params, head_params, probes, has_aux=True)
    stacked, pair_loss = extras
    grad_params, grad_head, grad_probes = pullback(jnp.ones((), jnp.float32))
    hidden_out = stacked.transpose(1, 0, 2, 3, 4).reshape(BLOCKS, PAIRS * SEQ, D).astype(jnp.bfloat16)
    return (hidden_out, grad_probes, grad_params[0], grad_params[1], grad_params[2], grad_params[3], grad_params[4], grad_params[5], grad_params[6], grad_params[7], grad_head[0], grad_head[1], grad_head[2], pair_loss)
```

```python
import functools
import math

import jax
import jax.numpy as jnp
from jax import lax
from jax.experimental import pallas as pl
from jax.experimental.pallas import tpu as pltpu
from jax.sharding import PartitionSpec as P

HEADS = 12
HEAD = 64
PAIR = 2 * HEAD
ROWS = 256
EPS = 1e-06
MASKED = -1000000000.0
BF = jnp.bfloat16
F32 = jnp.float32
ANY = pl.BlockSpec(memory_space=pltpu.HBM)
SMEM = pl.BlockSpec(memory_space=pltpu.SMEM)
VMEM = pl.BlockSpec(memory_space=pltpu.VMEM)
VLIM = 24 << 20
UNROLL = 6
FREE = pl.CostEstimate(flops=1, bytes_accessed=1, transcendentals=0)
SECTION, GROUP, LENS = range(3)


def hbm(v):
    return pltpu.with_memory_space_constraint(v, pltpu.HBM)


def vmem(v):
    return pltpu.with_memory_space_constraint(v, pltpu.VMEM)


def mm(a, b):
    return jnp.dot(a, b, preferred_element_type=F32)


def mm_nt(a, b):
    return lax.dot_general(a, b, (((1,), (1,)), ((), ())), preferred_element_type=F32)


def mm_tn(a, b):
    return lax.dot_general(a, b, (((0,), (0,)), ((), ())), preferred_element_type=F32)


def norm_of(v):
    c = v - jnp.mean(v, -1, keepdims=True)
    r = lax.rsqrt(jnp.mean(c * c, -1, keepdims=True) + EPS)
    return c * r, r


def norm_back(n, r, w):
    return r * (w - jnp.mean(w, -1, keepdims=True) - n * jnp.mean(w * n, -1, keepdims=True))


def gelu_pair(u):
    k = 0.7978845608028654
    u2 = u * u
    t = jnp.tanh(u * (k + (k * 0.044715) * u2))
    p = 0.5 + 0.5 * t
    g = p + (0.5 * u) * ((1.0 - t * t) * (k + (3.0 * k * 0.044715) * u2))
    return u * p, g


def split_heads(v, low):
    z = jnp.zeros_like(v)
    return jnp.concatenate([jnp.where(low, v, z), jnp.where(low, z, v)], axis=0)


def low_lanes():
    return lax.broadcasted_iota(jnp.int32, (PAIR, PAIR), 1) < HEAD


def chunk(j, width):
    return pl.ds(pl.multiple_of(j * width, 128), width)


class Weights:
    def __init__(self, sources, held, sem, model):
        self.sem, self.jobs, self.due = sem, {}, sources is not None
        if not self.due:
            return
        k = 0
        for name, src, dst in zip(("qkv", "out", "up", "down"), sources, held):
            rows, cols = dst.shape
            for j in range(max(rows, cols) // model):
                piece = pl.ds(j * model, model)
                at = (slice(None), piece) if cols > model else (piece, slice(None))
                self.jobs[name, j] = (src, dst, at, k)
                k += 1

    def copy(self, name, j, offset=0):
        src, dst, at, k = self.jobs[name, j]
        return pltpu.make_async_copy(src.at[(0,) + at], dst.at[at], self.sem.at[k + offset])

    def start(self, name, *pieces):
        for j in pieces or [j for n, j in self.jobs if n == name]:
            self.copy(name, j).start()

    def wait(self, name, j=0):
        if self.due:
            self.copy(name, 0, j).wait()


def fwd_kernel(fresh, place, slot, own, last, first_at, model, ff, info, first, norms, w1, w2, w3, w4, *rest):
    (X, A, QKV, PP, O, H, C, MM, GP, HID, NB, Y, wqkv, wo, wup, wdn, yout,
     xs, as_, qs, ps, os_, hs, cs, ms, gs, ys, acc, nb, sem, wsem) = rest
    weights = Weights((w1, w2, w3, w4) if fresh else None, (wqkv, wo, wup, wdn), wsem, model)
    names = ("qkv", "out", "up", "down")
    if fresh:
        @pl.when(info[SECTION] != place)
        def _():
            for name in names:
                weights.start(name)
            for name, j in weights.jobs:
                weights.wait(name, j)

    seqs = ROWS // 64

    def length(i):
        return info[LENS + slot * seqs + i]

    @pl.when(info[SECTION] == place)
    def _():
        come = pltpu.make_async_copy(first.at[pl.ds(first_at, ROWS)], xs, sem.at[0])
        come.start()
        weights.start("qkv")
        come.wait()
        copies = []

        def out(src, dst, k):
            cp = pltpu.make_async_copy(src, dst, sem.at[k])
            cp.start()
            copies.append(cp)

        out(xs, X.at[slot], 18)
        gain, bias = norms[0:1, :], norms[1:2, :]
        for i in range(seqs):
            sl = pl.ds(i * 64, 64)
            n, _r = norm_of(xs[sl, :].astype(F32))
            as_[sl, :] = (n * gain + bias).astype(BF)
        out(as_, A.at[slot], 2)

        @pl.loop(0, 3)
        def _(j):
            sl = chunk(j, model)
            weights.wait("qkv", j)
            qs[:, sl] = mm(as_[...], wqkv[:, sl]).astype(BF)

        weights.start("out")
        weights.start("up")

        out(qs, QKV.at[slot], 3)
        low = low_lanes()
        row = lax.broadcasted_iota(jnp.int32, (PAIR, PAIR), 0)
        col = lax.broadcasted_iota(jnp.int32, (PAIR, PAIR), 1)

        @pl.loop(0, ROWS // 128 * (HEADS // 2), unroll=UNROLL)
        def _(it):
            p = it // (HEADS // 2)
            hp = it % (HEADS // 2)
            l0 = length(2 * p)
            l1 = length(2 * p + 1)
            ok = ((col < 64) & (row < l0)) | ((col >= 64) & (row >= 64) & (row < 64 + l1))
            rs = pl.ds(pl.multiple_of(p * 128, 128), 128)

            def lanes(block):
                return pl.ds(pl.multiple_of(block * model + hp * PAIR, 128), PAIR)

            q2 = qs[rs, lanes(0)] * jnp.asarray(HEAD**-0.5, BF)
            s = mm_nt(split_heads(qs[rs, lanes(1)], low), q2)
            halves = []
            for h in range(2):
                sh = jnp.where(ok, s[h * 128:(h + 1) * 128], MASKED)
                e = jnp.exp(sh - jnp.max(sh, 0, keepdims=True))
                halves.append((e * (1.0 / jnp.sum(e, 0, keepdims=True))).astype(BF))
            pc = jnp.concatenate(halves, axis=0)
            ps[it] = pc
            os_[rs, lanes(0)] = mm_tn(pc, split_heads(qs[rs, lanes(2)], low)).astype(BF)

        out(ps, PP.at[slot], 4)
        out(os_, O.at[slot], 5)
        weights.start("down")
        weights.wait("out")
        hs[...] = xs[...].astype(F32) + mm(os_[...], wo[...])
        out(hs, H.at[slot], 6)
        gain2, bias2 = norms[2:3, :], norms[3:4, :]
        for i in range(seqs):
            sl = pl.ds(i * 64, 64)
            n, _r = norm_of(hs[sl, :])
            cs[sl, :] = (n * gain2 + bias2).astype(BF)
        out(cs, C.at[slot], 7)
        acc[...] = hs[...]
        parts = ff // model

        @pl.loop(0, parts)
        def _(j):
            sl = chunk(j, model)
            weights.wait("up", j)
            m, g = gelu_pair(mm(cs[...], wup[:, sl]))
            ms[:, sl] = m.astype(BF)
            gs[:, sl] = g.astype(BF)
            pltpu.make_async_copy(ms.at[:, sl], MM.at[slot, :, sl], sem.at[10 + 2 * j]).start()
            pltpu.make_async_copy(gs.at[:, sl], GP.at[slot, :, sl], sem.at[11 + 2 * j]).start()
            weights.wait("down", j)
            acc[...] += mm(ms[:, sl], wdn[sl, :])

        ys[...] = acc[...].astype(BF)
        for j in range(parts):
            sl = pl.ds(j * model, model)
            copies.append(pltpu.make_async_copy(ms.at[:, sl], MM.at[slot, :, sl], sem.at[10 + 2 * j]))
            copies.append(pltpu.make_async_copy(gs.at[:, sl], GP.at[slot, :, sl], sem.at[11 + 2 * j]))
        out(ys, yout, 8)
        if last:
            out(ys, HID.at[slot], 9)
        if slot < own:
            out(ys, Y.at[slot], 1)

        if last and slot < own:
            for i in range(seqs):
                n, _r = norm_of(ys[pl.ds(i * 64, 64), :].astype(F32))
                count = length(i)
                ok = lax.broadcasted_iota(jnp.int32, (64, 1), 0) < count
                nb[pl.ds(i, 1), :] = jnp.sum(jnp.where(ok, n, 0.0), 0, keepdims=True) / count.astype(F32)
            cp = pltpu.make_async_copy(nb, NB.at[slot], sem.at[0])
            cp.start()
            cp.wait()

        for cp in copies:
            cp.wait()


def sub_call(body, fixed, specs, weights, held, shapes, scratch, bufs, last_shape, name):
    n, many = len(fixed) + 4, len(shapes)
    alias = {}
    extra = []
    kernel = body
    if held:
        alias = {len(fixed) + i: many + i for i in range(4)}
        weights = [vmem(w) for w in weights]
    else:
        weights = [hbm(w) for w in weights]
    if bufs is not None:
        alias |= {n + i: i for i in range(many)}
        extra = [hbm(v) for v in bufs]

        def kernel(*refs):
            body(*refs[:n], *refs[n + many:])

    res = pl.pallas_call(
        kernel,
        out_shape=[pltpu.HBM(s, d) for s, d in shapes]
        + [pltpu.VMEM(w.shape[-2:], BF) for w in weights]
        + [jax.ShapeDtypeStruct(*last_shape)],
        in_specs=specs + [VMEM if held else ANY] * 4 + [ANY] * len(extra),
        out_specs=[ANY] * many + [VMEM] * 4 + [pl.BlockSpec(memory_space=pl.ANY)],
        input_output_aliases=alias,
        scratch_shapes=scratch,
        compiler_params=pltpu.CompilerParams(vmem_limit_bytes=VLIM),
        cost_estimate=FREE,
        name=name,
    )(*fixed, *weights, *extra)
    return res[:many], res[many:many + 4], res[-1]


def fwd_call(place, slot, own, last, info, first, first_at, norms, weights, bufs, slots):
    model, ff = weights[2].shape[-2:]
    pairs = ROWS // 128 * (HEADS // 2)
    small = ((slots, ROWS, model), BF)
    wide = ((slots, ROWS, ff), BF)
    shapes = [
        small,
        small,
        ((slots, ROWS, 3 * model), BF),
        ((slots, pairs, 256, 128), BF),
        small,
        ((slots, ROWS, model), F32),
        small,
        wide,
        wide,
        small,
        ((own, ROWS // 64, model), F32),
        ((own, ROWS, model), BF),
    ]
    scratch = [
        pltpu.VMEM((ROWS, model), BF),
        pltpu.VMEM((ROWS, model), BF),
        pltpu.VMEM((ROWS, 3 * model), BF),
        pltpu.VMEM((pairs, 256, 128), BF),
        pltpu.VMEM((ROWS, model), BF),
        pltpu.VMEM((ROWS, model), F32),
        pltpu.VMEM((ROWS, model), BF),
        pltpu.VMEM((ROWS, ff), BF),
        pltpu.VMEM((ROWS, ff), BF),
        pltpu.VMEM((ROWS, model), BF),
        pltpu.VMEM((ROWS, model), F32),
        pltpu.VMEM((ROWS // 64, model), F32),
        pltpu.SemaphoreType.DMA((11 + 2 * (ff // model),)),
        pltpu.SemaphoreType.DMA((4 + 2 * (ff // model),)),
    ]
    fresh = bufs is None
    fixed = [info, first, norms]
    specs = [SMEM, pl.BlockSpec(memory_space=pl.ANY), VMEM]
    body = functools.partial(fwd_kernel, fresh, place, slot, own, last, first_at, model, ff)
    return sub_call(body, fixed, specs, weights, not fresh, shapes, scratch, bufs, ((ROWS, model), BF), "block_forward")


def bwd_kernel(place, slot, own, first_at, model, ff, info, first, norms, X, QKV, PP, H, GP, w1, w2, w3, w4, *rest):
    (E, DU, F, DQ, LNG, DXO, wqkv, wo, wup, wdn, dxo,
     es, xs, qs, ps, hs, gs, dus, dcs, dhs, fs, dos, dqs, dxs, dxb, lng, sem, gsem) = rest
    seqs = ROWS // 64

    @pl.when(info[SECTION] == place)
    def _():
        come = pltpu.make_async_copy(first.at[pl.ds(first_at, ROWS)], es, sem.at[0])
        come.start()
        copies = []

        def out(src, dst, k):
            cp = pltpu.make_async_copy(src, dst, sem.at[k])
            cp.start()
            copies.append(cp)

        def gelu_slope(j):
            sl = chunk(j, model)
            return pltpu.make_async_copy(GP.at[slot, :, sl], gs.at[:, sl], gsem.at[j])

        parts = ff // model
        for j in range(parts):
            gelu_slope(j).start()
        loads = {}
        for k, (name, src, dst) in enumerate((("h", H, hs), ("p", PP, ps), ("qkv", QKV, qs), ("x", X, xs))):
            loads[name] = pltpu.make_async_copy(src.at[slot], dst, sem.at[1 + k])
        come.wait()
        out(es, E.at[slot], 6)
        dcs[...] = jnp.zeros_like(dcs)

        @pl.loop(0, parts)
        def _(j):
            sl = chunk(j, model)
            gelu_slope(j).wait()

            @pl.when(j == 1)
            def _():
                loads["h"].start()
                loads["p"].start()
                loads["qkv"].start()

            du = (mm_nt(es[...], wdn[sl, :]) * gs[:, sl].astype(F32)).astype(BF)
            dus[:, sl] = du
            dcs[...] += mm_nt(du, wup[:, sl])

        out(dus, DU.at[slot], 7)
        loads["x"].start()
        loads["h"].wait()
        sums = [jnp.zeros((8, model), F32) for _ in range(4)]

        def fold(v):
            return jnp.sum(v.reshape(8, 8, model), axis=0)

        gain = norms[2:3, :]
        for i in range(seqs):
            sl = pl.ds(i * 64, 64)
            n, r = norm_of(hs[sl, :])
            dc = dcs[sl, :]
            sums[2] += fold(dc * n)
            sums[3] += fold(dc)
            dh = es[sl, :].astype(F32) + norm_back(n, r, dc * gain)
            dhs[sl, :] = dh
            fs[sl, :] = dh.astype(BF)
        lng[2] = sums[2]
        lng[3] = sums[3]
        out(fs, F.at[slot], 8)
        dos[...] = mm_nt(fs[...], wo[...]).astype(BF)
        loads["p"].wait()
        loads["qkv"].wait()
        low = low_lanes()

        @pl.loop(0, ROWS // 128 * (HEADS // 2), unroll=UNROLL)
        def _(it):
            p = it // (HEADS // 2)
            hp = it % (HEADS // 2)
            rs = pl.ds(pl.multiple_of(p * 128, 128), 128)

            def lanes(block):
                return pl.ds(pl.multiple_of(block * model + hp * PAIR, 128), PAIR)

            q2 = qs[rs, lanes(0)]
            do2 = dos[rs, lanes(0)]
            pc = ps[it]
            t = pc.astype(F32) * mm_nt(split_heads(qs[rs, lanes(2)], low), do2)
            halves = []
            for h in range(2):
                hl = slice(h * 128, (h + 1) * 128)
                halves.append((t[hl] - pc[hl].astype(F32) * jnp.sum(t[hl], 0, keepdims=True)).astype(BF))
            ds = jnp.concatenate(halves, axis=0)
            scale = HEAD**-0.5
            dq = mm_tn(ds, split_heads(qs[rs, lanes(1)], low)) * scale
            dk = mm(ds, q2) * scale
            dv = mm(pc, do2)
            dqs[rs, lanes(0)] = dq.astype(BF)
            dqs[rs, lanes(1)] = jnp.where(low, dk[:128], dk[128:]).astype(BF)
            dqs[rs, lanes(2)] = jnp.where(low, dv[:128], dv[128:]).astype(BF)

        out(dqs, DQ.at[slot], 9)
        dcs[...] = jnp.zeros_like(dcs)

        @pl.loop(0, 3)
        def _(j):
            sl = chunk(j, model)
            dcs[...] += mm_nt(dqs[:, sl], wqkv[:, sl])

        loads["x"].wait()
        gain = norms[0:1, :]
        for i in range(seqs):
            sl = pl.ds(i * 64, 64)
            n, r = norm_of(xs[sl, :].astype(F32))
            da = dcs[sl, :]
            sums[0] += fold(da * n)
            sums[1] += fold(da)
            dx = dhs[sl, :] + norm_back(n, r, da * gain)
            dxs[sl, :] = dx
            dxb[sl, :] = dx.astype(BF)
        out(dxb, dxo, 10)
        lng[0] = sums[0]
        lng[1] = sums[1]
        out(lng, LNG.at[slot], 11)

        if slot < own:
            out(dxs, DXO.at[slot], 12)

        for cp in copies:
            cp.wait()


def bwd_call(place, slot, own, info, first, first_at, norms, weights, saved, bufs, slots):
    model, ff = weights[2].shape[-2:]
    pairs = ROWS // 128 * (HEADS // 2)
    X, A, QKV, PP, O, H, C, MM, GP = saved
    small = ((slots, ROWS, model), BF)
    shapes = [
        small,
        ((slots, ROWS, ff), BF),
        small,
        ((slots, ROWS, 3 * model), BF),
        ((slots, 4, 8, model), F32),
        ((own, ROWS, model), F32),
    ]
    scratch = [
        pltpu.VMEM((ROWS, model), BF),
        pltpu.VMEM((ROWS, model), BF),
        pltpu.VMEM((ROWS, 3 * model), BF),
        pltpu.VMEM((pairs, 256, 128), BF),
        pltpu.VMEM((ROWS, model), F32),
        pltpu.VMEM((ROWS, ff), BF),
        pltpu.VMEM((ROWS, ff), BF),
        pltpu.VMEM((ROWS, model), F32),
        pltpu.VMEM((ROWS, model), F32),
        pltpu.VMEM((ROWS, model), BF),
        pltpu.VMEM((ROWS, model), BF),
        pltpu.VMEM((ROWS, 3 * model), BF),
        pltpu.VMEM((ROWS, model), F32),
        pltpu.VMEM((ROWS, model), BF),
        pltpu.VMEM((4, 8, model), F32),
        pltpu.SemaphoreType.DMA((13,)),
        pltpu.SemaphoreType.DMA((ff // model,)),
    ]
    fixed = [info, first, norms, *[hbm(v) for v in (X, QKV, PP, H, GP)]]
    specs = [SMEM, pl.BlockSpec(memory_space=pl.ANY), VMEM] + [ANY] * 5
    body = functools.partial(bwd_kernel, place, slot, own, first_at, model, ff)
    return sub_call(body, fixed, specs, weights, True, shapes, scratch, bufs, ((ROWS, model), BF), "block_backward")


def head_kernel(own, flip, last, info, fg, fb, proj, hid, first, *rest):
    more, (loss, gproj, gfin, hdy, dpool, ysc, dsc, sem) = rest[:-8], rest[-8:]
    model = proj.shape[0]
    scale = 1.5 * model**0.5
    gain, bias = fg[...].reshape(1, model), fb[...].reshape(1, model)
    about = first[...]
    if more:
        about = jnp.where(info[SECTION] == len(more), about, sum(v[...] for v in more))
    nbar = about[:, 0:model]
    image = about[:, model:2 * model]
    pidx = about[:, 2 * model:2 * model + 1].astype(jnp.int32)
    pooled = (nbar * gain + bias).astype(BF)
    text = mm(pooled, proj[...])
    inv = lax.rsqrt(jnp.sum(text * text, -1, keepdims=True) + EPS)
    unit = text * inv
    iunit = (image * lax.rsqrt(jnp.sum(image * image, -1, keepdims=True) + EPS)).astype(BF)
    logits = scale * mm_nt(unit.astype(BF), iunit)
    rmax = jnp.max(logits, 1, keepdims=True)
    rlse = rmax + jnp.log(jnp.sum(jnp.exp(logits - rmax), 1, keepdims=True))
    cmax = jnp.max(logits, 0, keepdims=True)
    clse = cmax + jnp.log(jnp.sum(jnp.exp(logits - cmax), 0, keepdims=True))
    n = logits.shape[0]
    hot = lax.broadcasted_iota(jnp.int32, (n, n), 1) == pidx
    g = 0.5 * jnp.exp(logits - rlse) + 0.5 * jnp.exp(logits - clse) - jnp.where(hot, 1.0, 0.0)
    dt = scale * mm(g.astype(BF), iunit)
    dtext = ((dt - unit * jnp.sum(dt * unit, -1, keepdims=True)) * inv).astype(BF)
    dp = mm_nt(dtext, proj[...])
    if last is None:
        at = jnp.sum(jnp.where(hot, logits, 0.0), 1, keepdims=True)
        col = jnp.sum(jnp.where(hot, jnp.broadcast_to(clse, (n, n)), 0.0), 1, keepdims=True)
        loss[...] = jnp.broadcast_to(0.5 * (rlse - at) + 0.5 * (col - at), loss.shape)
        gproj[...] = mm_tn(pooled, dtext)
        gfin[0:1, :] = jnp.sum(dp * nbar, 0, keepdims=True)
        gfin[1:2, :] = jnp.sum(dp, 0, keepdims=True)

    @pl.when(info[SECTION] == (-1 if last is None else last))
    def _():
        dpool[...] = dp
        per = ROWS // 64
        blocks = hid.shape[0]
        loads, stores = [], []
        for m in range(blocks):
            cp = pltpu.make_async_copy(hid.at[m], ysc.at[m], sem.at[m])
            cp.start()
            loads.append(cp)
        for m in range(blocks):
            loads[m].wait()
            of = info[GROUP] if m < own else info[GROUP] ^ flip
            for i in range(per):
                count = info[LENS + m * per + i]
                nn, r = norm_of(ysc[m, pl.ds(i * 64, 64), :].astype(F32))
                w = dpool[pl.ds(of * own * per + (m % own) * per + i, 1), :] * (gain / count.astype(F32))
                ok = lax.broadcasted_iota(jnp.int32, (64, 1), 0) < count
                dsc[pl.ds(m * ROWS + i * 64, 64), :] = jnp.where(ok, norm_back(nn, r, w), 0.0).astype(BF)
            part = pl.ds(m * ROWS, ROWS)
            cp = pltpu.make_async_copy(dsc.at[part], hdy.at[part], sem.at[blocks + m])
            cp.start()
            stores.append(cp)
        for cp in stores:
            cp.wait()


def head_call(own, flip, last, info, fg, fb, proj, hid, *about):
    blocks, _, model = hid.shape
    pairs = about[0].shape[0]
    return pl.pallas_call(
        functools.partial(head_kernel, own, flip, last),
        out_shape=[
            jax.ShapeDtypeStruct((pairs, 128), F32),
            jax.ShapeDtypeStruct((model, model), F32),
            jax.ShapeDtypeStruct((8, model), F32),
            pltpu.HBM((blocks * ROWS, model), BF),
        ],
        in_specs=[SMEM] + [VMEM] * 3 + [ANY] + [VMEM] * len(about),
        out_specs=[VMEM, VMEM, VMEM, ANY],
        scratch_shapes=[
            pltpu.VMEM((pairs, model), F32),
            pltpu.VMEM((blocks, ROWS, model), BF),
            pltpu.VMEM((blocks * ROWS, model), BF),
            pltpu.SemaphoreType.DMA((2 * blocks,)),
        ],
        compiler_params=pltpu.CompilerParams(vmem_limit_bytes=VLIM),
        cost_estimate=FREE,
        name="head",
    )(info, fg, fb, proj, hbm(hid), *about)


def wgrad_kernel(where, a, e, o, turned):
    @pl.when(pl.program_id(1) == 0)
    def _():
        for s in range(a.shape[0]):
            turned[:, pl.ds(s * ROWS, ROWS)] = a[s].T

    right = e[...].reshape(e.shape[0] * ROWS, e.shape[2])
    o[...] = mm(turned[...], right).astype(BF)


def wgrad(where, left, right):
    slots, _, wide = left.shape
    cols = right.shape[2]
    mine = wide // 2
    step = math.gcd(mine, 768)
    width = 768
    left_blocks = mine // step
    return pl.pallas_call(
        wgrad_kernel,
        grid_spec=pltpu.PrefetchScalarGridSpec(
            num_scalar_prefetch=1,
            grid=(left_blocks, cols // width),
            in_specs=[
                pl.BlockSpec((slots, ROWS, step), lambda i, j, w: (0, 0, w[0] * left_blocks + i)),
                pl.BlockSpec((slots, ROWS, width), lambda i, j, w: (0, 0, j)),
            ],
            out_specs=pl.BlockSpec((step, width), lambda i, j, w: (i, j)),
            scratch_shapes=[pltpu.VMEM((step, slots * ROWS), BF)],
        ),
        out_shape=pltpu.HBM((mine, cols), BF),
        compiler_params=pltpu.CompilerParams(vmem_limit_bytes=VLIM),
        cost_estimate=FREE,
        name="weight_grad",
    )(where, hbm(left), hbm(right))


def swap_bit(value, axis, bit):
    peers = lax.axis_size(axis)
    return lax.ppermute(value, axis, [(i, i ^ (1 << bit)) for i in range(peers)])


def pack_kernel(pairs, nb, img, o):
    model = img.shape[1]
    n, per = nb.shape[:2]
    for i in range(n):
        o[pl.ds(i * per, per), 0:model] = nb[i]
    o[:, model:2 * model] = img[...].astype(F32)
    for i in range(n * per):
        o[pl.ds(i, 1), 2 * model:] = jnp.full((1, 128), pairs[i], jnp.int32).astype(F32)


def join_kernel(bit, info, value, other, o):
    n = value.shape[0]
    high = (info[GROUP] >> bit) & 1
    o[pl.ds(pl.multiple_of(high * n, 8), n), :] = value[...]
    o[pl.ds(pl.multiple_of((1 - high) * n, 8), n), :] = other[...]


def small_call(body, specs, shape, name, *args):
    return pl.pallas_call(
        body,
        out_shape=jax.ShapeDtypeStruct(shape, F32),
        in_specs=specs,
        out_specs=VMEM,
        compiler_params=pltpu.CompilerParams(vmem_limit_bytes=8 << 20),
        cost_estimate=FREE,
        name=name,
    )(*args)


def joined(info, bit, value, other):
    shape = (2 * value.shape[0], value.shape[1])
    return small_call(functools.partial(join_kernel, bit), [SMEM, VMEM, VMEM], shape, "join", info, value, other)


def scattered(value, axis, bits, total_bits):
    me = lax.axis_index(axis)
    rows, cols = value.shape
    value = value.reshape((2,) * total_bits + (rows >> total_bits, cols))
    left = list(range(total_bits - 1, -1, -1))
    for place, bit in enumerate(bits):
        at = left.index(bit)
        mine = (me >> bit) & 1
        keep = lax.dynamic_index_in_dim(value, mine, at, keepdims=False)
        send = lax.dynamic_index_in_dim(value, 1 - mine, at, keepdims=False)
        value = keep.astype(F32) + swap_bit(send, axis, bit).astype(F32)
        if place < len(bits) - 1:
            value = value.astype(BF)
        left.remove(bit)
    return value


def on_device(tokens, lengths, pair_index, images, ln1_gain, ln1_bias, qkv_weight, out_weight,
              ln2_gain, ln2_bias, up_weight, down_weight, final_gain, final_bias, proj_weight):
    groups = lax.axis_size("dp")
    sections = lax.axis_size("section")
    section = lax.axis_index("section")
    group = lax.axis_index("dp")
    model = tokens.shape[1]
    n_seq = lengths.shape[0]
    flip = groups - 2
    half = group // (groups // 2)
    own = tokens.shape[0] // ROWS
    slots = 2 * own

    places = sorted(((s * 1.6 + m, s, m) for s in range(sections) for m in range(slots)))
    places = [(s, m) for _, s, m in places]
    last = sections - 1
    norms = jnp.concatenate([ln1_gain, ln1_bias, ln2_gain, ln2_bias], 0)
    weights = (qkv_weight, out_weight, up_weight, down_weight)
    who = jnp.stack([section, group]).astype(jnp.int32)
    info_own = jnp.concatenate([who, lengths, lengths])
    theirs = lax.ppermute(
        tokens, ("dp", "section"), [(d * sections, (d ^ flip) * sections) for d in range(groups)]
    )
    theirs_lengths = lax.ppermute(lengths, "dp", [(d, d ^ flip) for d in range(groups)])
    info = jnp.concatenate([who, lengths, theirs_lengths])
    bufs = about = coming = bit = None
    hop = {}
    for k, (s, m) in enumerate(places):
        source, at = (tokens, m * ROWS) if m < own else (theirs, (m - own) * ROWS)
        if s > 0:
            source, at = hop[s - 1, m], 0
        bufs, weights, y = fwd_call(
            s, m, own, s == last, info_own if m < own else info, source, at, norms, weights, bufs, slots
        )
        if s < last:
            hop[s, m] = lax.ppermute(y, "section", [(s, s + 1)])
        if s == last and m >= own - 1:
            if m == own - 1:
                about = small_call(
                    pack_kernel, [SMEM, VMEM, VMEM], (n_seq, 2 * model + 128), "pack", pair_index, bufs[10], images
                )
                bit = 0
            else:
                coming, _ = lax.optimization_barrier((coming, y))
                about = joined(info, bit, about, coming)
                bit += 1
            coming = swap_bit(about, "dp", bit)
    saved, hid = bufs[:9], bufs[9]
    for bit in range(bit, groups.bit_length() - 1):
        about = joined(info, bit, about, coming)
        if bit < groups.bit_length() - 2:
            coming = swap_bit(about, "dp", bit + 1)
    hdy = head_call(own, flip, last, info, final_gain, final_bias, proj_weight, hid, about)[3]

    back = None
    step = {}
    shared = None
    for k, (s, m) in enumerate(places):
        source, at = (hdy, m * ROWS) if s == 0 else (step[s - 1, m], 0)
        here = last - s
        back, weights, dx = bwd_call(here, m, own, info, source, at, norms, weights, saved, back, slots)
        if here > 0:
            step[s, m] = lax.ppermute(dx, "section", [(here, here - 1)])
        if (s, m) == (0, 1):
            about_late, _ = lax.optimization_barrier((about, dx))
            shared = [lax.ppermute(about_late, "section", [(last, t)]) for t in range(last)]
    E, DU, F, DQ, LNG, DXO = back
    X, A, QKV, PP, O, H, C, MM, GP = saved

    where = half[None].astype(jnp.int32)
    bits = (groups // 2).bit_length() - 1
    low_first = list(range(bits))
    high_first = low_first[::-1]
    norm_sums = lax.dynamic_slice_in_dim(jnp.sum(LNG, (0, 2)), half * (model // 2), model // 2, 1)
    norm_sums = jnp.pad(norm_sums.T, ((0, 0), (0, 124))).astype(BF)
    sums = []
    for a, e in ((MM, E), (C, DU), (A, DQ), (O, F)):
        sums.append(wgrad(where, a, e))
        where, _ = lax.optimization_barrier((where, sums[-1]))
    sums[3] = jnp.concatenate([sums[3], norm_sums], 1)
    g_down, g_up, g_qkv, g_out = [
        scattered(v, "dp", order, bits) for v, order in zip(sums, (low_first, high_first, high_first, low_first))
    ]
    g_norm = g_out[:, model:model + 4].T
    about_late, _ = lax.optimization_barrier((about, sums[3]))
    tail = head_call(own, flip, None, info, final_gain, final_bias, proj_weight, hid, about_late, *shared)
    return (
        bufs[11].reshape(1, own * ROWS, model),
        DXO.reshape(1, own * ROWS, model),
        g_norm[0:1],
        g_norm[1:2],
        g_qkv[None],
        g_out[None, :, :model],
        g_norm[2:3],
        g_norm[3:4],
        g_up[None],
        g_down[None],
        tail[2][0],
        tail[2][1],
        tail[1],
        tail[0][:, 0],
    )


def solution(mesh):
    row = P("section", None)
    cube = P("section", None, None)
    in_specs = (P("dp", None), P("dp"), P("dp"), P("dp", None), row, row, cube, cube, row, row, cube, cube, P(), P(), P())
    big = P("section", "dp", None)
    small = P("section", "dp")
    out_specs = (big, big, small, small, big, big, small, small, big, big, P(), P(), P(), P())
    return jax.shard_map(on_device, mesh=mesh, in_specs=in_specs, out_specs=out_specs, check_vma=False)
```

```python
import functools
import math

import jax
import jax.numpy as jnp
from jax import lax
from jax.experimental import pallas as pl
from jax.experimental.pallas import tpu as pltpu
from jax.sharding import PartitionSpec as P

HEADS = 12
HEAD = 64
PAIR = 2 * HEAD
ROWS = 256
EPS = 1e-06
MASKED = -1000000000.0
BF = jnp.bfloat16
F32 = jnp.float32
ANY = pl.BlockSpec(memory_space=pltpu.HBM)
LOOSE = pl.BlockSpec(memory_space=pl.ANY)
SMEM = pl.BlockSpec(memory_space=pltpu.SMEM)
VMEM = pl.BlockSpec(memory_space=pltpu.VMEM)
VLIM = 24 << 20
LAG = 2
FREE = pl.CostEstimate(flops=1, bytes_accessed=1, transcendentals=0)
SECTION, GROUP, LENS = range(3)


def hbm(v):
    return pltpu.with_memory_space_constraint(v, pltpu.HBM)


def vmem(v):
    return pltpu.with_memory_space_constraint(v, pltpu.VMEM)


def mm(a, b):
    return jnp.dot(a, b, preferred_element_type=F32)


def mm_nt(a, b):
    return lax.dot_general(a, b, (((1,), (1,)), ((), ())), preferred_element_type=F32)


def mm_tn(a, b):
    return lax.dot_general(a, b, (((0,), (0,)), ((), ())), preferred_element_type=F32)


def norm_of(v):
    c = v - jnp.mean(v, -1, keepdims=True)
    r = lax.rsqrt(jnp.mean(c * c, -1, keepdims=True) + EPS)
    return c * r, r


def norm_back(n, r, w):
    return r * (w - jnp.mean(w, -1, keepdims=True) - n * jnp.mean(w * n, -1, keepdims=True))


def gelu_pair(u):
    k = 0.7978845608028654
    u2 = u * u
    t = jnp.tanh(u * (k + (k * 0.044715) * u2))
    p = 0.5 + 0.5 * t
    g = p + (0.5 * u) * ((1.0 - t * t) * (k + (3.0 * k * 0.044715) * u2))
    return u * p, g


def split_heads(v, low):
    z = jnp.zeros_like(v)
    return jnp.concatenate([jnp.where(low, v, z), jnp.where(low, z, v)], axis=0)


def low_lanes():
    return lax.broadcasted_iota(jnp.int32, (PAIR, PAIR), 1) < HEAD


def chunk(j, width):
    return pl.ds(pl.multiple_of(j * width, 128), width)


class Weights:
    def __init__(self, sources, held, sem, model):
        self.sem, self.jobs, self.due = sem, {}, sources is not None
        if not self.due:
            return
        k = 0
        for name, src, dst in zip(("qkv", "out", "up", "down"), sources, held):
            rows, cols = dst.shape
            for j in range(max(rows, cols) // model):
                piece = pl.ds(j * model, model)
                at = (slice(None), piece) if cols > model else (piece, slice(None))
                self.jobs[name, j] = (src, dst, at, k)
                k += 1

    def copy(self, name, j, offset=0):
        src, dst, at, k = self.jobs[name, j]
        return pltpu.make_async_copy(src.at[(0,) + at], dst.at[at], self.sem.at[k + offset])

    def start(self, name, *pieces):
        for j in pieces or [j for n, j in self.jobs if n == name]:
            self.copy(name, j).start()

    def wait(self, name, j=0):
        if self.due:
            self.copy(name, 0, j).wait()


def fetch(info, tok, tok_at, arr, dst, sem):
    def from_tok():
        pltpu.make_async_copy(tok.at[pl.ds(tok_at, ROWS)], dst, sem).start()

    def from_arr():
        pltpu.make_async_copy(arr.at[pl.ds(0, ROWS)], dst, sem).start()

    if tok is None:
        from_arr()
    elif arr is None:
        from_tok()
    else:
        pl.when(info == 0)(from_tok)
        pl.when(info != 0)(from_arr)
    return pltpu.make_async_copy((arr if tok is None else tok).at[pl.ds(0, ROWS)], dst, sem)


def fwd_kernel(fresh, site, slots, own, last, tok_at, has, model, ff, info, *rest):
    tok = rest[0] if has[0] else None
    arr = rest[has[0]] if has[1] else None
    norms, w1, w2, w3, w4, *rest = rest[sum(has):]
    (X, A, QKV, PP, O, H, C, MM, GP, HID, NB, Y, wqkv, wo, wup, wdn, yout,
     xs, as_, qs, ps, os_, hs, cs, ms, gs, ys, nb, sem, wsem) = rest
    weights = Weights((w1, w2, w3, w4) if fresh else None, (wqkv, wo, wup, wdn), wsem, model)
    names = ("qkv", "out", "up", "down")
    seqs = ROWS // 64
    section = info[SECTION]
    slot = site - LAG * section
    active = (slot >= 0) & (slot < slots)

    def length(i):
        return info[LENS + slot * seqs + i]

    if fresh:
        @pl.when(jnp.logical_not(active))
        def _():
            for name in names:
                weights.start(name)
            for name, j in weights.jobs:
                weights.wait(name, j)

    @pl.when(active)
    def _():
        come = fetch(section, tok, tok_at, arr, xs, sem.at[0])
        weights.start("qkv")
        come.wait()
        copies = []

        def out(src, dst, k):
            cp = pltpu.make_async_copy(src, dst, sem.at[k])
            cp.start()
            copies.append(cp)

        out(xs, X.at[slot], 18)
        gain, bias = norms[0:1, :], norms[1:2, :]
        for i in range(seqs):
            sl = pl.ds(i * 64, 64)
            n, _r = norm_of(xs[sl, :].astype(F32))
            as_[sl, :] = (n * gain + bias).astype(BF)
        out(as_, A.at[slot], 2)

        for j in range(3):
            sl = pl.ds(j * model, model)
            weights.wait("qkv", j)
            qs[:, sl] = mm(as_[...], wqkv[:, sl]).astype(BF)

        weights.start("out")
        weights.start("up")

        out(qs, QKV.at[slot], 3)
        low = low_lanes()
        row = lax.broadcasted_iota(jnp.int32, (PAIR, PAIR), 0)
        col = lax.broadcasted_iota(jnp.int32, (PAIR, PAIR), 1)

        for it in range(ROWS // 128 * (HEADS // 2)):
            p, hp = divmod(it, HEADS // 2)
            if hp == 0:
                ok = ((col < 64) & (row < length(2 * p))) | ((col >= 64) & (row >= 64) & (row < 64 + length(2 * p + 1)))
            rs = pl.ds(p * 128, 128)

            def lanes(block):
                return pl.ds(block * model + hp * PAIR, PAIR)

            q2 = qs[rs, lanes(0)] * jnp.asarray(HEAD**-0.5, BF)
            s = mm_nt(split_heads(qs[rs, lanes(1)], low), q2)
            halves = []
            for h in range(2):
                sh = jnp.where(ok, s[h * 128:(h + 1) * 128], MASKED)
                e = jnp.exp(sh - jnp.max(sh, 0, keepdims=True))
                halves.append((e * (1.0 / jnp.sum(e, 0, keepdims=True))).astype(BF))
            pc = jnp.concatenate(halves, axis=0)
            ps[it] = pc
            os_[rs, lanes(0)] = mm_tn(pc, split_heads(qs[rs, lanes(2)], low)).astype(BF)

        out(ps, PP.at[slot], 4)
        out(os_, O.at[slot], 5)
        weights.start("down")
        weights.wait("out")
        hs[...] = xs[...].astype(F32) + mm(os_[...], wo[...])
        out(hs, H.at[slot], 6)
        gain2, bias2 = norms[2:3, :], norms[3:4, :]
        for i in range(seqs):
            sl = pl.ds(i * 64, 64)
            n, _r = norm_of(hs[sl, :])
            cs[sl, :] = (n * gain2 + bias2).astype(BF)
        out(cs, C.at[slot], 7)
        parts = ff // model
        total = hs[...]
        for j in range(parts):
            sl = pl.ds(j * model, model)
            weights.wait("up", j)
            m, g = gelu_pair(mm(cs[...], wup[:, sl]))
            ms[:, sl] = m.astype(BF)
            gs[:, sl] = g.astype(BF)
            out(ms.at[:, sl], MM.at[slot, :, sl], 10 + 2 * j)
            out(gs.at[:, sl], GP.at[slot, :, sl], 11 + 2 * j)
            weights.wait("down", j)
            total = total + mm(ms[:, sl], wdn[sl, :])
        ys[...] = total.astype(BF)
        out(ys, yout, 8)
        for cp in copies:
            cp.wait()

        @pl.when(slot < own)
        def _():
            cp = pltpu.make_async_copy(ys, Y.at[slot], sem.at[1])
            cp.start()
            cp.wait()

        if site >= LAG * last:
            @pl.when(section == last)
            def _():
                cp = pltpu.make_async_copy(ys, HID.at[slot], sem.at[9])
                cp.start()
                if site - LAG * last < own:
                    for i in range(seqs):
                        n, _r = norm_of(ys[pl.ds(i * 64, 64), :].astype(F32))
                        count = length(i)
                        ok = lax.broadcasted_iota(jnp.int32, (64, 1), 0) < count
                        nb[pl.ds(i, 1), :] = jnp.sum(jnp.where(ok, n, 0.0), 0, keepdims=True) / count.astype(F32)
                    cp2 = pltpu.make_async_copy(nb, NB.at[slot], sem.at[0])
                    cp2.start()
                    cp2.wait()
                cp.wait()


def sub_call(body, fixed, specs, weights, held, shapes, scratch, bufs, last_shape, name):
    n, many = len(fixed) + 4, len(shapes)
    alias = {}
    extra = []
    kernel = body
    if held:
        alias = {len(fixed) + i: many + i for i in range(4)}
        weights = [vmem(w) for w in weights]
    else:
        weights = [hbm(w) for w in weights]
    if bufs is not None:
        alias |= {n + i: i for i in range(many)}
        extra = [hbm(v) for v in bufs]

        def kernel(*refs):
            body(*refs[:n], *refs[n + many:])

    res = pl.pallas_call(
        kernel,
        out_shape=[pltpu.HBM(s, d) for s, d in shapes]
        + [pltpu.VMEM(w.shape[-2:], BF) for w in weights]
        + [jax.ShapeDtypeStruct(*last_shape)],
        in_specs=specs + [VMEM if held else ANY] * 4 + [ANY] * len(extra),
        out_specs=[ANY] * many + [VMEM] * 4 + [pl.BlockSpec(memory_space=pl.ANY)],
        input_output_aliases=alias,
        scratch_shapes=scratch,
        compiler_params=pltpu.CompilerParams(vmem_limit_bytes=VLIM),
        cost_estimate=FREE,
        name=name,
    )(*fixed, *weights, *extra)
    return res[:many], res[many:many + 4], res[-1]


def site_inputs(tok, arr):
    has = (tok is not None, arr is not None)
    return has, [v for v in (None if tok is None else hbm(tok), arr) if v is not None]


def fwd_call(site, own, last, info, tok, tok_at, arr, norms, weights, bufs, slots):
    model, ff = weights[2].shape[-2:]
    pairs = ROWS // 128 * (HEADS // 2)
    small = ((slots, ROWS, model), BF)
    wide = ((slots, ROWS, ff), BF)
    shapes = [
        small,
        small,
        ((slots, ROWS, 3 * model), BF),
        ((slots, pairs, 256, 128), BF),
        small,
        ((slots, ROWS, model), F32),
        small,
        wide,
        wide,
        small,
        ((own, ROWS // 64, model), F32),
        ((own, ROWS, model), BF),
    ]
    scratch = [
        pltpu.VMEM((ROWS, model), BF),
        pltpu.VMEM((ROWS, model), BF),
        pltpu.VMEM((ROWS, 3 * model), BF),
        pltpu.VMEM((pairs, 256, 128), BF),
        pltpu.VMEM((ROWS, model), BF),
        pltpu.VMEM((ROWS, model), F32),
        pltpu.VMEM((ROWS, model), BF),
        pltpu.VMEM((ROWS, ff), BF),
        pltpu.VMEM((ROWS, ff), BF),
        pltpu.VMEM((ROWS, model), BF),
        pltpu.VMEM((ROWS // 64, model), F32),
        pltpu.SemaphoreType.DMA((11 + 2 * (ff // model),)),
        pltpu.SemaphoreType.DMA((4 + 2 * (ff // model),)),
    ]
    fresh = bufs is None
    has, sources = site_inputs(tok, arr)
    fixed = [info, *sources, norms]
    specs = [SMEM, *[LOOSE for _ in sources], VMEM]
    body = functools.partial(fwd_kernel, fresh, site, slots, own, last, tok_at, has, model, ff)
    return sub_call(body, fixed, specs, weights, not fresh, shapes, scratch, bufs, ((ROWS, model), BF), "block_forward")


def bwd_kernel(site, slots, own, last, tok_at, has, model, ff, info, *rest):
    tok = rest[0] if has[0] else None
    arr = rest[has[0]] if has[1] else None
    norms, X, QKV, PP, H, GP, w1, w2, w3, w4, *rest = rest[sum(has):]
    (E, DU, F, DQ, LNG, DXO, wqkv, wo, wup, wdn, dxo,
     es, xs, qs, ps, hs, gs, dus, dhs, fs, dos, dqs, dxs, dxb, lng, sem) = rest
    seqs = ROWS // 64
    place = last - info[SECTION]
    slot = site - LAG * place

    @pl.when((slot >= 0) & (slot < slots))
    def _():
        come = fetch(place, tok, tok_at, arr, es, sem.at[0])
        slope = pltpu.make_async_copy(GP.at[slot], gs, sem.at[5])
        slope.start()
        copies = []

        def out(src, dst, k):
            cp = pltpu.make_async_copy(src, dst, sem.at[k])
            cp.start()
            copies.append(cp)

        parts = ff // model
        loads = []
        for k, (src, dst) in enumerate(((H, hs), (PP, ps), (QKV, qs), (X, xs))):
            loads.append(pltpu.make_async_copy(src.at[slot], dst, sem.at[1 + k]))
        for cp in loads:
            cp.start()
        come.wait()
        slope.wait()
        out(es, E.at[slot], 6)
        dc_all = None
        for j in range(parts):
            sl = pl.ds(j * model, model)
            du = (mm_nt(es[...], wdn[sl, :]) * gs[:, sl].astype(F32)).astype(BF)
            dus[:, sl] = du
        dc_all = mm_nt(dus[...], wup[...])
        out(dus, DU.at[slot], 7)
        for cp in loads:
            cp.wait()
        sums = [jnp.zeros((8, model), F32) for _ in range(4)]

        def fold(v):
            return jnp.sum(v.reshape(8, 8, model), axis=0)

        gain = norms[2:3, :]
        for i in range(seqs):
            sl = pl.ds(i * 64, 64)
            n, r = norm_of(hs[sl, :])
            dc = dc_all[i * 64:(i + 1) * 64]
            sums[2] += fold(dc * n)
            sums[3] += fold(dc)
            dh = es[sl, :].astype(F32) + norm_back(n, r, dc * gain)
            dhs[sl, :] = dh
            fs[sl, :] = dh.astype(BF)
        lng[2] = sums[2]
        lng[3] = sums[3]
        out(fs, F.at[slot], 8)
        dos[...] = mm_nt(fs[...], wo[...]).astype(BF)
        low = low_lanes()

        for it in range(ROWS // 128 * (HEADS // 2)):
            p, hp = divmod(it, HEADS // 2)
            rs = pl.ds(p * 128, 128)

            def lanes(block):
                return pl.ds(block * model + hp * PAIR, PAIR)

            q2 = qs[rs, lanes(0)]
            do2 = dos[rs, lanes(0)]
            pc = ps[it]
            t = pc.astype(F32) * mm_nt(split_heads(qs[rs, lanes(2)], low), do2)
            halves = []
            for h in range(2):
                hl = slice(h * 128, (h + 1) * 128)
                halves.append((t[hl] - pc[hl].astype(F32) * jnp.sum(t[hl], 0, keepdims=True)).astype(BF))
            ds = jnp.concatenate(halves, axis=0)
            scale = HEAD**-0.5
            dq = mm_tn(ds, split_heads(qs[rs, lanes(1)], low)) * scale
            dk = mm(ds, q2) * scale
            dv = mm(pc, do2)
            dqs[rs, lanes(0)] = dq.astype(BF)
            dqs[rs, lanes(1)] = jnp.where(low, dk[:128], dk[128:]).astype(BF)
            dqs[rs, lanes(2)] = jnp.where(low, dv[:128], dv[128:]).astype(BF)

        out(dqs, DQ.at[slot], 9)
        da_all = mm_nt(dqs[...], wqkv[...])
        gain = norms[0:1, :]
        for i in range(seqs):
            sl = pl.ds(i * 64, 64)
            n, r = norm_of(xs[sl, :].astype(F32))
            da = da_all[i * 64:(i + 1) * 64]
            sums[0] += fold(da * n)
            sums[1] += fold(da)
            dx = dhs[sl, :] + norm_back(n, r, da * gain)
            dxs[sl, :] = dx
            dxb[sl, :] = dx.astype(BF)
        out(dxb, dxo, 10)
        lng[0] = sums[0]
        lng[1] = sums[1]
        out(lng, LNG.at[slot], 11)

        for cp in copies:
            cp.wait()

        @pl.when(slot < own)
        def _():
            cp = pltpu.make_async_copy(dxs, DXO.at[slot], sem.at[12])
            cp.start()
            cp.wait()


def bwd_call(site, own, last, info, tok, tok_at, arr, norms, weights, saved, bufs, slots):
    model, ff = weights[2].shape[-2:]
    pairs = ROWS // 128 * (HEADS // 2)
    X, A, QKV, PP, O, H, C, MM, GP = saved
    small = ((slots, ROWS, model), BF)
    shapes = [
        small,
        ((slots, ROWS, ff), BF),
        small,
        ((slots, ROWS, 3 * model), BF),
        ((slots, 4, 8, model), F32),
        ((own, ROWS, model), F32),
    ]
    scratch = [
        pltpu.VMEM((ROWS, model), BF),
        pltpu.VMEM((ROWS, model), BF),
        pltpu.VMEM((ROWS, 3 * model), BF),
        pltpu.VMEM((pairs, 256, 128), BF),
        pltpu.VMEM((ROWS, model), F32),
        pltpu.VMEM((ROWS, ff), BF),
        pltpu.VMEM((ROWS, ff), BF),
        pltpu.VMEM((ROWS, model), F32),
        pltpu.VMEM((ROWS, model), BF),
        pltpu.VMEM((ROWS, model), BF),
        pltpu.VMEM((ROWS, 3 * model), BF),
        pltpu.VMEM((ROWS, model), F32),
        pltpu.VMEM((ROWS, model), BF),
        pltpu.VMEM((4, 8, model), F32),
        pltpu.SemaphoreType.DMA((13,)),
    ]
    has, sources = site_inputs(tok, arr)
    fixed = [info, *sources, norms, *[hbm(v) for v in (X, QKV, PP, H, GP)]]
    specs = [SMEM, *[LOOSE for _ in sources], VMEM] + [ANY] * 5
    body = functools.partial(bwd_kernel, site, slots, own, last, tok_at, has, model, ff)
    return sub_call(body, fixed, specs, weights, True, shapes, scratch, bufs, ((ROWS, model), BF), "block_backward")


def head_kernel(own, flip, last, info, fg, fb, proj, hid, first, *rest):
    more, (loss, gproj, ggain, gbias, hdy, dpool, ysc, dsc, sem) = rest[:-9], rest[-9:]
    model = proj.shape[0]
    scale = 1.5 * model**0.5
    gain, bias = fg[...].reshape(1, model), fb[...].reshape(1, model)
    about = first[...]
    if more:
        about = jnp.where(info[SECTION] == len(more), about, sum(v[...] for v in more))
    nbar = about[:, 0:model]
    image = about[:, model:2 * model]
    pidx = about[:, 2 * model:2 * model + 1].astype(jnp.int32)
    pooled = (nbar * gain + bias).astype(BF)
    text = mm(pooled, proj[...])
    inv = lax.rsqrt(jnp.sum(text * text, -1, keepdims=True) + EPS)
    unit = text * inv
    iunit = (image * lax.rsqrt(jnp.sum(image * image, -1, keepdims=True) + EPS)).astype(BF)
    logits = scale * mm_nt(unit.astype(BF), iunit)
    rmax = jnp.max(logits, 1, keepdims=True)
    rlse = rmax + jnp.log(jnp.sum(jnp.exp(logits - rmax), 1, keepdims=True))
    cmax = jnp.max(logits, 0, keepdims=True)
    clse = cmax + jnp.log(jnp.sum(jnp.exp(logits - cmax), 0, keepdims=True))
    n = logits.shape[0]
    hot = lax.broadcasted_iota(jnp.int32, (n, n), 1) == pidx
    g = 0.5 * jnp.exp(logits - rlse) + 0.5 * jnp.exp(logits - clse) - jnp.where(hot, 1.0, 0.0)
    dt = scale * mm(g.astype(BF), iunit)
    dtext = ((dt - unit * jnp.sum(dt * unit, -1, keepdims=True)) * inv).astype(BF)
    dp = mm_nt(dtext, proj[...])
    if last is None:
        at = jnp.sum(jnp.where(hot, logits, 0.0), 1, keepdims=True)
        col = jnp.sum(jnp.where(hot, jnp.broadcast_to(clse, (n, n)), 0.0), 1, keepdims=True)
        loss[...] = jnp.broadcast_to(0.5 * (rlse - at) + 0.5 * (col - at), (n, 128)).T[0:1, :].reshape(n)
        gproj[...] = mm_tn(pooled, dtext)
        ggain[...] = jnp.sum(dp * nbar, 0, keepdims=True).reshape(model)
        gbias[...] = jnp.sum(dp, 0, keepdims=True).reshape(model)

    @pl.when(info[SECTION] == (-1 if last is None else last))
    def _():
        dpool[...] = dp
        per = ROWS // 64
        blocks = hid.shape[0]
        loads, stores = [], []
        for m in range(blocks):
            cp = pltpu.make_async_copy(hid.at[m], ysc.at[m], sem.at[m])
            cp.start()
            loads.append(cp)
        for m in range(blocks):
            loads[m].wait()
            of = info[GROUP] if m < own else info[GROUP] ^ flip
            for i in range(per):
                count = info[LENS + m * per + i]
                nn, r = norm_of(ysc[m, pl.ds(i * 64, 64), :].astype(F32))
                w = dpool[pl.ds(of * own * per + (m % own) * per + i, 1), :] * (gain / count.astype(F32))
                ok = lax.broadcasted_iota(jnp.int32, (64, 1), 0) < count
                dsc[pl.ds(m * ROWS + i * 64, 64), :] = jnp.where(ok, norm_back(nn, r, w), 0.0).astype(BF)
            part = pl.ds(m * ROWS, ROWS)
            cp = pltpu.make_async_copy(dsc.at[part], hdy.at[part], sem.at[blocks + m])
            cp.start()
            stores.append(cp)
        for cp in stores:
            cp.wait()


def head_call(own, flip, last, info, fg, fb, proj, hid, *about):
    blocks, _, model = hid.shape
    pairs = about[0].shape[0]
    return pl.pallas_call(
        functools.partial(head_kernel, own, flip, last),
        out_shape=[
            jax.ShapeDtypeStruct((pairs,), F32),
            jax.ShapeDtypeStruct((model, model), F32),
            jax.ShapeDtypeStruct((model,), F32),
            jax.ShapeDtypeStruct((model,), F32),
            pltpu.HBM((blocks * ROWS, model), BF),
        ],
        in_specs=[SMEM] + [VMEM] * 3 + [ANY] + [VMEM] * len(about),
        out_specs=[VMEM, VMEM, VMEM, VMEM, ANY],
        scratch_shapes=[
            pltpu.VMEM((pairs, model), F32),
            pltpu.VMEM((blocks, ROWS, model), BF),
            pltpu.VMEM((blocks * ROWS, model), BF),
            pltpu.SemaphoreType.DMA((2 * blocks,)),
        ],
        compiler_params=pltpu.CompilerParams(vmem_limit_bytes=VLIM),
        cost_estimate=FREE,
        name="head",
    )(info, fg, fb, proj, hbm(hid), *about)


def bit_of(w, bit):
    return (w[GROUP] >> bit) & 1


def wgrad_kernel(bit, waits, normed, where, a, e, *rest):
    norms = rest[0] if normed else None
    rest = rest[waits + normed:]

    left = a[...].reshape(a.shape[0] * ROWS, a.shape[2])
    right = e[...].reshape(e.shape[0] * ROWS, e.shape[2])
    g = mm_tn(left, right)
    if normed:
        sums = jnp.sum(jnp.sum(norms[...], 0), 1)
        sums = jnp.concatenate([sums, jnp.zeros((128 - sums.shape[0], sums.shape[1]), F32)], 0)
        g = jnp.concatenate([g, sums.T], 1)
    if bit is None:
        rest[0][...] = g.astype(BF)
        return
    send, keep = rest[:2]
    quarter = send.shape[1]
    if quarter == g.shape[0]:
        step = pl.program_id(0)

        @pl.when(step < 2)
        def _():
            send[0] = g.astype(BF)

        @pl.when(step >= 2)
        def _():
            keep[0] = g.astype(BF)
    else:
        high = bit_of(where, bit) == 1
        parts = [g[k * quarter:(k + 1) * quarter] for k in range(4)]
        for k in range(2):
            one, two = (parts[2 * k], parts[2 * k + 1]) if bit == 0 else (parts[k], parts[2 + k])
            send[k] = jnp.where(high, one, two).astype(BF)
            keep[k] = jnp.where(high, two, one).astype(BF)


def wgrad(info, left, right, after, bit, half_bit, norms=None):
    slots, _, wide = left.shape
    cols = right.shape[2]
    mine = wide // 2
    step = math.gcd(mine, 384)
    width = 768
    left_blocks = mine // step
    single = left_blocks == 4 and bit is not None
    normed = norms is not None
    more = 128 if normed else 0

    def left_at(i, j, w):
        if single:
            own_bit = bit_of(w, bit)
            other = jnp.where(i < 2, 1 - own_bit, own_bit)
            k = (i % 2) * 2 + other if bit == 0 else other * 2 + i % 2
        else:
            k = i
        return (0, 0, bit_of(w, half_bit) * left_blocks + k)

    if bit is None:
        out_shape = pltpu.HBM((mine, cols + more), BF)
        out_specs = pl.BlockSpec((step, width + more), lambda i, j, w: (i, j))
    else:
        out_shape = [pltpu.HBM((2, mine // 4, cols + more), BF)] * 2
        if single:
            out_specs = [
                pl.BlockSpec((1, step, width), lambda i, j, w: (jnp.minimum(i, 1), 0, j)),
                pl.BlockSpec((1, step, width), lambda i, j, w: (jnp.maximum(i - 2, 0), 0, j)),
            ]
        else:
            out_specs = [pl.BlockSpec((2, mine // 4, width + more), lambda i, j, w: (0, 0, j))] * 2
    return pl.pallas_call(
        functools.partial(wgrad_kernel, bit, len(after), normed),
        grid_spec=pltpu.PrefetchScalarGridSpec(
            num_scalar_prefetch=1,
            grid=(left_blocks, cols // width),
            in_specs=[
                pl.BlockSpec((slots, ROWS, step), left_at),
                pl.BlockSpec((slots, ROWS, width), lambda i, j, w: (0, 0, j)),
                *([pl.BlockSpec((slots, 4, 8, step), lambda i, j, w: (0, 0, 0, bit_of(w, half_bit)))] if normed else []),
                *[ANY for _ in after],
            ],
            out_specs=out_specs,
        ),
        out_shape=out_shape,
        compiler_params=pltpu.CompilerParams(vmem_limit_bytes=VLIM),
        cost_estimate=FREE,
        name="weight_grad",
    )(info, hbm(left), hbm(right), *([norms] if normed else []), *map(hbm, after))


def halves(g, info, bit):
    quarter = g.shape[0] // 4
    parts = [g[k * quarter:(k + 1) * quarter] for k in range(4)]
    high = bit_of(info, bit) == 1
    send, keep = [], []
    for k in range(2):
        one, two = (parts[2 * k], parts[2 * k + 1]) if bit == 0 else (parts[k], parts[2 + k])
        send.append(jnp.where(high, one, two).astype(BF))
        keep.append(jnp.where(high, two, one).astype(BF))
    return send, keep


def attention_kernel(info, a, o, dq, f, norms, after, send_one, keep_one, send_two, keep_two):
    j = pl.program_id(0)
    thirds = pl.num_programs(0) - 1

    def product(left, right):
        return mm_tn(left[...].reshape(-1, left.shape[2]), right[...].reshape(-1, right.shape[2]))

    def put(g, outs, bit, at, width):
        for value, out in zip(halves(g, info, bit), outs):
            for k in range(2):
                out[k, :, pl.ds(at, width)] = value[k]

    one, two = (send_one, keep_one), (send_two, keep_two)
    width = dq.shape[2]
    for k in range(3):
        @pl.when(j == k)
        def _():
            put(product(a, dq), one if k < 2 else two, 0 if k < 2 else 1, k * width if k < 2 else 0, width)

    @pl.when(j == thirds)
    def _():
        put(product(o, f), two, 1, width, width)
        sums = jnp.sum(jnp.sum(norms[...], 0), 1)
        sums = jnp.concatenate([sums, jnp.zeros((128 - sums.shape[0], sums.shape[1]), F32)], 0)
        put(sums.T, two, 1, 2 * width, 128)


def attention_wgrad(info, a, dq, o, f, norms, after, half_bit):
    slots, _, model = a.shape
    mine = model // 2
    left = pl.BlockSpec((slots, ROWS, mine), lambda j, w: (0, 0, bit_of(w, half_bit)))
    shapes = [(2, mine // 4, 2 * model)] * 2 + [(2, mine // 4, 2 * model + 128)] * 2
    return pl.pallas_call(
        attention_kernel,
        grid_spec=pltpu.PrefetchScalarGridSpec(
            num_scalar_prefetch=1,
            grid=(4,),
            in_specs=[
                left,
                left,
                pl.BlockSpec((slots, ROWS, model), lambda j, w: (0, 0, jnp.minimum(j, 2))),
                pl.BlockSpec((slots, ROWS, model), lambda j, w: (0, 0, 0)),
                pl.BlockSpec((slots, 4, 8, mine), lambda j, w: (0, 0, 0, bit_of(w, half_bit))),
                ANY,
            ],
            out_specs=[pl.BlockSpec(s, lambda j, w: (0, 0, 0)) for s in shapes],
        ),
        out_shape=[pltpu.HBM(s, BF) for s in shapes],
        compiler_params=pltpu.CompilerParams(vmem_limit_bytes=VLIM),
        cost_estimate=FREE,
        name="attention_weight_grad",
    )(info, hbm(a), hbm(o), hbm(dq), hbm(f), norms, hbm(after))


def attention_total_kernel(keep_one, came_one, keep_two, came_two, after, qkv, out, *norms):
    model = out.shape[1]
    qkv[:, 0:2 * model] = keep_one[...].astype(F32) + came_one[...].astype(F32)
    two = keep_two[...].astype(F32) + came_two[...].astype(F32)
    qkv[:, 2 * model:] = two[:, 0:model]
    out[...] = two[:, model:2 * model]
    rows = two.shape[0]
    sums = jnp.concatenate([two[:, 2 * model:], jnp.zeros((128 - rows, 128), F32)], 0).T
    for k, o in enumerate(norms):
        o[...] = sums[k:k + 1, 0:rows]


def attention_total(keep_one, came_one, keep_two, came_two, after):
    rows, cols = keep_one.shape
    model = cols // 2
    return pl.pallas_call(
        attention_total_kernel,
        in_specs=[VMEM] * 4 + [ANY],
        out_specs=[VMEM] * 6,
        out_shape=[jax.ShapeDtypeStruct(s, F32) for s in [(rows, 3 * model), (rows, model)] + [(1, rows)] * 4],
        cost_estimate=FREE,
        name="attention_total",
    )(keep_one, came_one, keep_two, came_two, hbm(after))


def fold_kernel(bit, info, keep, came, after, send, left):
    high = bit_of(info, bit) == 1
    one = keep[0].astype(F32) + came[0].astype(F32)
    two = keep[1].astype(F32) + came[1].astype(F32)
    send[...] = jnp.where(high, one, two).astype(BF)
    left[...] = jnp.where(high, two, one).astype(BF)


def fold(info, keep, came, after, bit):
    _, rows, cols = keep.shape
    width = 768 if cols % 768 == 0 else cols
    block = pl.BlockSpec((2, rows, width), lambda j, w: (0, 0, j))
    half = pl.BlockSpec((rows, width), lambda j, w: (0, j))
    return pl.pallas_call(
        functools.partial(fold_kernel, bit),
        grid_spec=pltpu.PrefetchScalarGridSpec(
            num_scalar_prefetch=1, grid=(cols // width,), in_specs=[block, block, ANY], out_specs=[half, half]
        ),
        out_shape=[pltpu.HBM((rows, cols), BF)] * 2,
        compiler_params=pltpu.CompilerParams(vmem_limit_bytes=VLIM),
        cost_estimate=FREE,
        name="fold",
    )(info, keep, came, hbm(after))


def total_kernel(keep, came, *rest):
    o = rest[-1]
    o[...] = keep[...].astype(F32) + came[...].astype(F32)


def total(keep, came, *after):
    rows, cols = keep.shape
    width = 768 if cols % 768 == 0 else cols
    block = pl.BlockSpec((rows, width), lambda j: (0, j))
    return pl.pallas_call(
        total_kernel,
        grid=(cols // width,),
        in_specs=[block, block] + [ANY] * len(after),
        out_specs=block,
        out_shape=pltpu.HBM((rows, cols), F32),
        compiler_params=pltpu.CompilerParams(vmem_limit_bytes=VLIM),
        cost_estimate=FREE,
        name="total",
    )(keep, came, *map(hbm, after))


def swap_bit(value, axis, bit):
    peers = lax.axis_size(axis)
    return lax.ppermute(value, axis, [(i, i ^ (1 << bit)) for i in range(peers)])


def pack_kernel(pairs, nb, img, o):
    model = img.shape[1]
    n, per = nb.shape[:2]
    for i in range(n):
        o[pl.ds(i * per, per), 0:model] = nb[i]
    o[:, model:2 * model] = img[...].astype(F32)
    for i in range(n * per):
        o[pl.ds(i, 1), 2 * model:] = jnp.full((1, 128), pairs[i], jnp.int32).astype(F32)


def join_kernel(bit, info, value, *rest):
    o, pieces = rest[-1], (value, *rest[:-2])
    n = value.shape[0]
    me = (info[GROUP] >> bit) & (len(pieces) - 1)
    for k, piece in enumerate(pieces):
        o[pl.ds(pl.multiple_of((me ^ k) * n, 8), n), :] = piece[...]


def copy_kernel(value, *rest):
    rest[-1][...] = value[...]


def numbers_kernel(info, after, o):
    for k in range(o.shape[0]):
        o[k] = info[k]


def numbers(info, after):
    return pl.pallas_call(
        numbers_kernel,
        out_shape=jax.ShapeDtypeStruct(info.shape, jnp.int32),
        in_specs=[SMEM, LOOSE],
        out_specs=SMEM,
        cost_estimate=FREE,
        name="numbers",
    )(info, after)


def small_call(body, specs, shape, name, *args):
    return pl.pallas_call(
        body,
        out_shape=jax.ShapeDtypeStruct(shape, F32),
        in_specs=specs,
        out_specs=VMEM,
        compiler_params=pltpu.CompilerParams(vmem_limit_bytes=8 << 20),
        cost_estimate=FREE,
        name=name,
    )(*args)


def joined(info, bit, value, others, after):
    shape = ((1 + len(others)) * value.shape[0], value.shape[1])
    body = functools.partial(join_kernel, bit)
    return small_call(body, [SMEM] + [VMEM] * (1 + len(others)) + [LOOSE], shape, "join", info, value, *others, after)


def split(value, at, mine):
    keep = lax.dynamic_index_in_dim(value, mine, at, keepdims=False)
    return lax.dynamic_index_in_dim(value, 1 - mine, at, keepdims=False), keep


def scattered(pair, axis, me, bits, total_bits):
    left = list(range(total_bits - 1, -1, -1))
    for place, bit in enumerate(bits):
        if place > 0:
            send, keep = split(value, left.index(bit), (me >> bit) & 1)
            came = swap_bit(send, axis, bit)
        else:
            came, keep = pair
        value = keep.astype(F32) + came.astype(F32)
        if place < len(bits) - 1:
            value = value.astype(BF)
        left.remove(bit)
    return value


def on_device(tokens, lengths, pair_index, images, ln1_gain, ln1_bias, qkv_weight, out_weight,
              ln2_gain, ln2_bias, up_weight, down_weight, final_gain, final_bias, proj_weight):
    groups = lax.axis_size("dp")
    sections = lax.axis_size("section")
    section = lax.axis_index("section")
    group = lax.axis_index("dp")
    model = tokens.shape[1]
    n_seq = lengths.shape[0]
    flip = groups - 2
    own = tokens.shape[0] // ROWS
    slots = 2 * own

    last = sections - 1
    norms = jnp.concatenate([ln1_gain, ln1_bias, ln2_gain, ln2_bias], 0)
    weights = (qkv_weight, out_weight, up_weight, down_weight)
    who = jnp.stack([section, group]).astype(jnp.int32)
    info_own = jnp.concatenate([who, lengths, lengths])
    theirs = lax.ppermute(
        tokens, ("dp", "section"), [(d * sections, (d ^ flip) * sections) for d in range(groups)]
    )
    theirs_lengths = lax.ppermute(lengths, "dp", [(d, d ^ flip) for d in range(groups)])
    info = jnp.concatenate([who, lengths, theirs_lengths])
    bufs = about = coming = None
    sites = slots + LAG * last

    def pairs_at(t, turn):
        return [turn(s) for s in range(last) if 0 <= t - LAG * s < slots]

    hop = {}
    for t in range(sites):
        tok, at = (None, 0) if t >= slots else (tokens, t * ROWS) if t < own else (theirs, (t - own) * ROWS)
        bufs, weights, y = fwd_call(
            t, own, last, info_own if t < own else info, tok, at, hop.get(t - LAG), norms, weights, bufs, slots
        )
        pairs = pairs_at(t, lambda s: (s, s + 1))
        if pairs:
            hop[t] = lax.ppermute(y, "section", pairs)
        m = t - LAG * last
        if m == own - 1:
            about = small_call(pack_kernel, [SMEM, VMEM, VMEM], (n_seq, 2 * model + 128), "pack", pair_index, bufs[10], images)
            coming = [swap_bit(about, "dp", 0)]
        elif m == own:
            about = joined(info, 0, about, coming, y)
            coming = [
                lax.ppermute(about, "dp", [(d, d ^ (2 * k)) for d in range(groups)]) for k in range(1, groups // 2)
            ]
    saved, hid = bufs[:9], bufs[9]
    about = joined(info, 1, about, coming, y)
    hdy = head_call(own, flip, last, info, final_gain, final_bias, proj_weight, hid, about)[4]

    back = None
    step = {}
    for t in range(sites):
        tok, at = (None, 0) if t >= slots else (hdy, t * ROWS)
        back, weights, dx = bwd_call(t, own, last, info, tok, at, step.get(t - LAG), norms, weights, saved, back, slots)
        pairs = pairs_at(t, lambda s: (last - s, last - s - 1))
        if pairs:
            step[t] = lax.ppermute(dx, "section", pairs)
    E, DU, F, DQ, LNG, DXO = back
    X, A, QKV, PP, O, H, C, MM, GP = saved

    bits = (groups // 2).bit_length() - 1
    low_first = list(range(bits))
    high_first = low_first[::-1]
    def head_again(after):
        late = small_call(copy_kernel, [VMEM, ANY], about.shape, "copy", about, hbm(after))
        shared = [lax.ppermute(late, "section", [(last, t)]) for t in range(last)]
        return head_call(own, flip, None, info, final_gain, final_bias, proj_weight, hid, late, *shared)

    if bits == 2:
        pieces = [wgrad(info, MM, E, [dx], 0, bits)]
        pieces.append(wgrad(info, C, DU, [pieces[0][0]], 1, bits))
        one, kept_one, two, kept_two = attention_wgrad(info, A, DQ, O, F, LNG, pieces[1][0], bits)
        pieces += [(one, kept_one), (two, kept_two)]
        orders = (low_first, high_first, low_first, high_first)
        sent = [swap_bit(send, "dp", order[0]) for (send, _), order in zip(pieces, orders)]
        tail = head_again(two)
        after = tail[1]
        held = []
        for came, (_, keep), order in zip(sent, pieces, orders):
            after, keep = fold(info, keep, came, after, order[1])
            held += [keep, swap_bit(after, "dp", order[1])]
        g_down = total(held[0], held[1], after)
        g_up = total(held[2], held[3], g_down)
        g_qkv, g_out, *g_norm = attention_total(*held[4:], g_up)
    else:
        me = numbers(info, dx)[GROUP]
        grads = []
        after = [dx]
        for a, e, norm, order in (
            (MM, E, None, low_first), (C, DU, None, high_first), (A, DQ, None, low_first), (O, F, LNG, high_first)
        ):
            after = [wgrad(info, a, e, after, None, bits, norm)]
            rows, cols = after[0].shape
            cut = after[0].reshape((2,) * bits + (rows >> bits, cols))
            send, keep = split(cut, bits - 1 - order[0], (me >> order[0]) & 1)
            grads.append(scattered((swap_bit(send, "dp", order[0]), keep), "dp", me, order, bits))
        g_down, g_up, g_qkv, g_out = grads
        g_out, g_norm = g_out[:, :model], [g_out[:, model + k][None] for k in range(4)]
        tail = head_again(after[0])
    return (
        bufs[11].reshape(1, own * ROWS, model),
        DXO.reshape(1, own * ROWS, model),
        g_norm[0],
        g_norm[1],
        g_qkv[None],
        g_out[None],
        g_norm[2],
        g_norm[3],
        g_up[None],
        g_down[None],
        tail[2],
        tail[3],
        tail[1],
        tail[0],
    )


def solution(mesh):
    row = P("section", None)
    cube = P("section", None, None)
    in_specs = (P("dp", None), P("dp"), P("dp"), P("dp", None), row, row, cube, cube, row, row, cube, cube, P(), P(), P())
    big = P("section", "dp", None)
    small = P("section", "dp")
    out_specs = (big, big, small, small, big, big, small, small, big, big, P(), P(), P(), P())
    return jax.shard_map(on_device, mesh=mesh, in_specs=in_specs, out_specs=out_specs, check_vma=False)
```

```python
import functools
import math

import jax
import jax.numpy as jnp
from jax import lax
from jax.experimental import pallas as pl
from jax.experimental.pallas import tpu as pltpu
from jax.sharding import PartitionSpec as P

HEADS = 12
HEAD = 64
PAIR = 2 * HEAD
ROWS = 256
EPS = 1e-06
MASKED = -1000000000.0
BF = jnp.bfloat16
F32 = jnp.float32
ANY = pl.BlockSpec(memory_space=pltpu.HBM)
LOOSE = pl.BlockSpec(memory_space=pl.ANY)
SMEM = pl.BlockSpec(memory_space=pltpu.SMEM)
VMEM = pl.BlockSpec(memory_space=pltpu.VMEM)
VLIM = 24 << 20
LAG = 2
FREE = pl.CostEstimate(flops=1, bytes_accessed=1, transcendentals=0)
SECTION, GROUP, LENS = range(3)


def hbm(v):
    return pltpu.with_memory_space_constraint(v, pltpu.HBM)


def vmem(v):
    return pltpu.with_memory_space_constraint(v, pltpu.VMEM)


def mm(a, b):
    return jnp.dot(a, b, preferred_element_type=F32)


def mm_nt(a, b):
    return lax.dot_general(a, b, (((1,), (1,)), ((), ())), preferred_element_type=F32)


def mm_tn(a, b):
    return lax.dot_general(a, b, (((0,), (0,)), ((), ())), preferred_element_type=F32)


def norm_of(v):
    c = v - jnp.mean(v, -1, keepdims=True)
    r = lax.rsqrt(jnp.mean(c * c, -1, keepdims=True) + EPS)
    return c * r, r


def norm_back(n, r, w):
    return r * (w - jnp.mean(w, -1, keepdims=True) - n * jnp.mean(w * n, -1, keepdims=True))


def gelu_pair(u):
    k = 0.7978845608028654
    u2 = u * u
    t = jnp.tanh(u * (k + (k * 0.044715) * u2))
    p = 0.5 + 0.5 * t
    g = p + (0.5 * u) * ((1.0 - t * t) * (k + (3.0 * k * 0.044715) * u2))
    return u * p, g


def split_heads(v, low):
    z = jnp.zeros_like(v)
    return jnp.concatenate([jnp.where(low, v, z), jnp.where(low, z, v)], axis=0)


def low_lanes():
    return lax.broadcasted_iota(jnp.int32, (PAIR, PAIR), 1) < HEAD


def chunk(j, width):
    return pl.ds(pl.multiple_of(j * width, 128), width)


class Weights:
    def __init__(self, sources, held, sem, model):
        self.sem, self.jobs, self.due = sem, {}, sources is not None
        if not self.due:
            return
        k = 0
        for name, src, dst in zip(("qkv", "out", "up", "down"), sources, held):
            rows, cols = dst.shape
            for j in range(max(rows, cols) // model):
                piece = pl.ds(j * model, model)
                at = (slice(None), piece) if cols > model else (piece, slice(None))
                self.jobs[name, j] = (src, dst, at, k)
                k += 1

    def copy(self, name, j, offset=0):
        src, dst, at, k = self.jobs[name, j]
        return pltpu.make_async_copy(src.at[(0,) + at], dst.at[at], self.sem.at[k + offset])

    def start(self, name, *pieces):
        for j in pieces or [j for n, j in self.jobs if n == name]:
            self.copy(name, j).start()

    def wait(self, name, j=0):
        if self.due:
            self.copy(name, 0, j).wait()


def fetch(place, tok, tok_at, arr, dst, sem):
    def copy():
        return pltpu.make_async_copy(tok.at[pl.ds(tok_at, ROWS)], dst, sem)

    def from_arr():
        dst[...] = arr[...]

    if tok is None:
        return from_arr
    if arr is None:
        copy().start()
        return lambda: copy().wait()
    pl.when(place == 0)(lambda: copy().start())

    def finish():
        pl.when(place == 0)(lambda: copy().wait())
        pl.when(place != 0)(from_arr)

    return finish


def fwd_kernel(fresh, site, slots, own, last, tok_at, has, model, ff, info, *rest):
    tok = rest[0] if has[0] else None
    arr = rest[has[0]] if has[1] else None
    norms, w1, w2, w3, w4, *rest = rest[sum(has):]
    (X, A, QKV, PP, O, H, C, MM, GP, HID, NB, Y, wqkv, wo, wup, wdn, yout,
     xs, as_, qs, ps, os_, hs, cs, ms, gs, ys, nb, sem, wsem) = rest
    weights = Weights((w1, w2, w3, w4) if fresh else None, (wqkv, wo, wup, wdn), wsem, model)
    names = ("qkv", "out", "up", "down")
    seqs = ROWS // 64
    section = info[SECTION]
    slot = site - LAG * section
    active = (slot >= 0) & (slot < slots)

    def length(i):
        return info[LENS + slot * seqs + i]

    if fresh:
        @pl.when(jnp.logical_not(active))
        def _():
            for name in names:
                weights.start(name)
            for name, j in weights.jobs:
                weights.wait(name, j)

    @pl.when(active)
    def _():
        come = fetch(section, tok, tok_at, arr, xs, sem.at[0])
        weights.start("qkv")
        come()
        copies = []

        def out(src, dst, k):
            cp = pltpu.make_async_copy(src, dst, sem.at[k])
            cp.start()
            copies.append(cp)

        out(xs, X.at[slot], 18)
        gain, bias = norms[0:1, :], norms[1:2, :]
        for i in range(seqs):
            sl = pl.ds(i * 64, 64)
            n, _r = norm_of(xs[sl, :].astype(F32))
            as_[sl, :] = (n * gain + bias).astype(BF)
        out(as_, A.at[slot], 2)

        for j in range(3):
            sl = pl.ds(j * model, model)
            weights.wait("qkv", j)
            qs[:, sl] = mm(as_[...], wqkv[:, sl]).astype(BF)

        weights.start("out")
        weights.start("up")

        out(qs, QKV.at[slot], 3)
        low = low_lanes()
        row = lax.broadcasted_iota(jnp.int32, (PAIR, PAIR), 0)
        col = lax.broadcasted_iota(jnp.int32, (PAIR, PAIR), 1)

        for it in range(ROWS // 128 * (HEADS // 2)):
            p, hp = divmod(it, HEADS // 2)
            if hp == 0:
                ok = ((col < 64) & (row < length(2 * p))) | ((col >= 64) & (row >= 64) & (row < 64 + length(2 * p + 1)))
            rs = pl.ds(p * 128, 128)

            def lanes(block):
                return pl.ds(block * model + hp * PAIR, PAIR)

            q2 = qs[rs, lanes(0)] * jnp.asarray(HEAD**-0.5, BF)
            s = mm_nt(split_heads(qs[rs, lanes(1)], low), q2)
            halves = []
            for h in range(2):
                sh = jnp.where(ok, s[h * 128:(h + 1) * 128], MASKED)
                e = jnp.exp(sh - jnp.max(sh, 0, keepdims=True))
                halves.append((e * (1.0 / jnp.sum(e, 0, keepdims=True))).astype(BF))
            pc = jnp.concatenate(halves, axis=0)
            ps[it] = pc
            os_[rs, lanes(0)] = mm_tn(pc, split_heads(qs[rs, lanes(2)], low)).astype(BF)

        out(ps, PP.at[slot], 4)
        out(os_, O.at[slot], 5)
        weights.start("down")
        weights.wait("out")
        hs[...] = xs[...].astype(F32) + mm(os_[...], wo[...])
        out(hs, H.at[slot], 6)
        gain2, bias2 = norms[2:3, :], norms[3:4, :]
        for i in range(seqs):
            sl = pl.ds(i * 64, 64)
            n, _r = norm_of(hs[sl, :])
            cs[sl, :] = (n * gain2 + bias2).astype(BF)
        out(cs, C.at[slot], 7)
        parts = ff // model
        total = hs[...]
        for j in range(parts):
            sl = pl.ds(j * model, model)
            weights.wait("up", j)
            m, g = gelu_pair(mm(cs[...], wup[:, sl]))
            ms[:, sl] = m.astype(BF)
            gs[:, sl] = g.astype(BF)
            out(ms.at[:, sl], MM.at[slot, :, sl], 10 + 2 * j)
            out(gs.at[:, sl], GP.at[slot, :, sl], 11 + 2 * j)
            weights.wait("down", j)
            total = total + mm(ms[:, sl], wdn[sl, :])
        ys[...] = total.astype(BF)
        yout[...] = ys[...]
        mine = pltpu.make_async_copy(ys, Y.at[slot], sem.at[1])
        pl.when(slot < own)(lambda: mine.start())
        if site >= LAG * last:
            top = pltpu.make_async_copy(ys, HID.at[slot], sem.at[9])
            means = pltpu.make_async_copy(nb, NB.at[slot], sem.at[0])
            first = site - LAG * last < own

            @pl.when(section == last)
            def _():
                top.start()
                if first:
                    for i in range(seqs):
                        n, _r = norm_of(ys[pl.ds(i * 64, 64), :].astype(F32))
                        count = length(i)
                        ok = lax.broadcasted_iota(jnp.int32, (64, 1), 0) < count
                        nb[pl.ds(i, 1), :] = jnp.sum(jnp.where(ok, n, 0.0), 0, keepdims=True) / count.astype(F32)
                    means.start()

        for cp in copies:
            cp.wait()
        pl.when(slot < own)(lambda: mine.wait())
        if site >= LAG * last:
            @pl.when(section == last)
            def _():
                top.wait()
                if first:
                    means.wait()


def sub_call(body, fixed, specs, weights, held, shapes, scratch, bufs, last_shape, name):
    n, many = len(fixed) + 4, len(shapes)
    alias = {}
    extra = []
    kernel = body
    if held:
        alias = {len(fixed) + i: many + i for i in range(4)}
        weights = [vmem(w) for w in weights]
    else:
        weights = [hbm(w) for w in weights]
    if bufs is not None:
        alias |= {n + i: i for i in range(many)}
        extra = [hbm(v) for v in bufs]

        def kernel(*refs):
            body(*refs[:n], *refs[n + many:])

    res = pl.pallas_call(
        kernel,
        out_shape=[pltpu.HBM(s, d) for s, d in shapes]
        + [pltpu.VMEM(w.shape[-2:], BF) for w in weights]
        + [jax.ShapeDtypeStruct(*last_shape)],
        in_specs=specs + [VMEM if held else ANY] * 4 + [ANY] * len(extra),
        out_specs=[ANY] * many + [VMEM] * 5,
        input_output_aliases=alias,
        scratch_shapes=scratch,
        compiler_params=pltpu.CompilerParams(vmem_limit_bytes=VLIM),
        cost_estimate=FREE,
        name=name,
    )(*fixed, *weights, *extra)
    return res[:many], res[many:many + 4], res[-1]


def site_inputs(tok, arr):
    has = (tok is not None, arr is not None)
    sources = [tok] if has[0] else []
    specs = [LOOSE] * has[0] + [VMEM] * has[1]
    return has, sources + ([arr] if has[1] else []), specs


def fwd_call(site, own, last, info, tok, tok_at, arr, norms, weights, bufs, slots):
    model, ff = weights[2].shape[-2:]
    pairs = ROWS // 128 * (HEADS // 2)
    small = ((slots, ROWS, model), BF)
    wide = ((slots, ROWS, ff), BF)
    shapes = [
        small,
        small,
        ((slots, ROWS, 3 * model), BF),
        ((slots, pairs, 256, 128), BF),
        small,
        ((slots, ROWS, model), F32),
        small,
        wide,
        wide,
        small,
        ((own, ROWS // 64, model), F32),
        ((own, ROWS, model), BF),
    ]
    scratch = [
        pltpu.VMEM((ROWS, model), BF),
        pltpu.VMEM((ROWS, model), BF),
        pltpu.VMEM((ROWS, 3 * model), BF),
        pltpu.VMEM((pairs, 256, 128), BF),
        pltpu.VMEM((ROWS, model), BF),
        pltpu.VMEM((ROWS, model), F32),
        pltpu.VMEM((ROWS, model), BF),
        pltpu.VMEM((ROWS, ff), BF),
        pltpu.VMEM((ROWS, ff), BF),
        pltpu.VMEM((ROWS, model), BF),
        pltpu.VMEM((ROWS // 64, model), F32),
        pltpu.SemaphoreType.DMA((11 + 2 * (ff // model),)),
        pltpu.SemaphoreType.DMA((4 + 2 * (ff // model),)),
    ]
    fresh = bufs is None
    has, sources, kinds = site_inputs(tok, arr)
    fixed = [info, *sources, norms]
    specs = [SMEM, *kinds, VMEM]
    body = functools.partial(fwd_kernel, fresh, site, slots, own, last, tok_at, has, model, ff)
    return sub_call(body, fixed, specs, weights, not fresh, shapes, scratch, bufs, ((ROWS, model), BF), "block_forward")


def bwd_kernel(site, slots, own, last, tok_at, has, model, ff, info, *rest):
    tok = rest[0] if has[0] else None
    arr = rest[has[0]] if has[1] else None
    norms, X, QKV, PP, H, GP, w1, w2, w3, w4, *rest = rest[sum(has):]
    (E, DU, F, DQ, LNG, DXO, wqkv, wo, wup, wdn, dxo,
     es, xs, qs, ps, hs, gs, dus, dhs, fs, dos, dqs, dxs, dxb, lng, sem) = rest
    seqs = ROWS // 64
    place = last - info[SECTION]
    slot = site - LAG * place

    @pl.when((slot >= 0) & (slot < slots))
    def _():
        come = fetch(place, tok, tok_at, arr, es, sem.at[0])
        slope = pltpu.make_async_copy(GP.at[slot], gs, sem.at[5])
        slope.start()
        copies = []

        def out(src, dst, k):
            cp = pltpu.make_async_copy(src, dst, sem.at[k])
            cp.start()
            copies.append(cp)

        parts = ff // model
        loads = []
        for k, (src, dst) in enumerate(((H, hs), (PP, ps), (QKV, qs), (X, xs))):
            loads.append(pltpu.make_async_copy(src.at[slot], dst, sem.at[1 + k]))
        for cp in loads:
            cp.start()
        come()
        slope.wait()
        out(es, E.at[slot], 6)
        dc_all = None
        for j in range(parts):
            sl = pl.ds(j * model, model)
            du = (mm_nt(es[...], wdn[sl, :]) * gs[:, sl].astype(F32)).astype(BF)
            dus[:, sl] = du
        dc_all = mm_nt(dus[...], wup[...])
        out(dus, DU.at[slot], 7)
        for cp in loads:
            cp.wait()
        sums = [jnp.zeros((8, model), F32) for _ in range(4)]

        def fold(v):
            return jnp.sum(v.reshape(8, 8, model), axis=0)

        gain = norms[2:3, :]
        for i in range(seqs):
            sl = pl.ds(i * 64, 64)
            n, r = norm_of(hs[sl, :])
            dc = dc_all[i * 64:(i + 1) * 64]
            sums[2] += fold(dc * n)
            sums[3] += fold(dc)
            dh = es[sl, :].astype(F32) + norm_back(n, r, dc * gain)
            dhs[sl, :] = dh
            fs[sl, :] = dh.astype(BF)
        lng[2] = sums[2]
        lng[3] = sums[3]
        out(fs, F.at[slot], 8)
        dos[...] = mm_nt(fs[...], wo[...]).astype(BF)
        low = low_lanes()

        for it in range(ROWS // 128 * (HEADS // 2)):
            p, hp = divmod(it, HEADS // 2)
            rs = pl.ds(p * 128, 128)

            def lanes(block):
                return pl.ds(block * model + hp * PAIR, PAIR)

            q2 = qs[rs, lanes(0)]
            do2 = dos[rs, lanes(0)]
            pc = ps[it]
            t = pc.astype(F32) * mm_nt(split_heads(qs[rs, lanes(2)], low), do2)
            halves = []
            for h in range(2):
                hl = slice(h * 128, (h + 1) * 128)
                halves.append((t[hl] - pc[hl].astype(F32) * jnp.sum(t[hl], 0, keepdims=True)).astype(BF))
            ds = jnp.concatenate(halves, axis=0)
            scale = HEAD**-0.5
            dq = mm_tn(ds, split_heads(qs[rs, lanes(1)], low)) * scale
            dk = mm(ds, q2) * scale
            dv = mm(pc, do2)
            dqs[rs, lanes(0)] = dq.astype(BF)
            dqs[rs, lanes(1)] = jnp.where(low, dk[:128], dk[128:]).astype(BF)
            dqs[rs, lanes(2)] = jnp.where(low, dv[:128], dv[128:]).astype(BF)

        out(dqs, DQ.at[slot], 9)
        da_all = mm_nt(dqs[...], wqkv[...])
        gain = norms[0:1, :]
        for i in range(seqs):
            sl = pl.ds(i * 64, 64)
            n, r = norm_of(xs[sl, :].astype(F32))
            da = da_all[i * 64:(i + 1) * 64]
            sums[0] += fold(da * n)
            sums[1] += fold(da)
            dx = dhs[sl, :] + norm_back(n, r, da * gain)
            dxs[sl, :] = dx
            dxb[sl, :] = dx.astype(BF)
        dxo[...] = dxb[...]
        lng[0] = sums[0]
        lng[1] = sums[1]
        out(lng, LNG.at[slot], 11)

        mine = pltpu.make_async_copy(dxs, DXO.at[slot], sem.at[12])
        pl.when(slot < own)(lambda: mine.start())
        for cp in copies:
            cp.wait()
        pl.when(slot < own)(lambda: mine.wait())


def bwd_call(site, own, last, info, tok, tok_at, arr, norms, weights, saved, bufs, slots):
    model, ff = weights[2].shape[-2:]
    pairs = ROWS // 128 * (HEADS // 2)
    X, A, QKV, PP, O, H, C, MM, GP = saved
    small = ((slots, ROWS, model), BF)
    shapes = [
        small,
        ((slots, ROWS, ff), BF),
        small,
        ((slots, ROWS, 3 * model), BF),
        ((slots, 4, 8, model), F32),
        ((own, ROWS, model), F32),
    ]
    scratch = [
        pltpu.VMEM((ROWS, model), BF),
        pltpu.VMEM((ROWS, model), BF),
        pltpu.VMEM((ROWS, 3 * model), BF),
        pltpu.VMEM((pairs, 256, 128), BF),
        pltpu.VMEM((ROWS, model), F32),
        pltpu.VMEM((ROWS, ff), BF),
        pltpu.VMEM((ROWS, ff), BF),
        pltpu.VMEM((ROWS, model), F32),
        pltpu.VMEM((ROWS, model), BF),
        pltpu.VMEM((ROWS, model), BF),
        pltpu.VMEM((ROWS, 3 * model), BF),
        pltpu.VMEM((ROWS, model), F32),
        pltpu.VMEM((ROWS, model), BF),
        pltpu.VMEM((4, 8, model), F32),
        pltpu.SemaphoreType.DMA((13,)),
    ]
    has, sources, kinds = site_inputs(tok, arr)
    fixed = [info, *sources, norms, *[hbm(v) for v in (X, QKV, PP, H, GP)]]
    specs = [SMEM, *kinds, VMEM] + [ANY] * 5
    body = functools.partial(bwd_kernel, site, slots, own, last, tok_at, has, model, ff)
    return sub_call(body, fixed, specs, weights, True, shapes, scratch, bufs, ((ROWS, model), BF), "block_backward")


def lay(info, bit, pieces, o):
    n = pieces[0].shape[0]
    me = (info[GROUP] >> bit) & (len(pieces) - 1)
    for k, piece in enumerate(pieces):
        o[pl.ds(pl.multiple_of((me ^ k) * n, 8), n), :] = piece[...]


def head_kernel(own, flip, last, info, fg, fb, proj, hid, first, *rest):
    more, (whole, loss, gproj, ggain, gbias, hdy, dpool, ysc, dsc, sem) = rest[:-10], rest[-10:]
    model = proj.shape[0]
    scale = 1.5 * model**0.5
    blocks = hid.shape[0]
    loads = [pltpu.make_async_copy(hid.at[m], ysc.at[m], sem.at[m]) for m in range(blocks)]
    if last is not None:
        @pl.when(info[SECTION] == last)
        def _():
            for cp in loads:
                cp.start()

    gain, bias = fg[...].reshape(1, model), fb[...].reshape(1, model)
    if last is None:
        about = jnp.where(info[SECTION] == len(more), first[...], sum(v[...] for v in more))
    else:
        lay(info, 1, (first, *more), whole)
        about = whole[...]
    nbar = about[:, 0:model]
    image = about[:, model:2 * model]
    pidx = about[:, 2 * model:2 * model + 1].astype(jnp.int32)
    pooled = (nbar * gain + bias).astype(BF)
    text = mm(pooled, proj[...])
    inv = lax.rsqrt(jnp.sum(text * text, -1, keepdims=True) + EPS)
    unit = text * inv
    iunit = (image * lax.rsqrt(jnp.sum(image * image, -1, keepdims=True) + EPS)).astype(BF)
    logits = scale * mm_nt(unit.astype(BF), iunit)
    rmax = jnp.max(logits, 1, keepdims=True)
    rlse = rmax + jnp.log(jnp.sum(jnp.exp(logits - rmax), 1, keepdims=True))
    cmax = jnp.max(logits, 0, keepdims=True)
    clse = cmax + jnp.log(jnp.sum(jnp.exp(logits - cmax), 0, keepdims=True))
    n = logits.shape[0]
    hot = lax.broadcasted_iota(jnp.int32, (n, n), 1) == pidx
    g = 0.5 * jnp.exp(logits - rlse) + 0.5 * jnp.exp(logits - clse) - jnp.where(hot, 1.0, 0.0)
    dt = scale * mm(g.astype(BF), iunit)
    dtext = ((dt - unit * jnp.sum(dt * unit, -1, keepdims=True)) * inv).astype(BF)
    dp = mm_nt(dtext, proj[...])
    if last is None:
        at = jnp.sum(jnp.where(hot, logits, 0.0), 1, keepdims=True)
        col = jnp.sum(jnp.where(hot, jnp.broadcast_to(clse, (n, n)), 0.0), 1, keepdims=True)
        loss[...] = jnp.broadcast_to(0.5 * (rlse - at) + 0.5 * (col - at), (n, 128)).T[0:1, :].reshape(n)
        gproj[...] = mm_tn(pooled, dtext)
        ggain[...] = jnp.sum(dp * nbar, 0, keepdims=True).reshape(model)
        gbias[...] = jnp.sum(dp, 0, keepdims=True).reshape(model)

    @pl.when(info[SECTION] == (-1 if last is None else last))
    def _():
        dpool[...] = dp
        per = ROWS // 64
        stores = []
        for m in range(blocks):
            loads[m].wait()
            of = info[GROUP] if m < own else info[GROUP] ^ flip
            for i in range(per):
                count = info[LENS + m * per + i]
                nn, r = norm_of(ysc[m, pl.ds(i * 64, 64), :].astype(F32))
                w = dpool[pl.ds(of * own * per + (m % own) * per + i, 1), :] * (gain / count.astype(F32))
                ok = lax.broadcasted_iota(jnp.int32, (64, 1), 0) < count
                dsc[pl.ds(m * ROWS + i * 64, 64), :] = jnp.where(ok, norm_back(nn, r, w), 0.0).astype(BF)
            part = pl.ds(m * ROWS, ROWS)
            cp = pltpu.make_async_copy(dsc.at[part], hdy.at[part], sem.at[blocks + m])
            cp.start()
            stores.append(cp)
        for cp in stores:
            cp.wait()


def head_call(own, flip, last, info, fg, fb, proj, hid, *about):
    blocks, _, model = hid.shape
    pairs = about[0].shape[0] * (1 if last is None else len(about))
    whole = (8, 128) if last is None else (pairs, about[0].shape[1])
    return pl.pallas_call(
        functools.partial(head_kernel, own, flip, last),
        out_shape=[
            jax.ShapeDtypeStruct(whole, F32),
            jax.ShapeDtypeStruct((pairs,), F32),
            jax.ShapeDtypeStruct((model, model), F32),
            jax.ShapeDtypeStruct((model,), F32),
            jax.ShapeDtypeStruct((model,), F32),
            pltpu.HBM((blocks * ROWS, model), BF),
        ],
        in_specs=[SMEM] + [VMEM] * 3 + [ANY] + [VMEM] * len(about),
        out_specs=[VMEM, VMEM, VMEM, VMEM, VMEM, ANY],
        scratch_shapes=[
            pltpu.VMEM((pairs, model), F32),
            pltpu.VMEM((blocks, ROWS, model), BF),
            pltpu.VMEM((blocks * ROWS, model), BF),
            pltpu.SemaphoreType.DMA((2 * blocks,)),
        ],
        compiler_params=pltpu.CompilerParams(vmem_limit_bytes=VLIM),
        cost_estimate=FREE,
        name="head",
    )(info, fg, fb, proj, hbm(hid), *about)


def bit_of(w, bit):
    return (w[GROUP] >> bit) & 1


def wgrad_kernel(bit, waits, normed, part, where, a, e, *rest):
    norms = rest[0] if normed else None
    rest = rest[waits + normed:]

    left = a[...].reshape(a.shape[0] * ROWS, a.shape[2])
    right = e[...].reshape(e.shape[0] * ROWS, e.shape[2])
    g = mm_tn(left, right)
    if normed:
        sums = jnp.sum(jnp.sum(norms[...], 0), 1)
        sums = jnp.concatenate([sums, jnp.zeros((128 - sums.shape[0], sums.shape[1]), F32)], 0)
        g = jnp.concatenate([g, sums.T], 1)
    if bit is None:
        rest[0][...] = g.astype(BF)
        return
    if part is not None:
        rest[0][0] = g.astype(BF)
        return
    send, keep = rest[:2]
    quarter = send.shape[1]
    if quarter == g.shape[0]:
        step = pl.program_id(0)

        @pl.when(step < 2)
        def _():
            send[0] = g.astype(BF)

        @pl.when(step >= 2)
        def _():
            keep[0] = g.astype(BF)
    else:
        high = bit_of(where, bit) == 1
        parts = [g[k * quarter:(k + 1) * quarter] for k in range(4)]
        for k in range(2):
            one, two = (parts[2 * k], parts[2 * k + 1]) if bit == 0 else (parts[k], parts[2 + k])
            send[k] = jnp.where(high, one, two).astype(BF)
            keep[k] = jnp.where(high, two, one).astype(BF)


def wgrad(info, left, right, after, bit, half_bit, norms=None, part=None):
    slots, _, wide = left.shape
    cols = right.shape[2]
    mine = wide // 2
    step = math.gcd(mine, 384)
    width = 1536 if cols % 1536 == 0 and mine <= 384 else 768
    left_blocks = mine // step
    single = left_blocks == 4 and bit is not None
    normed = norms is not None
    more = 128 if normed else 0

    def left_at(i, j, w):
        if single:
            own_bit = bit_of(w, bit)
            if part is None:
                other = jnp.where(i < 2, 1 - own_bit, own_bit)
            else:
                other = own_bit if part else 1 - own_bit
            k = (i % 2) * 2 + other if bit == 0 else other * 2 + i % 2
        else:
            k = i
        return (0, 0, bit_of(w, half_bit) * left_blocks + k)

    if bit is None:
        out_shape = pltpu.HBM((mine, cols + more), BF)
        out_specs = pl.BlockSpec((step, width + more), lambda i, j, w: (i, j))
    else:
        out_shape = [pltpu.HBM((2, mine // 4, cols + more), BF)] * 2
        if part is not None:
            out_shape = out_shape[0]
            out_specs = pl.BlockSpec((1, step, width), lambda i, j, w: (i, 0, j))
        elif single:
            out_specs = [
                pl.BlockSpec((1, step, width), lambda i, j, w: (jnp.minimum(i, 1), 0, j)),
                pl.BlockSpec((1, step, width), lambda i, j, w: (jnp.maximum(i - 2, 0), 0, j)),
            ]
        else:
            out_specs = [pl.BlockSpec((2, mine // 4, width + more), lambda i, j, w: (0, 0, j))] * 2
    return pl.pallas_call(
        functools.partial(wgrad_kernel, bit, len(after), normed, part),
        grid_spec=pltpu.PrefetchScalarGridSpec(
            num_scalar_prefetch=1,
            grid=(left_blocks if part is None else 2, cols // width),
            in_specs=[
                pl.BlockSpec((slots, ROWS, step), left_at),
                pl.BlockSpec((slots, ROWS, width), lambda i, j, w: (0, 0, j)),
                *([pl.BlockSpec((slots, 4, 8, step), lambda i, j, w: (0, 0, 0, bit_of(w, half_bit)))] if normed else []),
                *[ANY for _ in after],
            ],
            out_specs=out_specs,
        ),
        out_shape=out_shape,
        compiler_params=pltpu.CompilerParams(vmem_limit_bytes=VLIM),
        cost_estimate=FREE,
        name="weight_grad",
    )(info, hbm(left), hbm(right), *([norms] if normed else []), *map(hbm, after))


def halves(g, info, bit):
    quarter = g.shape[0] // 4
    parts = [g[k * quarter:(k + 1) * quarter] for k in range(4)]
    high = bit_of(info, bit) == 1
    send, keep = [], []
    for k in range(2):
        one, two = (parts[2 * k], parts[2 * k + 1]) if bit == 0 else (parts[k], parts[2 + k])
        send.append(jnp.where(high, one, two).astype(BF))
        keep.append(jnp.where(high, two, one).astype(BF))
    return send, keep


def attention_kernel(info, a, o, dq, f, norms, after, send_one, keep_one, send_two, keep_two):
    j = pl.program_id(0)
    thirds = pl.num_programs(0) - 1

    def product(left, right):
        return mm_tn(left[...].reshape(-1, left.shape[2]), right[...].reshape(-1, right.shape[2]))

    def put(g, outs, bit, at, width):
        for value, out in zip(halves(g, info, bit), outs):
            for k in range(2):
                out[k, :, pl.ds(at, width)] = value[k]

    one, two = (send_one, keep_one), (send_two, keep_two)
    width = dq.shape[2]
    for k in range(3):
        @pl.when(j == k)
        def _():
            put(product(a, dq), one if k < 2 else two, 0 if k < 2 else 1, k * width if k < 2 else 0, width)

    @pl.when(j == thirds)
    def _():
        put(product(o, f), two, 1, width, width)
        sums = jnp.sum(jnp.sum(norms[...], 0), 1)
        sums = jnp.concatenate([sums, jnp.zeros((128 - sums.shape[0], sums.shape[1]), F32)], 0)
        put(sums.T, two, 1, 2 * width, 128)


def attention_wgrad(info, a, dq, o, f, norms, after, half_bit):
    slots, _, model = a.shape
    mine = model // 2
    left = pl.BlockSpec((slots, ROWS, mine), lambda j, w: (0, 0, bit_of(w, half_bit)))
    shapes = [(2, mine // 4, 2 * model)] * 2 + [(2, mine // 4, 2 * model + 128)] * 2
    return pl.pallas_call(
        attention_kernel,
        grid_spec=pltpu.PrefetchScalarGridSpec(
            num_scalar_prefetch=1,
            grid=(4,),
            in_specs=[
                left,
                left,
                pl.BlockSpec((slots, ROWS, model), lambda j, w: (0, 0, jnp.minimum(j, 2))),
                pl.BlockSpec((slots, ROWS, model), lambda j, w: (0, 0, 0)),
                pl.BlockSpec((slots, 4, 8, mine), lambda j, w: (0, 0, 0, bit_of(w, half_bit))),
                ANY,
            ],
            out_specs=[pl.BlockSpec(s, lambda j, w: (0, 0, 0)) for s in shapes],
        ),
        out_shape=[pltpu.HBM(s, BF) for s in shapes],
        compiler_params=pltpu.CompilerParams(vmem_limit_bytes=VLIM),
        cost_estimate=FREE,
        name="attention_weight_grad",
    )(info, hbm(a), hbm(o), hbm(dq), hbm(f), norms, hbm(after))


def attention_total_kernel(keep_one, came_one, keep_two, came_two, after, qkv, out, *norms):
    model = out.shape[1]
    qkv[:, 0:2 * model] = keep_one[...].astype(F32) + came_one[...].astype(F32)
    two = keep_two[...].astype(F32) + came_two[...].astype(F32)
    qkv[:, 2 * model:] = two[:, 0:model]
    out[...] = two[:, model:2 * model]
    rows = two.shape[0]
    sums = jnp.concatenate([two[:, 2 * model:], jnp.zeros((128 - rows, 128), F32)], 0).T
    for k, o in enumerate(norms):
        o[...] = sums[k:k + 1, 0:rows]


def attention_total(keep_one, came_one, keep_two, came_two, after):
    rows, cols = keep_one.shape
    model = cols // 2
    return pl.pallas_call(
        attention_total_kernel,
        in_specs=[VMEM] * 4 + [ANY],
        out_specs=[VMEM] * 6,
        out_shape=[jax.ShapeDtypeStruct(s, F32) for s in [(rows, 3 * model), (rows, model)] + [(1, rows)] * 4],
        cost_estimate=FREE,
        name="attention_total",
    )(keep_one, came_one, keep_two, came_two, hbm(after))


def fold_kernel(bit, info, keep, came, after, send, left):
    high = bit_of(info, bit) == 1
    one = keep[0].astype(F32) + came[0].astype(F32)
    two = keep[1].astype(F32) + came[1].astype(F32)
    send[...] = jnp.where(high, one, two).astype(BF)
    left[...] = jnp.where(high, two, one).astype(BF)


def fold(info, keep, came, after, bit):
    _, rows, cols = keep.shape
    width = 768 if cols % 768 == 0 else cols
    block = pl.BlockSpec((2, rows, width), lambda j, w: (0, 0, j))
    half = pl.BlockSpec((rows, width), lambda j, w: (0, j))
    return pl.pallas_call(
        functools.partial(fold_kernel, bit),
        grid_spec=pltpu.PrefetchScalarGridSpec(
            num_scalar_prefetch=1, grid=(cols // width,), in_specs=[block, block, ANY], out_specs=[half, half]
        ),
        out_shape=[pltpu.HBM((rows, cols), BF)] * 2,
        compiler_params=pltpu.CompilerParams(vmem_limit_bytes=VLIM),
        cost_estimate=FREE,
        name="fold",
    )(info, keep, came, hbm(after))


def total_kernel(keep, came, *rest):
    o = rest[-1]
    o[...] = keep[...].astype(F32) + came[...].astype(F32)


def total(keep, came, *after):
    rows, cols = keep.shape
    width = 768 if cols % 768 == 0 else cols
    block = pl.BlockSpec((rows, width), lambda j: (0, j))
    return pl.pallas_call(
        total_kernel,
        grid=(cols // width,),
        in_specs=[block, block] + [ANY] * len(after),
        out_specs=block,
        out_shape=pltpu.HBM((rows, cols), F32),
        compiler_params=pltpu.CompilerParams(vmem_limit_bytes=VLIM),
        cost_estimate=FREE,
        name="total",
    )(keep, came, *map(hbm, after))


def swap_bit(value, axis, bit):
    peers = lax.axis_size(axis)
    return lax.ppermute(value, axis, [(i, i ^ (1 << bit)) for i in range(peers)])


def pack_kernel(pairs, nb, img, o):
    model = img.shape[1]
    n, per = nb.shape[:2]
    for i in range(n):
        o[pl.ds(i * per, per), 0:model] = nb[i]
    o[:, model:2 * model] = img[...].astype(F32)
    for i in range(n * per):
        o[pl.ds(i, 1), 2 * model:] = jnp.full((1, 128), pairs[i], jnp.int32).astype(F32)


def join_kernel(bit, info, *rest):
    lay(info, bit, rest[:-2], rest[-1])


def copy_kernel(value, *rest):
    rest[-1][...] = value[...]


def numbers_kernel(info, after, o):
    for k in range(o.shape[0]):
        o[k] = info[k]


def numbers(info, after):
    return pl.pallas_call(
        numbers_kernel,
        out_shape=jax.ShapeDtypeStruct(info.shape, jnp.int32),
        in_specs=[SMEM, LOOSE],
        out_specs=SMEM,
        cost_estimate=FREE,
        name="numbers",
    )(info, after)


def small_call(body, specs, shape, name, *args):
    return pl.pallas_call(
        body,
        out_shape=jax.ShapeDtypeStruct(shape, F32),
        in_specs=specs,
        out_specs=VMEM,
        compiler_params=pltpu.CompilerParams(vmem_limit_bytes=8 << 20),
        cost_estimate=FREE,
        name=name,
    )(*args)


def joined(info, bit, value, others, after):
    shape = ((1 + len(others)) * value.shape[0], value.shape[1])
    body = functools.partial(join_kernel, bit)
    return small_call(body, [SMEM] + [VMEM] * (1 + len(others)) + [LOOSE], shape, "join", info, value, *others, after)


def split(value, at, mine):
    keep = lax.dynamic_index_in_dim(value, mine, at, keepdims=False)
    return lax.dynamic_index_in_dim(value, 1 - mine, at, keepdims=False), keep


def scattered(pair, axis, me, bits, total_bits):
    left = list(range(total_bits - 1, -1, -1))
    for place, bit in enumerate(bits):
        if place > 0:
            send, keep = split(value, left.index(bit), (me >> bit) & 1)
            came = swap_bit(send, axis, bit)
        else:
            came, keep = pair
        value = keep.astype(F32) + came.astype(F32)
        if place < len(bits) - 1:
            value = value.astype(BF)
        left.remove(bit)
    return value


def on_device(tokens, lengths, pair_index, images, ln1_gain, ln1_bias, qkv_weight, out_weight,
              ln2_gain, ln2_bias, up_weight, down_weight, final_gain, final_bias, proj_weight):
    groups = lax.axis_size("dp")
    sections = lax.axis_size("section")
    section = lax.axis_index("section")
    group = lax.axis_index("dp")
    model = tokens.shape[1]
    n_seq = lengths.shape[0]
    flip = groups - 2
    own = tokens.shape[0] // ROWS
    slots = 2 * own

    last = sections - 1
    norms = jnp.concatenate([ln1_gain, ln1_bias, ln2_gain, ln2_bias], 0)
    weights = (qkv_weight, out_weight, up_weight, down_weight)
    who = jnp.stack([section, group]).astype(jnp.int32)
    info_own = jnp.concatenate([who, lengths, lengths])
    theirs = lax.ppermute(
        tokens, ("dp", "section"), [(d * sections, (d ^ flip) * sections) for d in range(groups)]
    )
    theirs_lengths = lax.ppermute(lengths, "dp", [(d, d ^ flip) for d in range(groups)])
    info = jnp.concatenate([who, lengths, theirs_lengths])
    bufs = about = coming = None
    sites = slots + LAG * last

    def pairs_at(t, turn):
        return [turn(s) for s in range(last) if 0 <= t - LAG * s < slots]

    hop = {}
    for t in range(sites):
        tok, at = (None, 0) if t >= slots else (hbm(tokens), t * ROWS) if t < own else (theirs, (t - own) * ROWS)
        bufs, weights, y = fwd_call(
            t, own, last, info_own if t < 1 else info, tok, at, hop.get(t - LAG), norms, weights, bufs, slots
        )
        pairs = pairs_at(t, lambda s: (s, s + 1))
        if pairs:
            hop[t] = lax.ppermute(y, "section", pairs)
        m = t - LAG * last
        if m == own - 1:
            about = small_call(pack_kernel, [SMEM, VMEM, VMEM], (n_seq, 2 * model + 128), "pack", pair_index, bufs[10], images)
            coming = [swap_bit(about, "dp", 0)]
        elif m == own:
            about = joined(info, 0, about, coming, y)
            coming = [
                lax.ppermute(about, "dp", [(d, d ^ (2 * k)) for d in range(groups)]) for k in range(1, groups // 2)
            ]
    saved, hid = bufs[:9], bufs[9]
    about, *_, hdy = head_call(own, flip, last, info, final_gain, final_bias, proj_weight, hid, about, *coming)

    back = None
    step = {}
    for t in range(sites):
        tok, at = (None, 0) if t >= slots else (hbm(hdy), t * ROWS)
        back, weights, dx = bwd_call(t, own, last, info, tok, at, step.get(t - LAG), norms, weights, saved, back, slots)
        pairs = pairs_at(t, lambda s: (last - s, last - s - 1))
        if pairs:
            step[t] = lax.ppermute(dx, "section", pairs)
    E, DU, F, DQ, LNG, DXO = back
    X, A, QKV, PP, O, H, C, MM, GP = saved

    bits = (groups // 2).bit_length() - 1
    low_first = list(range(bits))
    high_first = low_first[::-1]
    def head_again(after):
        late = small_call(copy_kernel, [VMEM, ANY], about.shape, "copy", about, hbm(after))
        shared = [lax.ppermute(late, "section", [(last, t)]) for t in range(last)]
        return head_call(own, flip, None, info, final_gain, final_bias, proj_weight, hid, late, *shared)

    if bits == 2:
        down = wgrad(info, MM, E, [dx], 0, bits, part=0)
        up = wgrad(info, C, DU, [down], 1, bits)
        one, kept_one, two, kept_two = attention_wgrad(info, A, DQ, O, F, LNG, up[0], bits)
        kept_down = wgrad(info, MM, E, [two], 0, bits, part=1)
        pieces = [(down, kept_down), up, (one, kept_one), (two, kept_two)]
        orders = (low_first, high_first, low_first, high_first)
        sent = [swap_bit(send, "dp", order[0]) for (send, _), order in zip(pieces, orders)]
        tail = head_again(kept_down)
        after = tail[2]
        held = []
        for came, (_, keep), order in zip(sent, pieces, orders):
            after, keep = fold(info, keep, came, after, order[1])
            held += [keep, swap_bit(after, "dp", order[1])]
        g_down = total(held[0], held[1], after)
        g_up = total(held[2], held[3], g_down)
        g_qkv, g_out, *g_norm = attention_total(*held[4:], g_up)
    else:
        me = numbers(info, dx)[GROUP]
        grads = []
        after = [dx]
        for a, e, norm, order in (
            (MM, E, None, low_first), (C, DU, None, high_first), (A, DQ, None, low_first), (O, F, LNG, high_first)
        ):
            after = [wgrad(info, a, e, after, None, bits, norm)]
            rows, cols = after[0].shape
            cut = after[0].reshape((2,) * bits + (rows >> bits, cols))
            send, keep = split(cut, bits - 1 - order[0], (me >> order[0]) & 1)
            grads.append(scattered((swap_bit(send, "dp", order[0]), keep), "dp", me, order, bits))
        g_down, g_up, g_qkv, g_out = grads
        g_out, g_norm = g_out[:, :model], [g_out[:, model + k][None] for k in range(4)]
        tail = head_again(after[0])
    return (
        bufs[11].reshape(1, own * ROWS, model),
        DXO.reshape(1, own * ROWS, model),
        g_norm[0],
        g_norm[1],
        g_qkv[None],
        g_out[None],
        g_norm[2],
        g_norm[3],
        g_up[None],
        g_down[None],
        tail[3],
        tail[4],
        tail[2],
        tail[1],
    )


def solution(mesh):
    row = P("section", None)
    cube = P("section", None, None)
    in_specs = (P("dp", None), P("dp"), P("dp"), P("dp", None), row, row, cube, cube, row, row, cube, cube, P(), P(), P())
    big = P("section", "dp", None)
    small = P("section", "dp")
    out_specs = (big, big, small, small, big, big, small, small, big, big, P(), P(), P(), P())
    return jax.shard_map(on_device, mesh=mesh, in_specs=in_specs, out_specs=out_specs, check_vma=False)
```

```python
import functools
import math

import jax
import jax.numpy as jnp
from jax import lax
from jax.experimental import pallas as pl
from jax.experimental.pallas import tpu as pltpu
from jax.sharding import PartitionSpec as P

HEADS = 12
HEAD = 64
PAIR = 2 * HEAD
ROWS = 256
EPS = 1e-06
MASKED = -1000000000.0
BF = jnp.bfloat16
F32 = jnp.float32
ANY = pl.BlockSpec(memory_space=pltpu.HBM)
LOOSE = pl.BlockSpec(memory_space=pl.ANY)
SMEM = pl.BlockSpec(memory_space=pltpu.SMEM)
VMEM = pl.BlockSpec(memory_space=pltpu.VMEM)
VLIM = 24 << 20
LAG = 2
FREE = pl.CostEstimate(flops=1, bytes_accessed=1, transcendentals=0)
SECTION, GROUP, LENS = range(3)


def hbm(v):
    return pltpu.with_memory_space_constraint(v, pltpu.HBM)


def vmem(v):
    return pltpu.with_memory_space_constraint(v, pltpu.VMEM)


def mm(a, b):
    return jnp.dot(a, b, preferred_element_type=F32)


def mm_nt(a, b):
    return lax.dot_general(a, b, (((1,), (1,)), ((), ())), preferred_element_type=F32)


def mm_tn(a, b):
    return lax.dot_general(a, b, (((0,), (0,)), ((), ())), preferred_element_type=F32)


def norm_of(v):
    c = v - jnp.mean(v, -1, keepdims=True)
    r = lax.rsqrt(jnp.mean(c * c, -1, keepdims=True) + EPS)
    return c * r, r


def norm_back(n, r, w):
    return r * (w - jnp.mean(w, -1, keepdims=True) - n * jnp.mean(w * n, -1, keepdims=True))


def gelu_pair(u):
    k = 0.7978845608028654
    u2 = u * u
    t = jnp.tanh(u * (k + (k * 0.044715) * u2))
    p = 0.5 + 0.5 * t
    g = p + (0.5 * u) * ((1.0 - t * t) * (k + (3.0 * k * 0.044715) * u2))
    return u * p, g


def split_heads(v, low):
    z = jnp.zeros_like(v)
    return jnp.concatenate([jnp.where(low, v, z), jnp.where(low, z, v)], axis=0)


def low_lanes():
    return lax.broadcasted_iota(jnp.int32, (PAIR, PAIR), 1) < HEAD


def chunk(j, width):
    return pl.ds(pl.multiple_of(j * width, 128), width)


class Weights:
    def __init__(self, sources, held, sem, model):
        self.sem, self.jobs, self.due = sem, {}, sources is not None
        if not self.due:
            return
        k = 0
        for name, src, dst in zip(("qkv", "out", "up", "down"), sources, held):
            rows, cols = dst.shape
            for j in range(max(rows, cols) // model):
                piece = pl.ds(j * model, model)
                at = (slice(None), piece) if cols > model else (piece, slice(None))
                self.jobs[name, j] = (src, dst, at, k)
                k += 1

    def copy(self, name, j, offset=0):
        src, dst, at, k = self.jobs[name, j]
        return pltpu.make_async_copy(src.at[(0,) + at], dst.at[at], self.sem.at[k + offset])

    def start(self, name, *pieces):
        for j in pieces or [j for n, j in self.jobs if n == name]:
            self.copy(name, j).start()

    def wait(self, name, j=0):
        if self.due:
            self.copy(name, 0, j).wait()


def fetch(place, tok, tok_at, arr, dst, sem):
    def copy():
        return pltpu.make_async_copy(tok.at[pl.ds(tok_at, ROWS)], dst, sem)

    def from_arr():
        dst[...] = arr[...]

    if tok is None:
        return from_arr
    if arr is None:
        copy().start()
        return lambda: copy().wait()
    pl.when(place == 0)(lambda: copy().start())

    def finish():
        pl.when(place == 0)(lambda: copy().wait())
        pl.when(place != 0)(from_arr)

    return finish


def fwd_kernel(fresh, site, slots, own, last, tok_at, has, model, ff, info, *rest):
    tok = rest[0] if has[0] else None
    arr = rest[has[0]] if has[1] else None
    norms, w1, w2, w3, w4, *rest = rest[sum(has):]
    (X, A, QKV, PP, O, H, C, MM, GP, HID, NB, Y, wqkv, wo, wup, wdn, yout,
     xs, as_, qs, ps, os_, hs, cs, ms, gs, ys, nb, sem, wsem) = rest
    weights = Weights((w1, w2, w3, w4) if fresh else None, (wqkv, wo, wup, wdn), wsem, model)
    names = ("qkv", "out", "up", "down")
    seqs = ROWS // 64
    section = info[SECTION]
    slot = site - LAG * section
    active = (slot >= 0) & (slot < slots)

    def length(i):
        return info[LENS + slot * seqs + i]

    if fresh:
        @pl.when(jnp.logical_not(active))
        def _():
            for name in names:
                weights.start(name)
            for name, j in weights.jobs:
                weights.wait(name, j)

    @pl.when(active)
    def _():
        come = fetch(section, tok, tok_at, arr, xs, sem.at[0])
        weights.start("qkv")
        come()
        weights.start("out")
        weights.start("up")
        copies = []

        def out(src, dst, k):
            cp = pltpu.make_async_copy(src, dst, sem.at[k])
            cp.start()
            copies.append(cp)

        out(xs, X.at[slot], 18)
        gain, bias = norms[0:1, :], norms[1:2, :]
        for i in range(seqs):
            sl = pl.ds(i * 64, 64)
            n, _r = norm_of(xs[sl, :].astype(F32))
            as_[sl, :] = (n * gain + bias).astype(BF)
        out(as_, A.at[slot], 2)

        for j in range(3):
            sl = pl.ds(j * model, model)
            weights.wait("qkv", j)
            qs[:, sl] = mm(as_[...], wqkv[:, sl]).astype(BF)

        weights.start("down")

        out(qs, QKV.at[slot], 3)
        low = low_lanes()
        row = lax.broadcasted_iota(jnp.int32, (PAIR, PAIR), 0)
        col = lax.broadcasted_iota(jnp.int32, (PAIR, PAIR), 1)

        for it in range(ROWS // 128 * (HEADS // 2)):
            p, hp = divmod(it, HEADS // 2)
            if hp == 0:
                ok = ((col < 64) & (row < length(2 * p))) | ((col >= 64) & (row >= 64) & (row < 64 + length(2 * p + 1)))
            rs = pl.ds(p * 128, 128)

            def lanes(block):
                return pl.ds(block * model + hp * PAIR, PAIR)

            q2 = qs[rs, lanes(0)] * jnp.asarray(HEAD**-0.5, BF)
            s = mm_nt(split_heads(qs[rs, lanes(1)], low), q2)
            halves = []
            for h in range(2):
                sh = jnp.where(ok, s[h * 128:(h + 1) * 128], MASKED)
                e = jnp.exp(sh - jnp.max(sh, 0, keepdims=True))
                halves.append((e * (1.0 / jnp.sum(e, 0, keepdims=True))).astype(BF))
            pc = jnp.concatenate(halves, axis=0)
            ps[it] = pc
            os_[rs, lanes(0)] = mm_tn(pc, split_heads(qs[rs, lanes(2)], low)).astype(BF)

        out(ps, PP.at[slot], 4)
        out(os_, O.at[slot], 5)
        weights.wait("out")
        hs[...] = xs[...].astype(F32) + mm(os_[...], wo[...])
        out(hs, H.at[slot], 6)
        gain2, bias2 = norms[2:3, :], norms[3:4, :]
        for i in range(seqs):
            sl = pl.ds(i * 64, 64)
            n, _r = norm_of(hs[sl, :])
            cs[sl, :] = (n * gain2 + bias2).astype(BF)
        out(cs, C.at[slot], 7)
        parts = ff // model
        total = hs[...]
        for j in range(parts):
            sl = pl.ds(j * model, model)
            weights.wait("up", j)
            m, g = gelu_pair(mm(cs[...], wup[:, sl]))
            ms[:, sl] = m.astype(BF)
            gs[:, sl] = g.astype(BF)
            out(ms.at[:, sl], MM.at[slot, :, sl], 10 + 2 * j)
            out(gs.at[:, sl], GP.at[slot, :, sl], 11 + 2 * j)
            weights.wait("down", j)
            total = total + mm(ms[:, sl], wdn[sl, :])
        ys[...] = total.astype(BF)
        yout[...] = ys[...]
        mine = pltpu.make_async_copy(ys, Y.at[slot], sem.at[1])
        pl.when(slot < own)(lambda: mine.start())
        if site >= LAG * last:
            top = pltpu.make_async_copy(ys, HID.at[slot], sem.at[9])
            means = pltpu.make_async_copy(nb, NB.at[slot], sem.at[0])
            first = site - LAG * last < own

            @pl.when(section == last)
            def _():
                top.start()
                if first:
                    for i in range(seqs):
                        n, _r = norm_of(ys[pl.ds(i * 64, 64), :].astype(F32))
                        count = length(i)
                        ok = lax.broadcasted_iota(jnp.int32, (64, 1), 0) < count
                        nb[pl.ds(i, 1), :] = jnp.sum(jnp.where(ok, n, 0.0), 0, keepdims=True) / count.astype(F32)
                    means.start()

        for cp in copies:
            cp.wait()
        pl.when(slot < own)(lambda: mine.wait())
        if site >= LAG * last:
            @pl.when(section == last)
            def _():
                top.wait()
                if first:
                    means.wait()


def sub_call(body, fixed, specs, weights, held, shapes, scratch, bufs, last_shape, name):
    n, many = len(fixed) + 4, len(shapes)
    alias = {}
    extra = []
    kernel = body
    if held:
        alias = {len(fixed) + i: many + i for i in range(4)}
        weights = [vmem(w) for w in weights]
    else:
        weights = [hbm(w) for w in weights]
    if bufs is not None:
        alias |= {n + i: i for i in range(many)}
        extra = [hbm(v) for v in bufs]

        def kernel(*refs):
            body(*refs[:n], *refs[n + many:])

    res = pl.pallas_call(
        kernel,
        out_shape=[pltpu.HBM(s, d) for s, d in shapes]
        + [pltpu.VMEM(w.shape[-2:], BF) for w in weights]
        + [jax.ShapeDtypeStruct(*last_shape)],
        in_specs=specs + [VMEM if held else ANY] * 4 + [ANY] * len(extra),
        out_specs=[ANY] * many + [VMEM] * 5,
        input_output_aliases=alias,
        scratch_shapes=scratch,
        compiler_params=pltpu.CompilerParams(vmem_limit_bytes=VLIM),
        cost_estimate=FREE,
        name=name,
    )(*fixed, *weights, *extra)
    return res[:many], res[many:many + 4], res[-1]


def site_inputs(tok, arr):
    has = (tok is not None, arr is not None)
    sources = [tok] if has[0] else []
    specs = [LOOSE] * has[0] + [VMEM] * has[1]
    return has, sources + ([arr] if has[1] else []), specs


def fwd_call(site, own, last, info, tok, tok_at, arr, norms, weights, bufs, slots):
    model, ff = weights[2].shape[-2:]
    pairs = ROWS // 128 * (HEADS // 2)
    small = ((slots, ROWS, model), BF)
    wide = ((slots, ROWS, ff), BF)
    shapes = [
        small,
        small,
        ((slots, ROWS, 3 * model), BF),
        ((slots, pairs, 256, 128), BF),
        small,
        ((slots, ROWS, model), F32),
        small,
        wide,
        wide,
        small,
        ((own, ROWS // 64, model), F32),
        ((own, ROWS, model), BF),
    ]
    scratch = [
        pltpu.VMEM((ROWS, model), BF),
        pltpu.VMEM((ROWS, model), BF),
        pltpu.VMEM((ROWS, 3 * model), BF),
        pltpu.VMEM((pairs, 256, 128), BF),
        pltpu.VMEM((ROWS, model), BF),
        pltpu.VMEM((ROWS, model), F32),
        pltpu.VMEM((ROWS, model), BF),
        pltpu.VMEM((ROWS, ff), BF),
        pltpu.VMEM((ROWS, ff), BF),
        pltpu.VMEM((ROWS, model), BF),
        pltpu.VMEM((ROWS // 64, model), F32),
        pltpu.SemaphoreType.DMA((11 + 2 * (ff // model),)),
        pltpu.SemaphoreType.DMA((4 + 2 * (ff // model),)),
    ]
    fresh = bufs is None
    has, sources, kinds = site_inputs(tok, arr)
    fixed = [info, *sources, norms]
    specs = [SMEM, *kinds, VMEM]
    body = functools.partial(fwd_kernel, fresh, site, slots, own, last, tok_at, has, model, ff)
    return sub_call(body, fixed, specs, weights, not fresh, shapes, scratch, bufs, ((ROWS, model), BF), "block_forward")


def bwd_kernel(site, slots, own, last, tok_at, has, model, ff, info, *rest):
    tok = rest[0] if has[0] else None
    arr = rest[has[0]] if has[1] else None
    norms, X, QKV, PP, H, GP, w1, w2, w3, w4, *rest = rest[sum(has):]
    (E, DU, F, DQ, LNG, DXO, wqkv, wo, wup, wdn, dxo,
     es, xs, qs, ps, hs, gs, dus, dhs, fs, dos, dqs, dxs, dxb, lng, sem) = rest
    seqs = ROWS // 64
    place = last - info[SECTION]
    slot = site - LAG * place

    @pl.when((slot >= 0) & (slot < slots))
    def _():
        come = fetch(place, tok, tok_at, arr, es, sem.at[0])
        slope = pltpu.make_async_copy(GP.at[slot], gs, sem.at[5])
        slope.start()
        copies = []

        def out(src, dst, k):
            cp = pltpu.make_async_copy(src, dst, sem.at[k])
            cp.start()
            copies.append(cp)

        parts = ff // model
        loads = []
        for k, (src, dst) in enumerate(((H, hs), (PP, ps), (QKV, qs), (X, xs))):
            loads.append(pltpu.make_async_copy(src.at[slot], dst, sem.at[1 + k]))
        for cp in loads:
            cp.start()
        come()
        slope.wait()
        out(es, E.at[slot], 6)
        dc_all = None
        for j in range(parts):
            sl = pl.ds(j * model, model)
            du = (mm_nt(es[...], wdn[sl, :]) * gs[:, sl].astype(F32)).astype(BF)
            dus[:, sl] = du
        dc_all = mm_nt(dus[...], wup[...])
        out(dus, DU.at[slot], 7)
        for cp in loads:
            cp.wait()
        sums = [jnp.zeros((8, model), F32) for _ in range(4)]

        def fold(v):
            return jnp.sum(v.reshape(8, 8, model), axis=0)

        gain = norms[2:3, :]
        for i in range(seqs):
            sl = pl.ds(i * 64, 64)
            n, r = norm_of(hs[sl, :])
            dc = dc_all[i * 64:(i + 1) * 64]
            sums[2] += fold(dc * n)
            sums[3] += fold(dc)
            dh = es[sl, :].astype(F32) + norm_back(n, r, dc * gain)
            dhs[sl, :] = dh
            fs[sl, :] = dh.astype(BF)
        lng[2] = sums[2]
        lng[3] = sums[3]
        out(fs, F.at[slot], 8)
        dos[...] = mm_nt(fs[...], wo[...]).astype(BF)
        low = low_lanes()

        for it in range(ROWS // 128 * (HEADS // 2)):
            p, hp = divmod(it, HEADS // 2)
            rs = pl.ds(p * 128, 128)

            def lanes(block):
                return pl.ds(block * model + hp * PAIR, PAIR)

            q2 = qs[rs, lanes(0)]
            do2 = dos[rs, lanes(0)]
            pc = ps[it]
            t = pc.astype(F32) * mm_nt(split_heads(qs[rs, lanes(2)], low), do2)
            halves = []
            for h in range(2):
                hl = slice(h * 128, (h + 1) * 128)
                halves.append((t[hl] - pc[hl].astype(F32) * jnp.sum(t[hl], 0, keepdims=True)).astype(BF))
            ds = jnp.concatenate(halves, axis=0)
            scale = HEAD**-0.5
            dq = mm_tn(ds, split_heads(qs[rs, lanes(1)], low)) * scale
            dk = mm(ds, q2) * scale
            dv = mm(pc, do2)
            dqs[rs, lanes(0)] = dq.astype(BF)
            dqs[rs, lanes(1)] = jnp.where(low, dk[:128], dk[128:]).astype(BF)
            dqs[rs, lanes(2)] = jnp.where(low, dv[:128], dv[128:]).astype(BF)

        out(dqs, DQ.at[slot], 9)
        da_all = mm_nt(dqs[...], wqkv[...])
        gain = norms[0:1, :]
        for i in range(seqs):
            sl = pl.ds(i * 64, 64)
            n, r = norm_of(xs[sl, :].astype(F32))
            da = da_all[i * 64:(i + 1) * 64]
            sums[0] += fold(da * n)
            sums[1] += fold(da)
            dx = dhs[sl, :] + norm_back(n, r, da * gain)
            dxs[sl, :] = dx
            dxb[sl, :] = dx.astype(BF)
        dxo[...] = dxb[...]
        lng[0] = sums[0]
        lng[1] = sums[1]
        out(lng, LNG.at[slot], 11)

        mine = pltpu.make_async_copy(dxs, DXO.at[slot], sem.at[12])
        pl.when(slot < own)(lambda: mine.start())
        for cp in copies:
            cp.wait()
        pl.when(slot < own)(lambda: mine.wait())


def bwd_call(site, own, last, info, tok, tok_at, arr, norms, weights, saved, bufs, slots):
    model, ff = weights[2].shape[-2:]
    pairs = ROWS // 128 * (HEADS // 2)
    X, A, QKV, PP, O, H, C, MM, GP = saved
    small = ((slots, ROWS, model), BF)
    shapes = [
        small,
        ((slots, ROWS, ff), BF),
        small,
        ((slots, ROWS, 3 * model), BF),
        ((slots, 4, 8, model), F32),
        ((own, ROWS, model), F32),
    ]
    scratch = [
        pltpu.VMEM((ROWS, model), BF),
        pltpu.VMEM((ROWS, model), BF),
        pltpu.VMEM((ROWS, 3 * model), BF),
        pltpu.VMEM((pairs, 256, 128), BF),
        pltpu.VMEM((ROWS, model), F32),
        pltpu.VMEM((ROWS, ff), BF),
        pltpu.VMEM((ROWS, ff), BF),
        pltpu.VMEM((ROWS, model), F32),
        pltpu.VMEM((ROWS, model), BF),
        pltpu.VMEM((ROWS, model), BF),
        pltpu.VMEM((ROWS, 3 * model), BF),
        pltpu.VMEM((ROWS, model), F32),
        pltpu.VMEM((ROWS, model), BF),
        pltpu.VMEM((4, 8, model), F32),
        pltpu.SemaphoreType.DMA((13,)),
    ]
    has, sources, kinds = site_inputs(tok, arr)
    fixed = [info, *sources, norms, *[hbm(v) for v in (X, QKV, PP, H, GP)]]
    specs = [SMEM, *kinds, VMEM] + [ANY] * 5
    body = functools.partial(bwd_kernel, site, slots, own, last, tok_at, has, model, ff)
    return sub_call(body, fixed, specs, weights, True, shapes, scratch, bufs, ((ROWS, model), BF), "block_backward")


def lay(info, bit, pieces, o):
    n = pieces[0].shape[0]
    me = (info[GROUP] >> bit) & (len(pieces) - 1)
    for k, piece in enumerate(pieces):
        o[pl.ds(pl.multiple_of((me ^ k) * n, 8), n), :] = piece[...]


def head_kernel(own, flip, last, info, fg, fb, proj, hid, first, *rest):
    more, (whole, loss, gproj, ggain, gbias, hdy, dpool, ysc, dsc, sem) = rest[:-10], rest[-10:]
    model = proj.shape[0]
    scale = 1.5 * model**0.5
    blocks = hid.shape[0]
    loads = [pltpu.make_async_copy(hid.at[m], ysc.at[m], sem.at[m]) for m in range(blocks)]
    if last is not None:
        @pl.when(info[SECTION] == last)
        def _():
            for cp in loads:
                cp.start()

    gain, bias = fg[...].reshape(1, model), fb[...].reshape(1, model)
    if last is None:
        about = jnp.where(info[SECTION] == len(more), first[...], sum(v[...] for v in more))
    else:
        lay(info, 1, (first, *more), whole)
        about = whole[...]
    nbar = about[:, 0:model]
    image = about[:, model:2 * model]
    pidx = about[:, 2 * model:2 * model + 1].astype(jnp.int32)
    pooled = (nbar * gain + bias).astype(BF)
    text = mm(pooled, proj[...])
    inv = lax.rsqrt(jnp.sum(text * text, -1, keepdims=True) + EPS)
    unit = text * inv
    iunit = (image * lax.rsqrt(jnp.sum(image * image, -1, keepdims=True) + EPS)).astype(BF)
    logits = scale * mm_nt(unit.astype(BF), iunit)
    rmax = jnp.max(logits, 1, keepdims=True)
    rlse = rmax + jnp.log(jnp.sum(jnp.exp(logits - rmax), 1, keepdims=True))
    cmax = jnp.max(logits, 0, keepdims=True)
    clse = cmax + jnp.log(jnp.sum(jnp.exp(logits - cmax), 0, keepdims=True))
    n = logits.shape[0]
    hot = lax.broadcasted_iota(jnp.int32, (n, n), 1) == pidx
    g = 0.5 * jnp.exp(logits - rlse) + 0.5 * jnp.exp(logits - clse) - jnp.where(hot, 1.0, 0.0)
    dt = scale * mm(g.astype(BF), iunit)
    dtext = ((dt - unit * jnp.sum(dt * unit, -1, keepdims=True)) * inv).astype(BF)
    dp = mm_nt(dtext, proj[...])
    if last is None:
        at = jnp.sum(jnp.where(hot, logits, 0.0), 1, keepdims=True)
        col = jnp.sum(jnp.where(hot, jnp.broadcast_to(clse, (n, n)), 0.0), 1, keepdims=True)
        loss[...] = jnp.broadcast_to(0.5 * (rlse - at) + 0.5 * (col - at), (n, 128)).T[0:1, :].reshape(n)
        gproj[...] = mm_tn(pooled, dtext)
        ggain[...] = jnp.sum(dp * nbar, 0, keepdims=True).reshape(model)
        gbias[...] = jnp.sum(dp, 0, keepdims=True).reshape(model)

    @pl.when(info[SECTION] == (-1 if last is None else last))
    def _():
        dpool[...] = dp
        per = ROWS // 64
        stores = []
        for m in range(blocks):
            loads[m].wait()
            of = info[GROUP] if m < own else info[GROUP] ^ flip
            for i in range(per):
                count = info[LENS + m * per + i]
                nn, r = norm_of(ysc[m, pl.ds(i * 64, 64), :].astype(F32))
                w = dpool[pl.ds(of * own * per + (m % own) * per + i, 1), :] * (gain / count.astype(F32))
                ok = lax.broadcasted_iota(jnp.int32, (64, 1), 0) < count
                dsc[pl.ds(m * ROWS + i * 64, 64), :] = jnp.where(ok, norm_back(nn, r, w), 0.0).astype(BF)
            part = pl.ds(m * ROWS, ROWS)
            cp = pltpu.make_async_copy(dsc.at[part], hdy.at[part], sem.at[blocks + m])
            cp.start()
            stores.append(cp)
        for cp in stores:
            cp.wait()


def head_call(own, flip, last, info, fg, fb, proj, hid, *about):
    blocks, _, model = hid.shape
    pairs = about[0].shape[0] * (1 if last is None else len(about))
    whole = (8, 128) if last is None else (pairs, about[0].shape[1])
    return pl.pallas_call(
        functools.partial(head_kernel, own, flip, last),
        out_shape=[
            jax.ShapeDtypeStruct(whole, F32),
            jax.ShapeDtypeStruct((pairs,), F32),
            jax.ShapeDtypeStruct((model, model), F32),
            jax.ShapeDtypeStruct((model,), F32),
            jax.ShapeDtypeStruct((model,), F32),
            pltpu.HBM((blocks * ROWS, model), BF),
        ],
        in_specs=[SMEM] + [VMEM] * 3 + [ANY] + [VMEM] * len(about),
        out_specs=[VMEM, VMEM, VMEM, VMEM, VMEM, ANY],
        scratch_shapes=[
            pltpu.VMEM((pairs, model), F32),
            pltpu.VMEM((blocks, ROWS, model), BF),
            pltpu.VMEM((blocks * ROWS, model), BF),
            pltpu.SemaphoreType.DMA((2 * blocks,)),
        ],
        compiler_params=pltpu.CompilerParams(vmem_limit_bytes=VLIM),
        cost_estimate=FREE,
        name="head",
    )(info, fg, fb, proj, hbm(hid), *about)


def bit_of(w, bit):
    return (w[GROUP] >> bit) & 1


def wgrad_kernel(bit, waits, normed, part, where, a, e, *rest):
    norms = rest[0] if normed else None
    rest = rest[waits + normed:]

    left = a[...].reshape(a.shape[0] * ROWS, a.shape[2])
    right = e[...].reshape(e.shape[0] * ROWS, e.shape[2])
    g = mm_tn(left, right)
    if normed:
        sums = jnp.sum(jnp.sum(norms[...], 0), 1)
        sums = jnp.concatenate([sums, jnp.zeros((128 - sums.shape[0], sums.shape[1]), F32)], 0)
        g = jnp.concatenate([g, sums.T], 1)
    if bit is None:
        rest[0][...] = g.astype(BF)
        return
    if part is not None:
        rest[0][0] = g.astype(BF)
        return
    send, keep = rest[:2]
    quarter = send.shape[1]
    if quarter == g.shape[0]:
        step = pl.program_id(0)

        @pl.when(step < 2)
        def _():
            send[0] = g.astype(BF)

        @pl.when(step >= 2)
        def _():
            keep[0] = g.astype(BF)
    else:
        high = bit_of(where, bit) == 1
        parts = [g[k * quarter:(k + 1) * quarter] for k in range(4)]
        for k in range(2):
            one, two = (parts[2 * k], parts[2 * k + 1]) if bit == 0 else (parts[k], parts[2 + k])
            send[k] = jnp.where(high, one, two).astype(BF)
            keep[k] = jnp.where(high, two, one).astype(BF)


def wgrad(info, left, right, after, bit, half_bit, norms=None, part=None):
    slots, _, wide = left.shape
    cols = right.shape[2]
    mine = wide // 2
    step = math.gcd(mine, 384)
    width = 1536 if cols % 1536 == 0 and mine <= 384 else 768
    left_blocks = mine // step
    single = left_blocks == 4 and bit is not None
    normed = norms is not None
    more = 128 if normed else 0

    def left_at(i, j, w):
        if single:
            own_bit = bit_of(w, bit)
            if part is None:
                other = jnp.where(i < 2, 1 - own_bit, own_bit)
            else:
                other = own_bit if part else 1 - own_bit
            k = (i % 2) * 2 + other if bit == 0 else other * 2 + i % 2
        else:
            k = i
        return (0, 0, bit_of(w, half_bit) * left_blocks + k)

    if bit is None:
        out_shape = pltpu.HBM((mine, cols + more), BF)
        out_specs = pl.BlockSpec((step, width + more), lambda i, j, w: (i, j))
    else:
        out_shape = [pltpu.HBM((2, mine // 4, cols + more), BF)] * 2
        if part is not None:
            out_shape = out_shape[0]
            out_specs = pl.BlockSpec((1, step, width), lambda i, j, w: (i, 0, j))
        elif single:
            out_specs = [
                pl.BlockSpec((1, step, width), lambda i, j, w: (jnp.minimum(i, 1), 0, j)),
                pl.BlockSpec((1, step, width), lambda i, j, w: (jnp.maximum(i - 2, 0), 0, j)),
            ]
        else:
            out_specs = [pl.BlockSpec((2, mine // 4, width + more), lambda i, j, w: (0, 0, j))] * 2
    return pl.pallas_call(
        functools.partial(wgrad_kernel, bit, len(after), normed, part),
        grid_spec=pltpu.PrefetchScalarGridSpec(
            num_scalar_prefetch=1,
            grid=(left_blocks if part is None else 2, cols // width),
            in_specs=[
                pl.BlockSpec((slots, ROWS, step), left_at),
                pl.BlockSpec((slots, ROWS, width), lambda i, j, w: (0, 0, j)),
                *([pl.BlockSpec((slots, 4, 8, step), lambda i, j, w: (0, 0, 0, bit_of(w, half_bit)))] if normed else []),
                *[ANY for _ in after],
            ],
            out_specs=out_specs,
        ),
        out_shape=out_shape,
        compiler_params=pltpu.CompilerParams(vmem_limit_bytes=VLIM),
        cost_estimate=FREE,
        name="weight_grad",
    )(info, hbm(left), hbm(right), *([norms] if normed else []), *map(hbm, after))


def halves(g, info, bit):
    quarter = g.shape[0] // 4
    parts = [g[k * quarter:(k + 1) * quarter] for k in range(4)]
    high = bit_of(info, bit) == 1
    send, keep = [], []
    for k in range(2):
        one, two = (parts[2 * k], parts[2 * k + 1]) if bit == 0 else (parts[k], parts[2 + k])
        send.append(jnp.where(high, one, two).astype(BF))
        keep.append(jnp.where(high, two, one).astype(BF))
    return send, keep


def attention_kernel(info, a, o, dq, f, norms, after, send_one, keep_one, send_two, keep_two):
    j = pl.program_id(0)
    thirds = pl.num_programs(0) - 1

    def product(left, right):
        return mm_tn(left[...].reshape(-1, left.shape[2]), right[...].reshape(-1, right.shape[2]))

    def put(g, outs, bit, at, width):
        for value, out in zip(halves(g, info, bit), outs):
            for k in range(2):
                out[k, :, pl.ds(at, width)] = value[k]

    one, two = (send_one, keep_one), (send_two, keep_two)
    width = dq.shape[2]
    for k in range(3):
        @pl.when(j == k)
        def _():
            put(product(a, dq), one if k < 2 else two, 0 if k < 2 else 1, k * width if k < 2 else 0, width)

    @pl.when(j == thirds)
    def _():
        put(product(o, f), two, 1, width, width)
        sums = jnp.sum(jnp.sum(norms[...], 0), 1)
        sums = jnp.concatenate([sums, jnp.zeros((128 - sums.shape[0], sums.shape[1]), F32)], 0)
        put(sums.T, two, 1, 2 * width, 128)


def attention_wgrad(info, a, dq, o, f, norms, after, half_bit):
    slots, _, model = a.shape
    mine = model // 2
    left = pl.BlockSpec((slots, ROWS, mine), lambda j, w: (0, 0, bit_of(w, half_bit)))
    shapes = [(2, mine // 4, 2 * model)] * 2 + [(2, mine // 4, 2 * model + 128)] * 2
    return pl.pallas_call(
        attention_kernel,
        grid_spec=pltpu.PrefetchScalarGridSpec(
            num_scalar_prefetch=1,
            grid=(4,),
            in_specs=[
                left,
                left,
                pl.BlockSpec((slots, ROWS, model), lambda j, w: (0, 0, jnp.minimum(j, 2))),
                pl.BlockSpec((slots, ROWS, model), lambda j, w: (0, 0, 0)),
                pl.BlockSpec((slots, 4, 8, mine), lambda j, w: (0, 0, 0, bit_of(w, half_bit))),
                ANY,
            ],
            out_specs=[pl.BlockSpec(s, lambda j, w: (0, 0, 0)) for s in shapes],
        ),
        out_shape=[pltpu.HBM(s, BF) for s in shapes],
        compiler_params=pltpu.CompilerParams(vmem_limit_bytes=VLIM),
        cost_estimate=FREE,
        name="attention_weight_grad",
    )(info, hbm(a), hbm(o), hbm(dq), hbm(f), norms, hbm(after))


def attention_total_kernel(keep_one, came_one, keep_two, came_two, after, qkv, out, *norms):
    model = out.shape[1]
    qkv[:, 0:2 * model] = keep_one[...].astype(F32) + came_one[...].astype(F32)
    two = keep_two[...].astype(F32) + came_two[...].astype(F32)
    qkv[:, 2 * model:] = two[:, 0:model]
    out[...] = two[:, model:2 * model]
    rows = two.shape[0]
    sums = jnp.concatenate([two[:, 2 * model:], jnp.zeros((128 - rows, 128), F32)], 0).T
    for k, o in enumerate(norms):
        o[...] = sums[k:k + 1, 0:rows]


def attention_total(keep_one, came_one, keep_two, came_two, after):
    rows, cols = keep_one.shape
    model = cols // 2
    return pl.pallas_call(
        attention_total_kernel,
        in_specs=[VMEM] * 4 + [ANY],
        out_specs=[VMEM] * 6,
        out_shape=[jax.ShapeDtypeStruct(s, F32) for s in [(rows, 3 * model), (rows, model)] + [(1, rows)] * 4],
        cost_estimate=FREE,
        name="attention_total",
    )(keep_one, came_one, keep_two, came_two, hbm(after))


def fold_kernel(bit, info, keep, came, after, send, left):
    high = bit_of(info, bit) == 1
    one = keep[0].astype(F32) + came[0].astype(F32)
    two = keep[1].astype(F32) + came[1].astype(F32)
    send[...] = jnp.where(high, one, two).astype(BF)
    left[...] = jnp.where(high, two, one).astype(BF)


def fold(info, keep, came, after, bit):
    _, rows, cols = keep.shape
    width = 768 if cols % 768 == 0 else cols
    block = pl.BlockSpec((2, rows, width), lambda j, w: (0, 0, j))
    half = pl.BlockSpec((rows, width), lambda j, w: (0, j))
    return pl.pallas_call(
        functools.partial(fold_kernel, bit),
        grid_spec=pltpu.PrefetchScalarGridSpec(
            num_scalar_prefetch=1, grid=(cols // width,), in_specs=[block, block, ANY], out_specs=[half, half]
        ),
        out_shape=[pltpu.HBM((rows, cols), BF)] * 2,
        compiler_params=pltpu.CompilerParams(vmem_limit_bytes=VLIM),
        cost_estimate=FREE,
        name="fold",
    )(info, keep, came, hbm(after))


def total_kernel(keep, came, *rest):
    o = rest[-1]
    o[...] = keep[...].astype(F32) + came[...].astype(F32)


def total(keep, came, *after):
    rows, cols = keep.shape
    width = 768 if cols % 768 == 0 else cols
    block = pl.BlockSpec((rows, width), lambda j: (0, j))
    return pl.pallas_call(
        total_kernel,
        grid=(cols // width,),
        in_specs=[block, block] + [ANY] * len(after),
        out_specs=block,
        out_shape=pltpu.HBM((rows, cols), F32),
        compiler_params=pltpu.CompilerParams(vmem_limit_bytes=VLIM),
        cost_estimate=FREE,
        name="total",
    )(keep, came, *map(hbm, after))


def swap_bit(value, axis, bit):
    peers = lax.axis_size(axis)
    return lax.ppermute(value, axis, [(i, i ^ (1 << bit)) for i in range(peers)])


def pack_kernel(pairs, nb, img, o):
    model = img.shape[1]
    n, per = nb.shape[:2]
    for i in range(n):
        o[pl.ds(i * per, per), 0:model] = nb[i]
    o[:, model:2 * model] = img[...].astype(F32)
    for i in range(n * per):
        o[pl.ds(i, 1), 2 * model:] = jnp.full((1, 128), pairs[i], jnp.int32).astype(F32)


def join_kernel(bit, info, *rest):
    lay(info, bit, rest[:-2], rest[-1])


def copy_kernel(value, *rest):
    rest[-1][...] = value[...]


def numbers_kernel(info, after, o):
    for k in range(o.shape[0]):
        o[k] = info[k]


def numbers(info, after):
    return pl.pallas_call(
        numbers_kernel,
        out_shape=jax.ShapeDtypeStruct(info.shape, jnp.int32),
        in_specs=[SMEM, LOOSE],
        out_specs=SMEM,
        cost_estimate=FREE,
        name="numbers",
    )(info, after)


def small_call(body, specs, shape, name, *args):
    return pl.pallas_call(
        body,
        out_shape=jax.ShapeDtypeStruct(shape, F32),
        in_specs=specs,
        out_specs=VMEM,
        compiler_params=pltpu.CompilerParams(vmem_limit_bytes=8 << 20),
        cost_estimate=FREE,
        name=name,
    )(*args)


def joined(info, bit, value, others, after):
    shape = ((1 + len(others)) * value.shape[0], value.shape[1])
    body = functools.partial(join_kernel, bit)
    return small_call(body, [SMEM] + [VMEM] * (1 + len(others)) + [LOOSE], shape, "join", info, value, *others, after)


def split(value, at, mine):
    keep = lax.dynamic_index_in_dim(value, mine, at, keepdims=False)
    return lax.dynamic_index_in_dim(value, 1 - mine, at, keepdims=False), keep


def scattered(pair, axis, me, bits, total_bits):
    left = list(range(total_bits - 1, -1, -1))
    for place, bit in enumerate(bits):
        if place > 0:
            send, keep = split(value, left.index(bit), (me >> bit) & 1)
            came = swap_bit(send, axis, bit)
        else:
            came, keep = pair
        value = keep.astype(F32) + came.astype(F32)
        if place < len(bits) - 1:
            value = value.astype(BF)
        left.remove(bit)
    return value


def on_device(tokens, lengths, pair_index, images, ln1_gain, ln1_bias, qkv_weight, out_weight,
              ln2_gain, ln2_bias, up_weight, down_weight, final_gain, final_bias, proj_weight):
    groups = lax.axis_size("dp")
    sections = lax.axis_size("section")
    section = lax.axis_index("section")
    group = lax.axis_index("dp")
    model = tokens.shape[1]
    n_seq = lengths.shape[0]
    flip = groups - 2
    own = tokens.shape[0] // ROWS
    slots = 2 * own

    last = sections - 1
    norms = jnp.concatenate([ln1_gain, ln1_bias, ln2_gain, ln2_bias], 0)
    weights = (qkv_weight, out_weight, up_weight, down_weight)
    who = jnp.stack([section, group]).astype(jnp.int32)
    info_own = jnp.concatenate([who, lengths, lengths])
    theirs = lax.ppermute(
        tokens, ("dp", "section"), [(d * sections, (d ^ flip) * sections) for d in range(groups)]
    )
    theirs_lengths = lax.ppermute(lengths, "dp", [(d, d ^ flip) for d in range(groups)])
    info = jnp.concatenate([who, lengths, theirs_lengths])
    bufs = about = coming = None
    sites = slots + LAG * last

    def pairs_at(t, turn):
        return [turn(s) for s in range(last) if 0 <= t - LAG * s < slots]

    hop = {}
    for t in range(sites):
        tok, at = (None, 0) if t >= slots else (hbm(tokens), t * ROWS) if t < own else (theirs, (t - own) * ROWS)
        bufs, weights, y = fwd_call(
            t, own, last, info_own if t < 1 else info, tok, at, hop.get(t - LAG), norms, weights, bufs, slots
        )
        pairs = pairs_at(t, lambda s: (s, s + 1))
        if pairs:
            hop[t] = lax.ppermute(y, "section", pairs)
        m = t - LAG * last
        if m == own - 1:
            about = small_call(pack_kernel, [SMEM, VMEM, VMEM], (n_seq, 2 * model + 128), "pack", pair_index, bufs[10], images)
            coming = [swap_bit(about, "dp", 0)]
        elif m == own:
            about = joined(info, 0, about, coming, y)
            coming = [
                lax.ppermute(about, "dp", [(d, d ^ (2 * k)) for d in range(groups)]) for k in range(1, groups // 2)
            ]
    saved, hid = bufs[:9], bufs[9]
    about, *_, hdy = head_call(own, flip, last, info, final_gain, final_bias, proj_weight, hid, about, *coming)

    back = None
    step = {}
    for t in range(sites):
        tok, at = (None, 0) if t >= slots else (hbm(hdy), t * ROWS)
        back, weights, dx = bwd_call(t, own, last, info, tok, at, step.get(t - LAG), norms, weights, saved, back, slots)
        pairs = pairs_at(t, lambda s: (last - s, last - s - 1))
        if pairs:
            step[t] = lax.ppermute(dx, "section", pairs)
    E, DU, F, DQ, LNG, DXO = back
    X, A, QKV, PP, O, H, C, MM, GP = saved

    bits = (groups // 2).bit_length() - 1
    low_first = list(range(bits))
    high_first = low_first[::-1]
    def head_again(after):
        late = small_call(copy_kernel, [VMEM, ANY], about.shape, "copy", about, hbm(after))
        shared = [lax.ppermute(late, "section", [(last, t)]) for t in range(last)]
        return head_call(own, flip, None, info, final_gain, final_bias, proj_weight, hid, late, *shared)

    if bits == 2:
        down = wgrad(info, MM, E, [dx], 0, bits, part=0)
        up = wgrad(info, C, DU, [down], 1, bits)
        one, kept_one, two, kept_two = attention_wgrad(info, A, DQ, O, F, LNG, up[0], bits)
        kept_down = wgrad(info, MM, E, [two], 0, bits, part=1)
        pieces = [(down, kept_down), up, (one, kept_one), (two, kept_two)]
        orders = (low_first, high_first, low_first, high_first)
        sent = [swap_bit(send, "dp", order[0]) for (send, _), order in zip(pieces, orders)]
        tail = head_again(kept_down)
        after = tail[2]
        held = []
        for came, (_, keep), order in zip(sent, pieces, orders):
            after, keep = fold(info, keep, came, after, order[1])
            held += [keep, swap_bit(after, "dp", order[1])]
        g_up = total(held[2], held[3], after)
        g_down = total(held[0], held[1], g_up)
        g_qkv, g_out, *g_norm = attention_total(*held[4:], g_down)
    else:
        me = numbers(info, dx)[GROUP]
        grads = []
        after = [dx]
        for a, e, norm, order in (
            (MM, E, None, low_first), (C, DU, None, high_first), (A, DQ, None, low_first), (O, F, LNG, high_first)
        ):
            after = [wgrad(info, a, e, after, None, bits, norm)]
            rows, cols = after[0].shape
            cut = after[0].reshape((2,) * bits + (rows >> bits, cols))
            send, keep = split(cut, bits - 1 - order[0], (me >> order[0]) & 1)
            grads.append(scattered((swap_bit(send, "dp", order[0]), keep), "dp", me, order, bits))
        g_down, g_up, g_qkv, g_out = grads
        g_out, g_norm = g_out[:, :model], [g_out[:, model + k][None] for k in range(4)]
        tail = head_again(after[0])
    return (
        bufs[11].reshape(1, own * ROWS, model),
        DXO.reshape(1, own * ROWS, model),
        g_norm[0],
        g_norm[1],
        g_qkv[None],
        g_out[None],
        g_norm[2],
        g_norm[3],
        g_up[None],
        g_down[None],
        tail[3],
        tail[4],
        tail[2],
        tail[1],
    )


def solution(mesh):
    row = P("section", None)
    cube = P("section", None, None)
    in_specs = (P("dp", None), P("dp"), P("dp"), P("dp", None), row, row, cube, cube, row, row, cube, cube, P(), P(), P())
    big = P("section", "dp", None)
    small = P("section", "dp")
    out_specs = (big, big, small, small, big, big, small, small, big, big, P(), P(), P(), P())
    return jax.shard_map(on_device, mesh=mesh, in_specs=in_specs, out_specs=out_specs, check_vma=False)
```

```python
import functools
import math

import jax
import jax.numpy as jnp
from jax import lax
from jax.experimental import pallas as pl
from jax.experimental.pallas import tpu as pltpu
from jax.sharding import PartitionSpec as P

HEADS = 12
HEAD = 64
PAIR = 2 * HEAD
ROWS = 256
EPS = 1e-06
MASKED = -1000000000.0
BF = jnp.bfloat16
F32 = jnp.float32
ANY = pl.BlockSpec(memory_space=pltpu.HBM)
LOOSE = pl.BlockSpec(memory_space=pl.ANY)
SMEM = pl.BlockSpec(memory_space=pltpu.SMEM)
VMEM = pl.BlockSpec(memory_space=pltpu.VMEM)
VLIM = 24 << 20
LAG = 2
FREE = pl.CostEstimate(flops=1, bytes_accessed=1, transcendentals=0)
SECTION, GROUP, LENS = range(3)


def hbm(v):
    return pltpu.with_memory_space_constraint(v, pltpu.HBM)


def vmem(v):
    return pltpu.with_memory_space_constraint(v, pltpu.VMEM)


def mm(a, b):
    return jnp.dot(a, b, preferred_element_type=F32)


def mm_nt(a, b):
    return lax.dot_general(a, b, (((1,), (1,)), ((), ())), preferred_element_type=F32)


def mm_tn(a, b):
    return lax.dot_general(a, b, (((0,), (0,)), ((), ())), preferred_element_type=F32)


def norm_of(v):
    c = v - jnp.mean(v, -1, keepdims=True)
    r = lax.rsqrt(jnp.mean(c * c, -1, keepdims=True) + EPS)
    return c * r, r


def norm_back(n, r, w):
    return r * (w - jnp.mean(w, -1, keepdims=True) - n * jnp.mean(w * n, -1, keepdims=True))


def gelu_pair(u):
    k = 0.7978845608028654
    u2 = u * u
    t = jnp.tanh(u * (k + (k * 0.044715) * u2))
    p = 0.5 + 0.5 * t
    g = p + (0.5 * u) * ((1.0 - t * t) * (k + (3.0 * k * 0.044715) * u2))
    return u * p, g


def split_heads(v, low):
    z = jnp.zeros_like(v)
    return jnp.concatenate([jnp.where(low, v, z), jnp.where(low, z, v)], axis=0)


def low_lanes():
    return lax.broadcasted_iota(jnp.int32, (PAIR, PAIR), 1) < HEAD


def chunk(j, width):
    return pl.ds(pl.multiple_of(j * width, 128), width)


class Weights:
    def __init__(self, sources, held, sem, model):
        self.sem, self.jobs, self.due = sem, {}, sources is not None
        if not self.due:
            return
        k = 0
        for name, src, dst in zip(("qkv", "out", "up", "down"), sources, held):
            rows, cols = dst.shape
            for j in range(max(rows, cols) // model):
                piece = pl.ds(j * model, model)
                at = (slice(None), piece) if cols > model else (piece, slice(None))
                self.jobs[name, j] = (src, dst, at, k)
                k += 1

    def copy(self, name, j, offset=0):
        src, dst, at, k = self.jobs[name, j]
        return pltpu.make_async_copy(src.at[(0,) + at], dst.at[at], self.sem.at[k + offset])

    def start(self, name, *pieces):
        for j in pieces or [j for n, j in self.jobs if n == name]:
            self.copy(name, j).start()

    def wait(self, name, j=0):
        if self.due:
            self.copy(name, 0, j).wait()


def fetch(place, tok, tok_at, arr, dst, sem):
    def copy():
        return pltpu.make_async_copy(tok.at[pl.ds(tok_at, ROWS)], dst, sem)

    def from_arr():
        dst[...] = arr[...]

    if tok is None:
        return from_arr
    if arr is None:
        copy().start()
        return lambda: copy().wait()
    pl.when(place == 0)(lambda: copy().start())

    def finish():
        pl.when(place == 0)(lambda: copy().wait())
        pl.when(place != 0)(from_arr)

    return finish


def fwd_kernel(fresh, site, slots, own, last, tok_at, has, model, ff, info, *rest):
    tok = rest[0] if has[0] else None
    arr = rest[has[0]] if has[1] else None
    norms, w1, w2, w3, w4, *rest = rest[sum(has):]
    (X, A, QKV, PP, O, H, C, MM, GP, HID, NB, Y, wqkv, wo, wup, wdn, yout,
     xs, as_, qs, ps, os_, hs, cs, ms, gs, ys, nb, sem, wsem) = rest
    weights = Weights((w1, w2, w3, w4) if fresh else None, (wqkv, wo, wup, wdn), wsem, model)
    names = ("qkv", "out", "up", "down")
    seqs = ROWS // 64
    section = info[SECTION]
    slot = site - LAG * section
    active = (slot >= 0) & (slot < slots)

    def length(i):
        return info[LENS + slot * seqs + i]

    if fresh:
        @pl.when(jnp.logical_not(active))
        def _():
            for name in names:
                weights.start(name)
            for name, j in weights.jobs:
                weights.wait(name, j)

    @pl.when(active)
    def _():
        come = fetch(section, tok, tok_at, arr, xs, sem.at[0])
        weights.start("qkv")
        come()
        weights.start("out")
        weights.start("up")
        copies = []

        def out(src, dst, k):
            cp = pltpu.make_async_copy(src, dst, sem.at[k])
            cp.start()
            copies.append(cp)

        out(xs, X.at[slot], 18)
        gain, bias = norms[0:1, :], norms[1:2, :]
        for i in range(seqs):
            sl = pl.ds(i * 64, 64)
            n, _r = norm_of(xs[sl, :].astype(F32))
            as_[sl, :] = (n * gain + bias).astype(BF)
        out(as_, A.at[slot], 2)

        for j in range(3):
            sl = pl.ds(j * model, model)
            weights.wait("qkv", j)
            qs[:, sl] = mm(as_[...], wqkv[:, sl]).astype(BF)

        weights.start("down")

        out(qs, QKV.at[slot], 3)
        low = low_lanes()
        row = lax.broadcasted_iota(jnp.int32, (PAIR, PAIR), 0)
        col = lax.broadcasted_iota(jnp.int32, (PAIR, PAIR), 1)

        for it in range(ROWS // 128 * (HEADS // 2)):
            p, hp = divmod(it, HEADS // 2)
            if hp == 0:
                ok = ((col < 64) & (row < length(2 * p))) | ((col >= 64) & (row >= 64) & (row < 64 + length(2 * p + 1)))
            rs = pl.ds(p * 128, 128)

            def lanes(block):
                return pl.ds(block * model + hp * PAIR, PAIR)

            q2 = qs[rs, lanes(0)] * jnp.asarray(HEAD**-0.5, BF)
            s = mm_nt(split_heads(qs[rs, lanes(1)], low), q2)
            halves = []
            for h in range(2):
                sh = jnp.where(ok, s[h * 128:(h + 1) * 128], MASKED)
                e = jnp.exp(sh - jnp.max(sh, 0, keepdims=True))
                halves.append((e * (1.0 / jnp.sum(e, 0, keepdims=True))).astype(BF))
            pc = jnp.concatenate(halves, axis=0)
            ps[it] = pc
            os_[rs, lanes(0)] = mm_tn(pc, split_heads(qs[rs, lanes(2)], low)).astype(BF)

        out(ps, PP.at[slot], 4)
        out(os_, O.at[slot], 5)
        weights.wait("out")
        hs[...] = xs[...].astype(F32) + mm(os_[...], wo[...])
        out(hs, H.at[slot], 6)
        gain2, bias2 = norms[2:3, :], norms[3:4, :]
        for i in range(seqs):
            sl = pl.ds(i * 64, 64)
            n, _r = norm_of(hs[sl, :])
            cs[sl, :] = (n * gain2 + bias2).astype(BF)
        out(cs, C.at[slot], 7)
        parts = ff // model
        total = hs[...]
        for j in range(parts):
            sl = pl.ds(j * model, model)
            weights.wait("up", j)
            m, g = gelu_pair(mm(cs[...], wup[:, sl]))
            ms[:, sl] = m.astype(BF)
            gs[:, sl] = g.astype(BF)
            out(ms.at[:, sl], MM.at[slot, :, sl], 10 + 2 * j)
            out(gs.at[:, sl], GP.at[slot, :, sl], 11 + 2 * j)
            weights.wait("down", j)
            total = total + mm(ms[:, sl], wdn[sl, :])
        ys[...] = total.astype(BF)
        yout[...] = ys[...]
        mine = pltpu.make_async_copy(ys, Y.at[slot], sem.at[1])
        pl.when(slot < own)(lambda: mine.start())
        if site >= LAG * last:
            top = pltpu.make_async_copy(ys, HID.at[slot], sem.at[9])
            means = pltpu.make_async_copy(nb, NB.at[slot], sem.at[0])
            first = site - LAG * last < own

            @pl.when(section == last)
            def _():
                top.start()
                if first:
                    for i in range(seqs):
                        n, _r = norm_of(ys[pl.ds(i * 64, 64), :].astype(F32))
                        count = length(i)
                        ok = lax.broadcasted_iota(jnp.int32, (64, 1), 0) < count
                        nb[pl.ds(i, 1), :] = jnp.sum(jnp.where(ok, n, 0.0), 0, keepdims=True) / count.astype(F32)
                    means.start()

        for cp in copies:
            cp.wait()
        pl.when(slot < own)(lambda: mine.wait())
        if site >= LAG * last:
            @pl.when(section == last)
            def _():
                top.wait()
                if first:
                    means.wait()


def sub_call(body, fixed, specs, weights, held, shapes, scratch, bufs, last_shape, name):
    n, many = len(fixed) + 4, len(shapes)
    alias = {}
    extra = []
    kernel = body
    if held:
        alias = {len(fixed) + i: many + i for i in range(4)}
        weights = [vmem(w) for w in weights]
    else:
        weights = [hbm(w) for w in weights]
    if bufs is not None:
        alias |= {n + i: i for i in range(many)}
        extra = [hbm(v) for v in bufs]

        def kernel(*refs):
            body(*refs[:n], *refs[n + many:])

    res = pl.pallas_call(
        kernel,
        out_shape=[pltpu.HBM(s, d) for s, d in shapes]
        + [pltpu.VMEM(w.shape[-2:], BF) for w in weights]
        + [jax.ShapeDtypeStruct(*last_shape)],
        in_specs=specs + [VMEM if held else ANY] * 4 + [ANY] * len(extra),
        out_specs=[ANY] * many + [VMEM] * 5,
        input_output_aliases=alias,
        scratch_shapes=scratch,
        compiler_params=pltpu.CompilerParams(vmem_limit_bytes=VLIM),
        cost_estimate=FREE,
        name=name,
    )(*fixed, *weights, *extra)
    return res[:many], res[many:many + 4], res[-1]


def site_inputs(tok, arr):
    has = (tok is not None, arr is not None)
    sources = [tok] if has[0] else []
    specs = [LOOSE] * has[0] + [VMEM] * has[1]
    return has, sources + ([arr] if has[1] else []), specs


def fwd_call(site, own, last, info, tok, tok_at, arr, norms, weights, bufs, slots):
    model, ff = weights[2].shape[-2:]
    pairs = ROWS // 128 * (HEADS // 2)
    small = ((slots, ROWS, model), BF)
    wide = ((slots, ROWS, ff), BF)
    shapes = [
        small,
        small,
        ((slots, ROWS, 3 * model), BF),
        ((slots, pairs, 256, 128), BF),
        small,
        ((slots, ROWS, model), F32),
        small,
        wide,
        wide,
        small,
        ((own, ROWS // 64, model), F32),
        ((own, ROWS, model), BF),
    ]
    scratch = [
        pltpu.VMEM((ROWS, model), BF),
        pltpu.VMEM((ROWS, model), BF),
        pltpu.VMEM((ROWS, 3 * model), BF),
        pltpu.VMEM((pairs, 256, 128), BF),
        pltpu.VMEM((ROWS, model), BF),
        pltpu.VMEM((ROWS, model), F32),
        pltpu.VMEM((ROWS, model), BF),
        pltpu.VMEM((ROWS, ff), BF),
        pltpu.VMEM((ROWS, ff), BF),
        pltpu.VMEM((ROWS, model), BF),
        pltpu.VMEM((ROWS // 64, model), F32),
        pltpu.SemaphoreType.DMA((11 + 2 * (ff // model),)),
        pltpu.SemaphoreType.DMA((4 + 2 * (ff // model),)),
    ]
    fresh = bufs is None
    has, sources, kinds = site_inputs(tok, arr)
    fixed = [info, *sources, norms]
    specs = [SMEM, *kinds, VMEM]
    body = functools.partial(fwd_kernel, fresh, site, slots, own, last, tok_at, has, model, ff)
    return sub_call(body, fixed, specs, weights, not fresh, shapes, scratch, bufs, ((ROWS, model), BF), "block_forward")


def bwd_kernel(site, slots, own, last, tok_at, has, model, ff, info, *rest):
    tok = rest[0] if has[0] else None
    arr = rest[has[0]] if has[1] else None
    norms, X, QKV, PP, H, GP, w1, w2, w3, w4, *rest = rest[sum(has):]
    (E, DU, F, DQ, LNG, DXO, wqkv, wo, wup, wdn, dxo,
     es, xs, qs, ps, hs, gs, dus, dhs, fs, dos, dqs, dxs, dxb, lng, sem) = rest
    seqs = ROWS // 64
    place = last - info[SECTION]
    slot = site - LAG * place

    @pl.when((slot >= 0) & (slot < slots))
    def _():
        come = fetch(place, tok, tok_at, arr, es, sem.at[0])
        slope = pltpu.make_async_copy(GP.at[slot], gs, sem.at[5])
        slope.start()
        copies = []

        def out(src, dst, k):
            cp = pltpu.make_async_copy(src, dst, sem.at[k])
            cp.start()
            copies.append(cp)

        parts = ff // model
        loads = []
        for k, (src, dst) in enumerate(((H, hs), (PP, ps), (QKV, qs), (X, xs))):
            loads.append(pltpu.make_async_copy(src.at[slot], dst, sem.at[1 + k]))
        for cp in loads:
            cp.start()
        come()
        slope.wait()
        out(es, E.at[slot], 6)
        dc_all = None
        for j in range(parts):
            sl = pl.ds(j * model, model)
            du = (mm_nt(es[...], wdn[sl, :]) * gs[:, sl].astype(F32)).astype(BF)
            dus[:, sl] = du
        dc_all = mm_nt(dus[...], wup[...])
        out(dus, DU.at[slot], 7)
        for cp in loads:
            cp.wait()
        sums = [jnp.zeros((8, model), F32) for _ in range(4)]

        def fold(v):
            return jnp.sum(v.reshape(8, 8, model), axis=0)

        gain = norms[2:3, :]
        for i in range(seqs):
            sl = pl.ds(i * 64, 64)
            n, r = norm_of(hs[sl, :])
            dc = dc_all[i * 64:(i + 1) * 64]
            sums[2] += fold(dc * n)
            sums[3] += fold(dc)
            dh = es[sl, :].astype(F32) + norm_back(n, r, dc * gain)
            dhs[sl, :] = dh
            fs[sl, :] = dh.astype(BF)
        lng[2] = sums[2]
        lng[3] = sums[3]
        out(fs, F.at[slot], 8)
        dos[...] = mm_nt(fs[...], wo[...]).astype(BF)
        low = low_lanes()

        for it in range(ROWS // 128 * (HEADS // 2)):
            p, hp = divmod(it, HEADS // 2)
            rs = pl.ds(p * 128, 128)

            def lanes(block):
                return pl.ds(block * model + hp * PAIR, PAIR)

            q2 = qs[rs, lanes(0)]
            do2 = dos[rs, lanes(0)]
            pc = ps[it]
            t = pc.astype(F32) * mm_nt(split_heads(qs[rs, lanes(2)], low), do2)
            halves = []
            for h in range(2):
                hl = slice(h * 128, (h + 1) * 128)
                halves.append((t[hl] - pc[hl].astype(F32) * jnp.sum(t[hl], 0, keepdims=True)).astype(BF))
            ds = jnp.concatenate(halves, axis=0)
            scale = HEAD**-0.5
            dq = mm_tn(ds, split_heads(qs[rs, lanes(1)], low)) * scale
            dk = mm(ds, q2) * scale
            dv = mm(pc, do2)
            dqs[rs, lanes(0)] = dq.astype(BF)
            dqs[rs, lanes(1)] = jnp.where(low, dk[:128], dk[128:]).astype(BF)
            dqs[rs, lanes(2)] = jnp.where(low, dv[:128], dv[128:]).astype(BF)

        out(dqs, DQ.at[slot], 9)
        da_all = mm_nt(dqs[...], wqkv[...])
        gain = norms[0:1, :]
        for i in range(seqs):
            sl = pl.ds(i * 64, 64)
            n, r = norm_of(xs[sl, :].astype(F32))
            da = da_all[i * 64:(i + 1) * 64]
            sums[0] += fold(da * n)
            sums[1] += fold(da)
            dx = dhs[sl, :] + norm_back(n, r, da * gain)
            dxs[sl, :] = dx
            dxb[sl, :] = dx.astype(BF)
        dxo[...] = dxb[...]
        lng[0] = sums[0]
        lng[1] = sums[1]
        out(lng, LNG.at[slot], 11)

        mine = pltpu.make_async_copy(dxs, DXO.at[slot], sem.at[12])
        pl.when(slot < own)(lambda: mine.start())
        for cp in copies:
            cp.wait()
        pl.when(slot < own)(lambda: mine.wait())


def bwd_call(site, own, last, info, tok, tok_at, arr, norms, weights, saved, bufs, slots):
    model, ff = weights[2].shape[-2:]
    pairs = ROWS // 128 * (HEADS // 2)
    X, A, QKV, PP, O, H, C, MM, GP = saved
    small = ((slots, ROWS, model), BF)
    shapes = [
        small,
        ((slots, ROWS, ff), BF),
        small,
        ((slots, ROWS, 3 * model), BF),
        ((slots, 4, 8, model), F32),
        ((own, ROWS, model), F32),
    ]
    scratch = [
        pltpu.VMEM((ROWS, model), BF),
        pltpu.VMEM((ROWS, model), BF),
        pltpu.VMEM((ROWS, 3 * model), BF),
        pltpu.VMEM((pairs, 256, 128), BF),
        pltpu.VMEM((ROWS, model), F32),
        pltpu.VMEM((ROWS, ff), BF),
        pltpu.VMEM((ROWS, ff), BF),
        pltpu.VMEM((ROWS, model), F32),
        pltpu.VMEM((ROWS, model), BF),
        pltpu.VMEM((ROWS, model), BF),
        pltpu.VMEM((ROWS, 3 * model), BF),
        pltpu.VMEM((ROWS, model), F32),
        pltpu.VMEM((ROWS, model), BF),
        pltpu.VMEM((4, 8, model), F32),
        pltpu.SemaphoreType.DMA((13,)),
    ]
    has, sources, kinds = site_inputs(tok, arr)
    fixed = [info, *sources, norms, *[hbm(v) for v in (X, QKV, PP, H, GP)]]
    specs = [SMEM, *kinds, VMEM] + [ANY] * 5
    body = functools.partial(bwd_kernel, site, slots, own, last, tok_at, has, model, ff)
    return sub_call(body, fixed, specs, weights, True, shapes, scratch, bufs, ((ROWS, model), BF), "block_backward")


def lay(info, bit, pieces, o):
    n = pieces[0].shape[0]
    me = (info[GROUP] >> bit) & (len(pieces) - 1)
    for k, piece in enumerate(pieces):
        o[pl.ds(pl.multiple_of((me ^ k) * n, 8), n), :] = piece[...]


def head_kernel(own, flip, last, info, fg, fb, proj, hid, first, *rest):
    more, (whole, loss, gproj, ggain, gbias, hdy, dpool, ysc, dsc, sem) = rest[:-10], rest[-10:]
    model = proj.shape[0]
    scale = 1.5 * model**0.5
    blocks = hid.shape[0]
    loads = [pltpu.make_async_copy(hid.at[m], ysc.at[m], sem.at[m]) for m in range(blocks)]
    if last is not None:
        @pl.when(info[SECTION] == last)
        def _():
            for cp in loads:
                cp.start()

    gain, bias = fg[...].reshape(1, model), fb[...].reshape(1, model)
    if last is None:
        about = jnp.where(info[SECTION] == len(more), first[...], sum(v[...] for v in more))
    else:
        lay(info, 1, (first, *more), whole)
        about = whole[...]
    nbar = about[:, 0:model]
    image = about[:, model:2 * model]
    pidx = about[:, 2 * model:2 * model + 1].astype(jnp.int32)
    pooled = (nbar * gain + bias).astype(BF)
    text = mm(pooled, proj[...])
    inv = lax.rsqrt(jnp.sum(text * text, -1, keepdims=True) + EPS)
    unit = text * inv
    iunit = (image * lax.rsqrt(jnp.sum(image * image, -1, keepdims=True) + EPS)).astype(BF)
    logits = scale * mm_nt(unit.astype(BF), iunit)
    rmax = jnp.max(logits, 1, keepdims=True)
    rlse = rmax + jnp.log(jnp.sum(jnp.exp(logits - rmax), 1, keepdims=True))
    cmax = jnp.max(logits, 0, keepdims=True)
    clse = cmax + jnp.log(jnp.sum(jnp.exp(logits - cmax), 0, keepdims=True))
    n = logits.shape[0]
    hot = lax.broadcasted_iota(jnp.int32, (n, n), 1) == pidx
    g = 0.5 * jnp.exp(logits - rlse) + 0.5 * jnp.exp(logits - clse) - jnp.where(hot, 1.0, 0.0)
    dt = scale * mm(g.astype(BF), iunit)
    dtext = ((dt - unit * jnp.sum(dt * unit, -1, keepdims=True)) * inv).astype(BF)
    dp = mm_nt(dtext, proj[...])
    if last is None:
        at = jnp.sum(jnp.where(hot, logits, 0.0), 1, keepdims=True)
        col = jnp.sum(jnp.where(hot, jnp.broadcast_to(clse, (n, n)), 0.0), 1, keepdims=True)
        loss[...] = jnp.broadcast_to(0.5 * (rlse - at) + 0.5 * (col - at), (n, 128)).T[0:1, :].reshape(n)
        gproj[...] = mm_tn(pooled, dtext)
        ggain[...] = jnp.sum(dp * nbar, 0, keepdims=True).reshape(model)
        gbias[...] = jnp.sum(dp, 0, keepdims=True).reshape(model)

    @pl.when(info[SECTION] == (-1 if last is None else last))
    def _():
        dpool[...] = dp
        per = ROWS // 64
        stores = []
        for m in range(blocks):
            loads[m].wait()
            of = info[GROUP] if m < own else info[GROUP] ^ flip
            for i in range(per):
                count = info[LENS + m * per + i]
                nn, r = norm_of(ysc[m, pl.ds(i * 64, 64), :].astype(F32))
                w = dpool[pl.ds(of * own * per + (m % own) * per + i, 1), :] * (gain / count.astype(F32))
                ok = lax.broadcasted_iota(jnp.int32, (64, 1), 0) < count
                dsc[pl.ds(m * ROWS + i * 64, 64), :] = jnp.where(ok, norm_back(nn, r, w), 0.0).astype(BF)
            part = pl.ds(m * ROWS, ROWS)
            cp = pltpu.make_async_copy(dsc.at[part], hdy.at[part], sem.at[blocks + m])
            cp.start()
            stores.append(cp)
        for cp in stores:
            cp.wait()


def head_call(own, flip, last, info, fg, fb, proj, hid, *about):
    blocks, _, model = hid.shape
    pairs = about[0].shape[0] * (1 if last is None else len(about))
    whole = (8, 128) if last is None else (pairs, about[0].shape[1])
    return pl.pallas_call(
        functools.partial(head_kernel, own, flip, last),
        out_shape=[
            jax.ShapeDtypeStruct(whole, F32),
            jax.ShapeDtypeStruct((pairs,), F32),
            jax.ShapeDtypeStruct((model, model), F32),
            jax.ShapeDtypeStruct((model,), F32),
            jax.ShapeDtypeStruct((model,), F32),
            pltpu.HBM((blocks * ROWS, model), BF),
        ],
        in_specs=[SMEM] + [VMEM] * 3 + [ANY] + [VMEM] * len(about),
        out_specs=[VMEM, VMEM, VMEM, VMEM, VMEM, ANY],
        scratch_shapes=[
            pltpu.VMEM((pairs, model), F32),
            pltpu.VMEM((blocks, ROWS, model), BF),
            pltpu.VMEM((blocks * ROWS, model), BF),
            pltpu.SemaphoreType.DMA((2 * blocks,)),
        ],
        compiler_params=pltpu.CompilerParams(vmem_limit_bytes=VLIM),
        cost_estimate=FREE,
        name="head",
    )(info, fg, fb, proj, hbm(hid), *about)


def bit_of(w, bit):
    return (w[GROUP] >> bit) & 1


def wgrad_kernel(bit, waits, normed, part, where, a, e, *rest):
    norms = rest[0] if normed else None
    rest = rest[waits + normed:]

    left = a[...].reshape(a.shape[0] * ROWS, a.shape[2])
    right = e[...].reshape(e.shape[0] * ROWS, e.shape[2])
    g = mm_tn(left, right)
    if normed:
        sums = jnp.sum(jnp.sum(norms[...], 0), 1)
        sums = jnp.concatenate([sums, jnp.zeros((128 - sums.shape[0], sums.shape[1]), F32)], 0)
        g = jnp.concatenate([g, sums.T], 1)
    if bit is None:
        rest[0][...] = g.astype(BF)
        return
    if part is not None:
        rest[0][0] = g.astype(BF)
        return
    send, keep = rest[:2]
    quarter = send.shape[1]
    if quarter == g.shape[0]:
        step = pl.program_id(0)

        @pl.when(step < 2)
        def _():
            send[0] = g.astype(BF)

        @pl.when(step >= 2)
        def _():
            keep[0] = g.astype(BF)
    else:
        high = bit_of(where, bit) == 1
        parts = [g[k * quarter:(k + 1) * quarter] for k in range(4)]
        for k in range(2):
            one, two = (parts[2 * k], parts[2 * k + 1]) if bit == 0 else (parts[k], parts[2 + k])
            send[k] = jnp.where(high, one, two).astype(BF)
            keep[k] = jnp.where(high, two, one).astype(BF)


def wgrad(info, left, right, after, bit, half_bit, norms=None, part=None):
    slots, _, wide = left.shape
    cols = right.shape[2]
    mine = wide // 2
    step = math.gcd(mine, 384)
    width = 1536 if cols % 1536 == 0 and mine <= 384 else 768
    left_blocks = mine // step
    single = left_blocks == 4 and bit is not None
    normed = norms is not None
    more = 128 if normed else 0

    def left_at(i, j, w):
        if single:
            own_bit = bit_of(w, bit)
            if part is None:
                other = jnp.where(i < 2, 1 - own_bit, own_bit)
            else:
                other = own_bit if part else 1 - own_bit
            k = (i % 2) * 2 + other if bit == 0 else other * 2 + i % 2
        else:
            k = i
        return (0, 0, bit_of(w, half_bit) * left_blocks + k)

    if bit is None:
        out_shape = pltpu.HBM((mine, cols + more), BF)
        out_specs = pl.BlockSpec((step, width + more), lambda i, j, w: (i, j))
    else:
        out_shape = [pltpu.HBM((2, mine // 4, cols + more), BF)] * 2
        if part is not None:
            out_shape = out_shape[0]
            out_specs = pl.BlockSpec((1, step, width), lambda i, j, w: (i, 0, j))
        elif single:
            out_specs = [
                pl.BlockSpec((1, step, width), lambda i, j, w: (jnp.minimum(i, 1), 0, j)),
                pl.BlockSpec((1, step, width), lambda i, j, w: (jnp.maximum(i - 2, 0), 0, j)),
            ]
        else:
            out_specs = [pl.BlockSpec((2, mine // 4, width + more), lambda i, j, w: (0, 0, j))] * 2
    return pl.pallas_call(
        functools.partial(wgrad_kernel, bit, len(after), normed, part),
        grid_spec=pltpu.PrefetchScalarGridSpec(
            num_scalar_prefetch=1,
            grid=(left_blocks if part is None else 2, cols // width),
            in_specs=[
                pl.BlockSpec((slots, ROWS, step), left_at),
                pl.BlockSpec((slots, ROWS, width), lambda i, j, w: (0, 0, j)),
                *([pl.BlockSpec((slots, 4, 8, step), lambda i, j, w: (0, 0, 0, bit_of(w, half_bit)))] if normed else []),
                *[ANY for _ in after],
            ],
            out_specs=out_specs,
        ),
        out_shape=out_shape,
        compiler_params=pltpu.CompilerParams(vmem_limit_bytes=VLIM),
        cost_estimate=FREE,
        name="weight_grad",
    )(info, hbm(left), hbm(right), *([norms] if normed else []), *map(hbm, after))


def halves(g, info, bit):
    quarter = g.shape[0] // 4
    parts = [g[k * quarter:(k + 1) * quarter] for k in range(4)]
    high = bit_of(info, bit) == 1
    send, keep = [], []
    for k in range(2):
        one, two = (parts[2 * k], parts[2 * k + 1]) if bit == 0 else (parts[k], parts[2 + k])
        send.append(jnp.where(high, one, two).astype(BF))
        keep.append(jnp.where(high, two, one).astype(BF))
    return send, keep


def attention_kernel(info, a, o, dq, f, norms, after, send_one, keep_one, send_two, keep_two):
    j = pl.program_id(0)
    thirds = pl.num_programs(0) - 1

    def product(left, right):
        return mm_tn(left[...].reshape(-1, left.shape[2]), right[...].reshape(-1, right.shape[2]))

    def put(g, outs, bit, at, width):
        for value, out in zip(halves(g, info, bit), outs):
            for k in range(2):
                out[k, :, pl.ds(at, width)] = value[k]

    one, two = (send_one, keep_one), (send_two, keep_two)
    width = dq.shape[2]
    for k in range(3):
        @pl.when(j == k)
        def _():
            put(product(a, dq), one if k < 2 else two, 0 if k < 2 else 1, k * width if k < 2 else 0, width)

    @pl.when(j == thirds)
    def _():
        g = product(o, f)
        half = width // 2
        put(g[:, :half], one, 0, 2 * width, half)
        put(g[:, half:], two, 1, width, half)
        sums = jnp.sum(jnp.sum(norms[...], 0), 1)
        sums = jnp.concatenate([sums, jnp.zeros((128 - sums.shape[0], sums.shape[1]), F32)], 0)
        put(sums.T, two, 1, width + half, 128)


def attention_wgrad(info, a, dq, o, f, norms, after, half_bit):
    slots, _, model = a.shape
    mine = model // 2
    left = pl.BlockSpec((slots, ROWS, mine), lambda j, w: (0, 0, bit_of(w, half_bit)))
    shapes = [(2, mine // 4, 2 * model + mine)] * 2 + [(2, mine // 4, model + mine + 128)] * 2
    return pl.pallas_call(
        attention_kernel,
        grid_spec=pltpu.PrefetchScalarGridSpec(
            num_scalar_prefetch=1,
            grid=(4,),
            in_specs=[
                left,
                left,
                pl.BlockSpec((slots, ROWS, model), lambda j, w: (0, 0, jnp.minimum(j, 2))),
                pl.BlockSpec((slots, ROWS, model), lambda j, w: (0, 0, 0)),
                pl.BlockSpec((slots, 4, 8, mine), lambda j, w: (0, 0, 0, bit_of(w, half_bit))),
                ANY,
            ],
            out_specs=[pl.BlockSpec(s, lambda j, w: (0, 0, 0)) for s in shapes],
        ),
        out_shape=[pltpu.HBM(s, BF) for s in shapes],
        compiler_params=pltpu.CompilerParams(vmem_limit_bytes=VLIM),
        cost_estimate=FREE,
        name="attention_weight_grad",
    )(info, hbm(a), hbm(o), hbm(dq), hbm(f), norms, hbm(after))


def attention_total_kernel(keep_one, came_one, keep_two, came_two, after, qkv, out, *norms):
    model = out.shape[1]
    half = model // 2
    one = keep_one[...].astype(F32) + came_one[...].astype(F32)
    two = keep_two[...].astype(F32) + came_two[...].astype(F32)
    qkv[:, 0:2 * model] = one[:, 0:2 * model]
    qkv[:, 2 * model:] = two[:, 0:model]
    out[:, 0:half] = one[:, 2 * model:]
    out[:, half:] = two[:, model:model + half]
    rows = two.shape[0]
    sums = jnp.concatenate([two[:, model + half:], jnp.zeros((128 - rows, 128), F32)], 0).T
    for k, o in enumerate(norms):
        o[...] = sums[k:k + 1, 0:rows]


def attention_total(keep_one, came_one, keep_two, came_two, after):
    rows, cols = keep_one.shape
    model = 2 * cols // 5
    return pl.pallas_call(
        attention_total_kernel,
        in_specs=[VMEM] * 4 + [ANY],
        out_specs=[VMEM] * 6,
        out_shape=[jax.ShapeDtypeStruct(s, F32) for s in [(rows, 3 * model), (rows, model)] + [(1, rows)] * 4],
        cost_estimate=FREE,
        name="attention_total",
    )(keep_one, came_one, keep_two, came_two, hbm(after))


def fold_kernel(bit, info, keep, came, after, send, left):
    high = bit_of(info, bit) == 1
    one = keep[0].astype(F32) + came[0].astype(F32)
    two = keep[1].astype(F32) + came[1].astype(F32)
    send[...] = jnp.where(high, one, two).astype(BF)
    left[...] = jnp.where(high, two, one).astype(BF)


def fold(info, keep, came, after, bit):
    _, rows, cols = keep.shape
    width = 768 if cols % 768 == 0 else cols
    block = pl.BlockSpec((2, rows, width), lambda j, w: (0, 0, j))
    half = pl.BlockSpec((rows, width), lambda j, w: (0, j))
    return pl.pallas_call(
        functools.partial(fold_kernel, bit),
        grid_spec=pltpu.PrefetchScalarGridSpec(
            num_scalar_prefetch=1, grid=(cols // width,), in_specs=[block, block, ANY], out_specs=[half, half]
        ),
        out_shape=[pltpu.HBM((rows, cols), BF)] * 2,
        compiler_params=pltpu.CompilerParams(vmem_limit_bytes=VLIM),
        cost_estimate=FREE,
        name="fold",
    )(info, keep, came, hbm(after))


def total_kernel(keep, came, *rest):
    o = rest[-1]
    o[...] = keep[...].astype(F32) + came[...].astype(F32)


def total(keep, came, *after):
    rows, cols = keep.shape
    width = 768 if cols % 768 == 0 else cols
    block = pl.BlockSpec((rows, width), lambda j: (0, j))
    return pl.pallas_call(
        total_kernel,
        grid=(cols // width,),
        in_specs=[block, block] + [ANY] * len(after),
        out_specs=block,
        out_shape=pltpu.HBM((rows, cols), F32),
        compiler_params=pltpu.CompilerParams(vmem_limit_bytes=VLIM),
        cost_estimate=FREE,
        name="total",
    )(keep, came, *map(hbm, after))


def swap_bit(value, axis, bit):
    peers = lax.axis_size(axis)
    return lax.ppermute(value, axis, [(i, i ^ (1 << bit)) for i in range(peers)])


def pack_kernel(pairs, nb, img, o):
    model = img.shape[1]
    n, per = nb.shape[:2]
    for i in range(n):
        o[pl.ds(i * per, per), 0:model] = nb[i]
    o[:, model:2 * model] = img[...].astype(F32)
    for i in range(n * per):
        o[pl.ds(i, 1), 2 * model:] = jnp.full((1, 128), pairs[i], jnp.int32).astype(F32)


def join_kernel(bit, info, *rest):
    lay(info, bit, rest[:-2], rest[-1])


def copy_kernel(value, *rest):
    rest[-1][...] = value[...]


def numbers_kernel(info, after, o):
    for k in range(o.shape[0]):
        o[k] = info[k]


def numbers(info, after):
    return pl.pallas_call(
        numbers_kernel,
        out_shape=jax.ShapeDtypeStruct(info.shape, jnp.int32),
        in_specs=[SMEM, LOOSE],
        out_specs=SMEM,
        cost_estimate=FREE,
        name="numbers",
    )(info, after)


def small_call(body, specs, shape, name, *args):
    return pl.pallas_call(
        body,
        out_shape=jax.ShapeDtypeStruct(shape, F32),
        in_specs=specs,
        out_specs=VMEM,
        compiler_params=pltpu.CompilerParams(vmem_limit_bytes=8 << 20),
        cost_estimate=FREE,
        name=name,
    )(*args)


def joined(info, bit, value, others, after):
    shape = ((1 + len(others)) * value.shape[0], value.shape[1])
    body = functools.partial(join_kernel, bit)
    return small_call(body, [SMEM] + [VMEM] * (1 + len(others)) + [LOOSE], shape, "join", info, value, *others, after)


def split(value, at, mine):
    keep = lax.dynamic_index_in_dim(value, mine, at, keepdims=False)
    return lax.dynamic_index_in_dim(value, 1 - mine, at, keepdims=False), keep


def scattered(pair, axis, me, bits, total_bits):
    left = list(range(total_bits - 1, -1, -1))
    for place, bit in enumerate(bits):
        if place > 0:
            send, keep = split(value, left.index(bit), (me >> bit) & 1)
            came = swap_bit(send, axis, bit)
        else:
            came, keep = pair
        value = keep.astype(F32) + came.astype(F32)
        if place < len(bits) - 1:
            value = value.astype(BF)
        left.remove(bit)
    return value


def on_device(tokens, lengths, pair_index, images, ln1_gain, ln1_bias, qkv_weight, out_weight,
              ln2_gain, ln2_bias, up_weight, down_weight, final_gain, final_bias, proj_weight):
    groups = lax.axis_size("dp")
    sections = lax.axis_size("section")
    section = lax.axis_index("section")
    group = lax.axis_index("dp")
    model = tokens.shape[1]
    n_seq = lengths.shape[0]
    flip = groups - 2
    own = tokens.shape[0] // ROWS
    slots = 2 * own

    last = sections - 1
    norms = jnp.concatenate([ln1_gain, ln1_bias, ln2_gain, ln2_bias], 0)
    weights = (qkv_weight, out_weight, up_weight, down_weight)
    who = jnp.stack([section, group]).astype(jnp.int32)
    info_own = jnp.concatenate([who, lengths, lengths])
    theirs = lax.ppermute(
        tokens, ("dp", "section"), [(d * sections, (d ^ flip) * sections) for d in range(groups)]
    )
    theirs_lengths = lax.ppermute(lengths, "dp", [(d, d ^ flip) for d in range(groups)])
    info = jnp.concatenate([who, lengths, theirs_lengths])
    bufs = about = coming = None
    sites = slots + LAG * last

    def pairs_at(t, turn):
        return [turn(s) for s in range(last) if 0 <= t - LAG * s < slots]

    hop = {}
    for t in range(sites):
        tok, at = (None, 0) if t >= slots else (hbm(tokens), t * ROWS) if t < own else (theirs, (t - own) * ROWS)
        bufs, weights, y = fwd_call(
            t, own, last, info_own if t < 1 else info, tok, at, hop.get(t - LAG), norms, weights, bufs, slots
        )
        pairs = pairs_at(t, lambda s: (s, s + 1))
        if pairs:
            hop[t] = lax.ppermute(y, "section", pairs)
        m = t - LAG * last
        if m == own - 1:
            about = small_call(pack_kernel, [SMEM, VMEM, VMEM], (n_seq, 2 * model + 128), "pack", pair_index, bufs[10], images)
            coming = [swap_bit(about, "dp", 0)]
        elif m == own:
            about = joined(info, 0, about, coming, y)
            coming = [
                lax.ppermute(about, "dp", [(d, d ^ (2 * k)) for d in range(groups)]) for k in range(1, groups // 2)
            ]
    saved, hid = bufs[:9], bufs[9]
    about, *_, hdy = head_call(own, flip, last, info, final_gain, final_bias, proj_weight, hid, about, *coming)

    back = None
    step = {}
    for t in range(sites):
        tok, at = (None, 0) if t >= slots else (hbm(hdy), t * ROWS)
        back, weights, dx = bwd_call(t, own, last, info, tok, at, step.get(t - LAG), norms, weights, saved, back, slots)
        pairs = pairs_at(t, lambda s: (last - s, last - s - 1))
        if pairs:
            step[t] = lax.ppermute(dx, "section", pairs)
    E, DU, F, DQ, LNG, DXO = back
    X, A, QKV, PP, O, H, C, MM, GP = saved

    bits = (groups // 2).bit_length() - 1
    low_first = list(range(bits))
    high_first = low_first[::-1]
    def head_again(after):
        late = small_call(copy_kernel, [VMEM, ANY], about.shape, "copy", about, hbm(after))
        shared = [lax.ppermute(late, "section", [(last, t)]) for t in range(last)]
        return head_call(own, flip, None, info, final_gain, final_bias, proj_weight, hid, late, *shared)

    if bits == 2:
        down = wgrad(info, MM, E, [dx], 0, bits, part=0)
        up = wgrad(info, C, DU, [down], 1, bits)
        one, kept_one, two, kept_two = attention_wgrad(info, A, DQ, O, F, LNG, up[0], bits)
        kept_down = wgrad(info, MM, E, [two], 0, bits, part=1)
        pieces = [(down, kept_down), up, (one, kept_one), (two, kept_two)]
        orders = (low_first, high_first, low_first, high_first)
        sent = [swap_bit(send, "dp", order[0]) for (send, _), order in zip(pieces, orders)]
        tail = head_again(kept_down)
        after = tail[2]
        held = []
        for came, (_, keep), order in zip(sent, pieces, orders):
            after, keep = fold(info, keep, came, after, order[1])
            held += [keep, swap_bit(after, "dp", order[1])]
        g_up = total(held[2], held[3], after)
        g_down = total(held[0], held[1], g_up)
        g_qkv, g_out, *g_norm = attention_total(*held[4:], g_down)
    else:
        me = numbers(info, dx)[GROUP]
        grads = []
        after = [dx]
        for a, e, norm, order in (
            (MM, E, None, low_first), (C, DU, None, high_first), (A, DQ, None, low_first), (O, F, LNG, high_first)
        ):
            after = [wgrad(info, a, e, after, None, bits, norm)]
            rows, cols = after[0].shape
            cut = after[0].reshape((2,) * bits + (rows >> bits, cols))
            send, keep = split(cut, bits - 1 - order[0], (me >> order[0]) & 1)
            grads.append(scattered((swap_bit(send, "dp", order[0]), keep), "dp", me, order, bits))
        g_down, g_up, g_qkv, g_out = grads
        g_out, g_norm = g_out[:, :model], [g_out[:, model + k][None] for k in range(4)]
        tail = head_again(after[0])
    return (
        bufs[11].reshape(1, own * ROWS, model),
        DXO.reshape(1, own * ROWS, model),
        g_norm[0],
        g_norm[1],
        g_qkv[None],
        g_out[None],
        g_norm[2],
        g_norm[3],
        g_up[None],
        g_down[None],
        tail[3],
        tail[4],
        tail[2],
        tail[1],
    )


def solution(mesh):
    row = P("section", None)
    cube = P("section", None, None)
    in_specs = (P("dp", None), P("dp"), P("dp"), P("dp", None), row, row, cube, cube, row, row, cube, cube, P(), P(), P())
    big = P("section", "dp", None)
    small = P("section", "dp")
    out_specs = (big, big, small, small, big, big, small, small, big, big, P(), P(), P(), P())
    return jax.shard_map(on_device, mesh=mesh, in_specs=in_specs, out_specs=out_specs, check_vma=False)
```
